32 devices in a mesh: fsdp: 4 (over x, core), ctx: 4 (over z), tp: 2 (over y).
Axes of the slice: x: 2, y: 2, z: 4, core: 2. Of those that a mesh axis runs over, the one named last changes fastest.
Arguments:
- images: bfloat16 [8, 2304, 768], P('fsdp', 'ctx'), may hold values from -6 to 6
- norm1_gain: bfloat16 [768], replicated, may hold values from 0.5 to 1.5
- norm1_bias: bfloat16 [768], replicated, may hold values from -1.25 to 1.25
- qkv_weight: bfloat16 [3, 768, 768], P(None, ('fsdp', 'ctx'), 'tp'), may hold values from -0.21875 to 0.21875
- qv_bias: bfloat16 [2, 768], P(None, 'tp'), may hold values from -1.25 to 1.25
- rel_pos_h: bfloat16 [95, 64], replicated, may hold values from -0.75 to 0.75
- rel_pos_w: bfloat16 [95, 64], replicated, may hold values from -0.75 to 0.75
- proj_weight: bfloat16 [768, 768], P(('fsdp', 'ctx'), 'tp'), may hold values from -2.5 to 2.5
- proj_bias: bfloat16 [768], replicated, may hold values from -1.25 to 1.25
- norm2_gain: bfloat16 [768], replicated, may hold values from 0.5 to 1.5
- norm2_bias: bfloat16 [768], replicated, may hold values from -1.25 to 1.25
- up_weight: bfloat16 [768, 3072], P(('fsdp', 'ctx'), 'tp'), may hold values from -0.21875 to 0.21875
- up_bias: bfloat16 [3072], P('tp'), may hold values from -1.75 to 1.75
- down_weight: bfloat16 [768, 3072], P(('fsdp', 'ctx'), 'tp'), may hold values from -0.109375 to 0.109375
- down_bias: bfloat16 [768], replicated, may hold values from -1.25 to 1.25
- out_cotangent: bfloat16 [8, 2304, 768], P('fsdp', 'ctx'), may hold values from -8 to 8
Outputs:
- block_out: bfloat16 [8, 2304, 768], P('fsdp', 'ctx')
- images_grad: bfloat16 [8, 2304, 768], P('fsdp', 'ctx')
- norm1_gain_grad: float32 [768], replicated
- norm1_bias_grad: float32 [768], replicated
- qkv_weight_grad: float32 [3, 768, 768], P(None, ('fsdp', 'ctx'), 'tp')
- qv_bias_grad: float32 [2, 768], P(None, 'tp')
- rel_pos_h_grad: float32 [95, 64], replicated
- rel_pos_w_grad: float32 [95, 64], replicated
- proj_weight_grad: float32 [768, 768], P(('fsdp', 'ctx'), 'tp')
- proj_bias_grad: float32 [768], replicated
- norm2_gain_grad: float32 [768], replicated
- norm2_bias_grad: float32 [768], replicated
- up_weight_grad: float32 [768, 3072], P(('fsdp', 'ctx'), 'tp')
- up_bias_grad: float32 [3072], P('tp')
- down_weight_grad: float32 [768, 3072], P(('fsdp', 'ctx'), 'tp')
- down_bias_grad: float32 [768], replicated
The draws below stay inside these ranges and needn't reach their ends.
All inputs are finite; a program needn't handle non-finite values.
Results may differ from the reference program's by a relative error of at most 0.018.
Values may be sent and summed in bfloat16 or wider, within the bound.
No kernel may reach another device: no remote copies, remote signals or barrier semaphores. Data moves between devices by JAX's collectives and lax.ppermute only.
A program may use at most 256 MiB of HBM per device.

```python
import jax
import jax.numpy as jnp
from jax import lax

D = 768
H = 12
FF = 3072
G = 48
HD = 64
TOKENS = 2304
IMAGES = 8


def with_spikes(drawn, stream_key, source, target, blocks, factor):
    owner, partner = [(jnp.arange(drawn.shape[dim]) // (drawn.shape[dim] // blocks)).reshape([-1 if axis == dim else 1 for axis in range(drawn.ndim)]) for dim in (source, target)]
    chosen = jax.random.permutation(stream_key, blocks)[partner]
    strong = (owner == chosen) | (owner == (partner + blocks // 2) % blocks)
    return jnp.where(strong, factor * drawn, drawn)


def shard_levels(key, dims, pieces, low, largest):
    factor_of = 1.0
    for dim, blocks in pieces:
        heights = jax.random.uniform(jax.random.fold_in(jax.random.fold_in(key, 6), dim), (blocks,), jnp.float32, low / len(pieces), largest / len(pieces))
        factor_of = factor_of * jnp.repeat(jnp.exp(heights), dims[dim] // blocks).reshape((-1,) + (1,) * (len(dims) - 1 - dim))
    return factor_of


def centred(stream_key, extent, scale, most, shards=(), kind=jnp.bfloat16):
    array = jax.random.normal(stream_key, extent, jnp.float32) * scale
    if len(shards) > 0:
        array = shard_levels(stream_key, extent, shards, -0.22, 0.18) * array
    return jnp.clip(array, min=-most, max=most).astype(kind)


def bell_draw_with(key, extent, deviation, most, shards, heavy, dtype=jnp.bfloat16):
    entries = deviation * jax.random.normal(key, extent, jnp.float32)
    if shards:
        entries = entries * shard_levels(key, extent, shards, -0.22, 0.18)
    return jnp.clip(with_spikes(entries, jax.random.fold_in(key, 3), *heavy), -most, most).astype(dtype)


def setup_inputs(seed: int = 0) -> dict:
    arg_keys = jax.random.split(jax.random.key(seed), 17)
    return {
        "images": centred(arg_keys[0], (IMAGES, TOKENS, D), 1.0, 6.0, ((0, 4), (1, 4))),
        "norm1_gain": jnp.clip(1.0 + 0.1 * jax.random.normal(arg_keys[1], (D,), jnp.float32), 0.5, 1.5).astype(jnp.bfloat16),
        "norm1_bias": centred(arg_keys[2], (D,), 0.2, 1.25),
        "qkv_weight": centred(arg_keys[3], (3, D, D), D ** -0.5, 0.21875, ((1, 16), (2, 2))),
        "qv_bias": centred(arg_keys[4], (2, D), 0.2, 1.25, ((1, 2),)),
        "rel_pos_h": centred(arg_keys[5], (2 * G - 1, HD), 0.125, 0.75),
        "rel_pos_w": centred(arg_keys[6], (2 * G - 1, HD), 0.125, 0.75),
        "proj_weight": centred(arg_keys[7], (D, D), (max(1, D * 16 // TOKENS)) ** -0.5, 2.5, ((0, 16), (1, 2))),
        "proj_bias": centred(arg_keys[8], (D,), 0.2, 1.25),
        "norm2_gain": jnp.clip(1.0 + 0.1 * jax.random.normal(arg_keys[9], (D,), jnp.float32), 0.5, 1.5).astype(jnp.bfloat16),
        "norm2_bias": centred(arg_keys[10], (D,), 0.2, 1.25),
        "up_weight": centred(arg_keys[11], (D, FF), D ** -0.5, 0.21875, ((0, 16), (1, 2))),
        "up_bias": centred(arg_keys[12], (FF,), 0.3, 1.75, ((0, 2),)),
        "down_weight": centred(arg_keys[13], (D, FF), FF ** -0.5, 0.109375, ((0, 16), (1, 2))),
        "down_bias": centred(arg_keys[14], (D,), 0.2, 1.25),
        "out_cotangent": bell_draw_with(arg_keys[15], (IMAGES, TOKENS, D), 1.0, 8.0, ((0, 4), (1, 4)), (1, 2, 4, 2.0)),
    }


@jax.custom_vjp
def low(v):
    return lax.optimization_barrier(v.astype(jnp.bfloat16)).astype(jnp.float32)

@jax.custom_vjp
def low_back(v):
    return v

def low_keep(v):
    return (low(v), None)

def low_pass(kept, grad):
    return (grad,)

def back_keep(v):
    return (v, None)

def back_low(kept, grad):
    return (low(grad),)
low.defvjp(low_keep, low_pass)
low_back.defvjp(back_keep, back_low)
eps = 1e-06
highest = lax.Precision.HIGHEST

def layer_norm(values, gain_vec, shift_vec):
    center = values - lax.optimization_barrier(jnp.mean(values, axis=-1, keepdims=True))
    scaled = center * lax.rsqrt(lax.optimization_barrier(jnp.mean(center * center, axis=-1, keepdims=True)) + eps)
    return scaled * gain_vec + shift_vec

def rel_table(pos_table):
    offsets = (jnp.arange(G)[:, None] - jnp.arange(G)[None, :] + (G - 1)).astype(jnp.int32)
    return pos_table[offsets]

def attention(query, keys, values, table_h, table_w):
    block_rows = min(G, 16)
    block_count = G // block_rows
    heads_q = query.reshape(block_count, block_rows, G, H, HD)
    keys_h = keys.reshape(TOKENS, H, HD)
    values_h = values.reshape(TOKENS, H, HD)
    near_h = rel_table(table_h).reshape(block_count, block_rows, G, HD)
    near_w = rel_table(table_w)
    factor = HD ** (-0.5)

    def one_block(pair):
        q_block, h_block = pair
        scores = jnp.einsum('awhc,khc->hawk', q_block, keys_h, precision=highest) * factor
        scores = scores.reshape(H, block_rows, G, G, G)
        along_h = jnp.einsum('awhc,akc->hawk', q_block, h_block, precision=highest)
        along_w = jnp.einsum('awhc,wkc->hawk', q_block, near_w, precision=highest)
        scores = scores + along_h[..., :, None] + along_w[..., None, :]
        scores = low_back(scores.reshape(H, block_rows * G, TOKENS))
        weights_p = low(jax.nn.softmax(scores, axis=-1))
        result = jnp.einsum('hqk,khc->qhc', weights_p, values_h, precision=highest)
        return result.reshape(block_rows * G, H * HD)
    outputs = lax.map(jax.checkpoint(one_block), (heads_q, near_h))
    return outputs.reshape(TOKENS, D)

def block_forward(picture, norm1_gain, norm1_bias, qkv_weight, qv_bias, rel_pos_h, rel_pos_w, proj_weight, proj_bias, norm2_gain, norm2_bias, up_weight, up_bias, down_weight, down_bias):
    normed = low(layer_norm(picture, norm1_gain, norm1_bias))
    query = low(low_back(jnp.dot(normed, qkv_weight[0], precision=highest) + qv_bias[0]))
    keys = low(low_back(jnp.dot(normed, qkv_weight[1], precision=highest)))
    values = low(low_back(jnp.dot(normed, qkv_weight[2], precision=highest) + qv_bias[1]))
    mixed = low(low_back(attention(query, keys, values, rel_pos_h, rel_pos_w)))
    branch = low_back(jnp.dot(mixed, proj_weight.T, precision=highest) + proj_bias)
    middle = picture + branch
    normed2 = low(layer_norm(middle, norm2_gain, norm2_bias))
    hidden = low_back(jnp.dot(normed2, up_weight, precision=highest) + up_bias)
    active = low(jax.nn.gelu(hidden, approximate=False))
    branch2 = low_back(jnp.dot(active, down_weight.T, precision=highest) + down_bias)
    return middle + branch2

def reference(images, norm1_gain, norm1_bias, qkv_weight, qv_bias, rel_pos_h, rel_pos_w, proj_weight, proj_bias, norm2_gain, norm2_bias, up_weight, up_bias, down_weight, down_bias, out_cotangent):
    params = tuple((member.astype(jnp.float32) for member in (norm1_gain, norm1_bias, qkv_weight, qv_bias, rel_pos_h, rel_pos_w, proj_weight, proj_bias, norm2_gain, norm2_bias, up_weight, up_bias, down_weight, down_bias)))

    def per_image(totals, pair):
        picture, cotangent = pair
        result, pullback = jax.vjp(block_forward, picture.astype(jnp.float32), *params)
        grads = pullback(cotangent.astype(jnp.float32))
        totals = jax.tree.map(lambda first_v, second_v: first_v + second_v, totals, tuple(grads[1:]))
        return (totals, (result.astype(jnp.bfloat16), grads[0].astype(jnp.bfloat16)))
    zeros = jax.tree.map(jnp.zeros_like, params)
    totals, (outputs, input_grads) = lax.scan(per_image, zeros, (images, out_cotangent))
    return (outputs, input_grads, totals[0], totals[1], totals[2], totals[3], totals[4], totals[5], totals[6], totals[7], totals[8], totals[9], totals[10], totals[11], totals[12], totals[13])
```

```python
from functools import partial

import jax
import jax.numpy as jnp
import ml_dtypes
import numpy as np
from jax import lax
from jax.experimental import pallas as pl
from jax.experimental.pallas import tpu as pltpu
from jax.sharding import PartitionSpec as P

G = 48
HD = 64


eps = 1e-06
highest = lax.Precision.HIGHEST
bf16, f32 = jnp.bfloat16, jnp.float32
VMEM_BYTES = 56 * 1024 * 1024
NN = (((1,), (0,)), ((), ()))
NT = (((1,), (1,)), ((), ()))
LH, LW = 64, 112


def mm(a, b, dims=NN):
    return lax.dot_general(a, b, dims, preferred_element_type=f32)


def roll(x, shift, stride=None):
    extra = {} if stride is None else dict(stride=stride, stride_axis=0)
    return pltpu.roll(x, shift, 1, **extra)


def lane_iota(shape):
    return lax.broadcasted_iota(jnp.int32, shape, 1)


def prep_kernel(order_ref, x_ref, w_ref, b_ref, tab_ref, hot_ref, q_ref, k_ref, v_ref, *, heads, sets, zparts):
    rows = x_ref.shape[1]
    part = rows // zparts
    where = order_ref[pl.program_id(0)]
    qkv = (mm(x_ref[0], w_ref[...]) + b_ref[...]).astype(bf16)
    lane = lane_iota((G, 128))
    hot_a = hot_ref[0, :, :128].astype(f32)
    hot_b = hot_ref[0, :, 128:]
    lane_all = lane_iota((rows, 128))
    for h in range(heads):
        q = qkv[:, h * 128:(h + 1) * 128]
        k = qkv[:, (heads + h) * 128:(heads + h + 1) * 128].astype(f32)
        v = qkv[:, (2 * heads + h) * 128:(2 * heads + h + 1) * 128].astype(f32)
        k_ref[h, :, :128] = jnp.where(lane_all < 64, k, hot_a).astype(bf16)
        k_ref[h, :, 128:] = hot_b
        v_ref[h] = jnp.where(lane_all < 64, v, jnp.where(lane_all < 67, 1.0, 0.0)).astype(bf16)
        turned = mm(q, tab_ref[...])
        qf = q.astype(f32) * (HD ** -0.5)
        for g in range(rows // G):
            zsrc, inner = divmod(g, part // G)
            r = zsrc * (sets * part // G) + where * (part // G) + inner
            along_h = turned[g * G:(g + 1) * G, :128]
            along_w = turned[g * G:(g + 1) * G, 128:]
            h_a = roll(along_h, (LH - (G - 1) + 128 + r) % 128)
            h_b = roll(along_h, (32 - (G - 1) + 128 + r) % 128)
            w_a = roll(along_w, (LW - (G - 1)) % 128, 1)
            w_b = roll(along_w, (80 - (G - 1)) % 128, 1)
            h_lo = h_b - h_b.astype(bf16).astype(f32)
            w_lo = w_b - w_b.astype(bf16).astype(f32)
            first = jnp.where(lane < LH, qf[g * G:(g + 1) * G], jnp.where(lane < LW, h_a, w_a))
            second = jnp.where(lane < 32, w_a, jnp.where(lane < 80, h_lo, w_lo))
            q_ref[h, g * G:(g + 1) * G, :128] = first.astype(bf16)
            q_ref[h, g * G:(g + 1) * G, 128:] = second.astype(bf16)


def prep(x, w, b, tab, hot, order, heads, zparts):
    sets, rows, d = x.shape
    tokens = sets * rows
    return pl.pallas_call(
        partial(prep_kernel, heads=heads, sets=sets, zparts=zparts),
        out_shape=(
            jax.ShapeDtypeStruct((heads, tokens, 256), bf16),
            jax.ShapeDtypeStruct((heads, tokens, 256), bf16),
            jax.ShapeDtypeStruct((heads, tokens, 128), bf16),
        ),
        grid_spec=pltpu.PrefetchScalarGridSpec(
            num_scalar_prefetch=1,
            grid=(sets,),
            in_specs=[
                pl.BlockSpec((1, rows, d), lambda i, o: (i, 0, 0)),
                pl.BlockSpec(w.shape, lambda i, o: (0, 0)),
                pl.BlockSpec(b.shape, lambda i, o: (0, 0)),
                pl.BlockSpec(tab.shape, lambda i, o: (0, 0)),
                pl.BlockSpec((1, rows, 256), lambda i, o: (o[i], 0, 0)),
            ],
            out_specs=[
                pl.BlockSpec((heads, rows, 256), lambda i, o: (0, o[i], 0)),
                pl.BlockSpec((heads, rows, 256), lambda i, o: (0, o[i], 0)),
                pl.BlockSpec((heads, rows, 128), lambda i, o: (0, o[i], 0)),
            ],
        ),
        compiler_params=pltpu.CompilerParams(vmem_limit_bytes=VMEM_BYTES),
        cost_estimate=pl.CostEstimate(flops=2 * tokens * d * w.shape[1], bytes_accessed=tokens * d * 2 + heads * tokens * 640 * 2, transcendentals=0),
        name="prep",
    )(order, x, w, b, tab, hot)


def fwd_kernel(q_ref, k_ref, v_ref, att_ref, mix_ref, q2_ref, *, tile):
    lane = lane_iota((tile, 128))
    for i in range(q_ref.shape[1] // tile):
        at = pl.ds(i * tile, tile)
        q = q_ref[0, at, :]
        s = mm(q, k_ref[0], NT)
        m = jnp.max(s, axis=1, keepdims=True)
        p = jnp.exp(s - m)
        o = mm(p.astype(bf16), v_ref[0])
        total = o[:, 64:65]
        att = o / total
        lse = m + jnp.log(total)
        att_ref[0, at, :] = att
        mix_ref[0, at, :] = att[:, :64].astype(bf16)
        a = q[:, :128].astype(f32)
        b = q[:, 128:].astype(f32)
        full = a + roll(b, 32) - lse
        high = full.astype(bf16)
        low = roll(full - high.astype(f32), 96)
        q2_ref[0, at, :128] = jnp.where((lane >= LH) & (lane < LW), high.astype(f32), a).astype(bf16)
        q2_ref[0, at, 128:] = jnp.where((lane >= 32) & (lane < 80), low, b).astype(bf16)


def attend(q, k, v, head, steps, tile):
    heads, tokens, _ = q.shape
    block = tokens // steps
    return pl.pallas_call(
        partial(fwd_kernel, tile=tile),
        out_shape=(
            jax.ShapeDtypeStruct((1, tokens, 128), f32),
            jax.ShapeDtypeStruct((1, tokens, 64), bf16),
            jax.ShapeDtypeStruct((1, tokens, 256), bf16),
        ),
        grid=(steps,),
        in_specs=[
            pl.BlockSpec((1, block, 256), lambda i: (head, i, 0)),
            pl.BlockSpec((1, tokens, 256), lambda i: (head, 0, 0)),
            pl.BlockSpec((1, tokens, 128), lambda i: (head, 0, 0)),
        ],
        out_specs=[
            pl.BlockSpec((1, block, 128), lambda i: (0, i, 0)),
            pl.BlockSpec((1, block, 64), lambda i: (0, i, 0)),
            pl.BlockSpec((1, block, 256), lambda i: (0, i, 0)),
        ],
        compiler_params=pltpu.CompilerParams(vmem_limit_bytes=VMEM_BYTES),
        cost_estimate=pl.CostEstimate(flops=2 * tokens * tokens * 512, bytes_accessed=tokens * 2000, transcendentals=tokens * tokens),
        name="attend",
    )(q, k, v)


def bwd_kernel(q_ref, k_ref, v_ref, g_ref, att_ref, tab_ref, turn_ref, dq_ref, dk_ref, dv_ref, gr_ref, go_ref, kt_ref, acc_ref, lo_ref, *, tile, sets, zparts):
    step = pl.program_id(0)
    tokens = q_ref.shape[1]
    lane = lane_iota((tokens, 128))

    @pl.when(step == 0)
    def _():
        go = jnp.concatenate([g_ref[0].astype(f32), jnp.zeros((tokens, 64), f32)], axis=1)
        dot = jnp.sum(go * att_ref[0], axis=1, keepdims=True)
        high = dot.astype(bf16).astype(f32)
        mid = (dot - high).astype(bf16).astype(f32)
        low = dot - high - mid
        go_ref[...] = jnp.where(lane < 64, go, jnp.where(lane == 64, -high, jnp.where(lane == 65, -mid, jnp.where(lane == 66, -low, 0.0)))).astype(bf16)
        acc_ref[...] = jnp.zeros_like(acc_ref)
        kt_ref[:LW] = k_ref[0, :, :128].T[:LW]
        kt_ref[LW:] = turn_ref[...]

    keys = k_ref.shape[1] // pl.num_programs(0)
    for i in range(keys // tile):
        at = pl.ds(pl.multiple_of(step * keys + i * tile, tile), tile)
        s = mm(k_ref[0, at, :], q_ref[0], NT)
        p = jnp.exp(s)
        pb = p.astype(bf16)
        d = (p * mm(v_ref[0, at, :], go_ref[...], NT)).astype(bf16)
        dv_ref[0, i * tile:(i + 1) * tile, :] = mm(pb, go_ref[...]).astype(bf16)
        dk_ref[0, i * tile:(i + 1) * tile, :] = mm(d, q_ref[0, :, :128]).astype(bf16)
        acc_ref[...] += mm(kt_ref[:, at], d)

    @pl.when(step == pl.num_programs(0) - 1)
    def _():
        rows = tokens // sets
        part = rows // zparts
        small = lane_iota((G, 128))
        a = acc_ref[:128].T
        b = jnp.concatenate([acc_ref[128:160], jnp.zeros((96, tokens), f32)], axis=0).T
        for g in range(tokens // G):
            st, rest = divmod(g, rows // G)
            zsrc, inner = divmod(rest, part // G)
            r = zsrc * (sets * part // G) + st * (part // G) + inner
            ag = a[g * G:(g + 1) * G]
            bg = b[g * G:(g + 1) * G]
            along_h = jnp.where((small >= LH) & (small < LW), ag, 0.0)
            along_w = jnp.where(small >= LW, ag, jnp.where(small < 32, bg, 0.0))
            along_h = roll(along_h, (G - 1 - LH - r) % 128)
            along_w = roll(along_w, (128 - LW) % 128, 1)
            h_hi = along_h.astype(bf16)
            w_hi = along_w.astype(bf16)
            gr_ref[0, g * G:(g + 1) * G, :128] = h_hi
            gr_ref[0, g * G:(g + 1) * G, 128:] = w_hi
            lo_ref[g * G:(g + 1) * G, :128] = (along_h - h_hi.astype(f32)).astype(bf16)
            lo_ref[g * G:(g + 1) * G, 128:] = (along_w - w_hi.astype(f32)).astype(bf16)
        turned = mm(gr_ref[0], tab_ref[...], NT) + mm(lo_ref[...], tab_ref[...], NT)
        dq_ref[0] = jnp.where(lane < 64, a * (HD ** -0.5) + turned, 0.0).astype(bf16)


def attend_back(q2, k, v, g, att, tab, turn, head, steps, tile, sets, zparts):
    _, tokens, _ = q2.shape
    block = tokens // steps
    return pl.pallas_call(
        partial(bwd_kernel, tile=tile, sets=sets, zparts=zparts),
        out_shape=(
            jax.ShapeDtypeStruct((1, tokens, 128), bf16),
            jax.ShapeDtypeStruct((1, tokens, 128), bf16),
            jax.ShapeDtypeStruct((1, tokens, 128), bf16),
            jax.ShapeDtypeStruct((1, tokens, 256), bf16),
        ),
        grid=(steps,),
        in_specs=[
            pl.BlockSpec((1, tokens, 256), lambda i: (0, 0, 0)),
            pl.BlockSpec((1, tokens, 256), lambda i: (head, 0, 0)),
            pl.BlockSpec((1, tokens, 128), lambda i: (head, 0, 0)),
            pl.BlockSpec((1, tokens, 64), lambda i: (0, 0, 0)),
            pl.BlockSpec((1, tokens, 128), lambda i: (0, 0, 0)),
            pl.BlockSpec(tab.shape, lambda i: (0, 0)),
            pl.BlockSpec(turn.shape, lambda i: (0, 0)),
        ],
        out_specs=[
            pl.BlockSpec((1, tokens, 128), lambda i: (0, 0, 0)),
            pl.BlockSpec((1, block, 128), lambda i: (0, i, 0)),
            pl.BlockSpec((1, block, 128), lambda i: (0, i, 0)),
            pl.BlockSpec((1, tokens, 256), lambda i: (0, 0, 0)),
        ],
        scratch_shapes=[
            pltpu.VMEM((tokens, 128), bf16),
            pltpu.VMEM((160, tokens), bf16),
            pltpu.VMEM((160, tokens), f32),
            pltpu.VMEM((tokens, 256), bf16),
        ],
        compiler_params=pltpu.CompilerParams(vmem_limit_bytes=VMEM_BYTES),
        cost_estimate=pl.CostEstimate(flops=2 * tokens * tokens * 1280, bytes_accessed=tokens * 3000, transcendentals=tokens * tokens),
        name="attend_back",
    )(q2, k, v, g, att, tab, turn)


TN = (((0,), (0,)), ((), ()))
GC = 384


def norm(v, gain, bias):
    mean = jnp.mean(v, axis=1, keepdims=True)
    centered = v - mean
    inverse = lax.rsqrt(jnp.mean(centered * centered, axis=1, keepdims=True) + eps)
    unit = centered * inverse
    return unit * gain + bias, unit, inverse


def norm_back(upstream, unit, inverse, gain):
    scaled = upstream * gain
    return inverse * (scaled - jnp.mean(scaled, axis=1, keepdims=True) - unit * jnp.mean(scaled * unit, axis=1, keepdims=True))


def mlp_kernel(mix_ref, src_ref, top_ref, up_ref, down_ref, proj_ref, ub_ref, vec_ref,
               out_ref, act_ref, hg_ref, n2_ref, mg_ref, br_ref, mgrad_ref, ubg_ref, vg_ref,
               mid_ref, unit_ref, inv_ref, acc_ref, ng_ref):
    step = pl.program_id(0)
    last = pl.num_programs(0) - 1
    d = src_ref.shape[1]
    half = proj_ref.shape[3]

    def proj(i):
        return proj_ref[:, i].reshape(d, half)

    @pl.when(step == 0)
    def _():
        mid = src_ref[...].astype(f32) + vec_ref[0:1] + mm(mix_ref[:, :half], proj(0), NT) + mm(mix_ref[:, half:], proj(1), NT)
        normed, unit, inverse = norm(mid, vec_ref[1:2], vec_ref[2:3])
        mid_ref[...] = mid
        unit_ref[...] = unit
        inv_ref[...] = inverse
        n2_ref[...] = normed.astype(bf16)

    tile = up_ref.shape[3]
    up = up_ref[:, 0].reshape(d, tile)
    down = down_ref[:, 0].reshape(d, tile)
    hidden = mm(n2_ref[...], up) + ub_ref[...]
    phi_all = 0.5 + 0.5 * lax.erf(hidden * (0.5 ** 0.5))
    slope = phi_all + hidden * (jnp.exp(-0.5 * hidden * hidden) * 0.3989422804014327)
    active = (hidden * phi_all).astype(bf16)
    hg = (mm(top_ref[...], down) * slope).astype(bf16)
    act_ref[...] = active
    hg_ref[...] = hg
    ubg_ref[...] = jnp.sum(hg.astype(f32), axis=0, keepdims=True)
    out = mm(active, down, NT)
    ng = mm(hg, up, NT)

    @pl.when(step == 0)
    def _():
        acc_ref[...] = out
        ng_ref[...] = ng

    @pl.when(step > 0)
    def _():
        acc_ref[...] += out
        ng_ref[...] += ng

    @pl.when(step == last)
    def _():
        top = top_ref[...].astype(f32)
        grad = ng_ref[...]
        unit = unit_ref[...]
        out_ref[...] = (mid_ref[...] + acc_ref[...] + vec_ref[3:4]).astype(bf16)
        middle = top + norm_back(grad, unit, inv_ref[...], vec_ref[1:2])
        branch = middle.astype(bf16)
        mg_ref[...] = middle
        br_ref[...] = branch
        mgrad_ref[:, :half] = mm(branch, proj(0)).astype(bf16)
        mgrad_ref[:, half:] = mm(branch, proj(1)).astype(bf16)
        vg_ref[0:1] = jnp.sum(branch.astype(f32), axis=0, keepdims=True)
        vg_ref[1:2] = jnp.sum(grad * unit, axis=0, keepdims=True)
        vg_ref[2:3] = jnp.sum(grad, axis=0, keepdims=True)
        vg_ref[3:4] = jnp.sum(top, axis=0, keepdims=True)


def mlp(mixed, src, top, packed, up_bias, vecs, half_ff, tile=512):
    rows, d = mixed.shape
    blocks, halves, depth, _ = packed.shape
    per = half_ff // tile
    steps = halves * per
    half = d // halves
    whole = lambda i: (0, 0)
    return pl.pallas_call(
        mlp_kernel,
        out_shape=(
            jax.ShapeDtypeStruct((rows, d), bf16),
            jax.ShapeDtypeStruct((rows, halves * half_ff), bf16),
            jax.ShapeDtypeStruct((rows, halves * half_ff), bf16),
            jax.ShapeDtypeStruct((rows, d), bf16),
            jax.ShapeDtypeStruct((rows, d), f32),
            jax.ShapeDtypeStruct((rows, d), bf16),
            jax.ShapeDtypeStruct((rows, d), bf16),
            jax.ShapeDtypeStruct((1, halves * half_ff), f32),
            jax.ShapeDtypeStruct((4, d), f32),
        ),
        grid=(steps,),
        in_specs=[
            pl.BlockSpec((rows, d), whole),
            pl.BlockSpec((rows, d), whole),
            pl.BlockSpec((rows, d), whole),
            pl.BlockSpec((blocks, 1, depth, tile), lambda i: (0, i // per, 0, i % per)),
            pl.BlockSpec((blocks, 1, depth, tile), lambda i: (0, i // per, 0, per + i % per)),
            pl.BlockSpec((blocks, halves, depth, half), lambda i: (0, 0, 0, 2 * half_ff // half)),
            pl.BlockSpec((1, tile), lambda i: (0, i)),
            pl.BlockSpec(vecs.shape, whole),
        ],
        out_specs=[
            pl.BlockSpec((rows, d), whole),
            pl.BlockSpec((rows, tile), lambda i: (0, i)),
            pl.BlockSpec((rows, tile), lambda i: (0, i)),
            pl.BlockSpec((rows, d), whole),
            pl.BlockSpec((rows, d), whole),
            pl.BlockSpec((rows, d), whole),
            pl.BlockSpec((rows, d), whole),
            pl.BlockSpec((1, tile), lambda i: (0, i)),
            pl.BlockSpec((4, d), whole),
        ],
        scratch_shapes=[
            pltpu.VMEM((rows, d), f32),
            pltpu.VMEM((rows, d), f32),
            pltpu.VMEM((rows, 1), f32),
            pltpu.VMEM((rows, d), f32),
            pltpu.VMEM((rows, d), f32),
        ],
        compiler_params=pltpu.CompilerParams(vmem_limit_bytes=VMEM_BYTES),
        cost_estimate=pl.CostEstimate(flops=2 * rows * d * (4 * halves * half_ff + 2 * d), bytes_accessed=4 * d * halves * half_ff + 20 * rows * d, transcendentals=2 * rows * halves * half_ff),
        name="mlp",
    )(mixed, src, top, packed, packed, packed, up_bias, vecs)


def wgrad_kernel(n2_ref, top_ref, br_ref, hg_ref, act_ref, mix_ref, out_ref, left_ref, *, per):
    half, block = pl.program_id(0), pl.program_id(1)
    blocks, depth = out_ref.shape[0], out_ref.shape[2]

    @pl.when((half == 0) & (block == 0))
    def _():
        left_ref[0] = n2_ref[...].T
        left_ref[1] = top_ref[...].T
        left_ref[2] = br_ref[...].T

    def put(i, right):
        out_ref[:, 0] = mm(left_ref[i], right[...]).astype(bf16).reshape(blocks, depth, -1)

    @pl.when(block < per)
    def _():
        put(0, hg_ref)

    @pl.when((block >= per) & (block < 2 * per))
    def _():
        put(1, act_ref)

    @pl.when(block == 2 * per)
    def _():
        put(2, mix_ref)


def wgrad(n2, top, branch, hg, active, mixed, blocks, halves):
    rows, d = n2.shape
    ff = hg.shape[1]
    tile = d // halves
    per = ff // halves // tile
    depth = d // blocks
    whole = lambda s, j: (0, 0)
    return pl.pallas_call(
        partial(wgrad_kernel, per=per),
        out_shape=jax.ShapeDtypeStruct((blocks, halves, depth, (2 * per + 1) * tile), bf16),
        grid=(halves, 2 * per + 1),
        in_specs=[
            pl.BlockSpec((rows, d), whole),
            pl.BlockSpec((rows, d), whole),
            pl.BlockSpec((rows, d), whole),
            pl.BlockSpec((rows, tile), lambda s, j: (0, s * per + jnp.minimum(j, per - 1))),
            pl.BlockSpec((rows, tile), lambda s, j: (0, s * per + jnp.clip(j - per, 0, per - 1))),
            pl.BlockSpec((rows, tile), lambda s, j: (0, s)),
        ],
        out_specs=pl.BlockSpec((blocks, 1, depth, tile), lambda s, j: (0, s, 0, j)),
        scratch_shapes=[pltpu.VMEM((3, d, rows), bf16)],
        compiler_params=pltpu.CompilerParams(vmem_limit_bytes=VMEM_BYTES),
        cost_estimate=pl.CostEstimate(flops=2 * rows * d * (2 * ff + d), bytes_accessed=4 * d * ff + 8 * rows * ff, transcendentals=0),
        name="wgrad",
    )(n2, top, branch, hg, active, mixed)


def close_kernel(order_ref, x_ref, w_ref, *refs, heads):
    parts, (ng_ref, wg_ref, bg_ref, acc_ref) = refs[:3 * heads], refs[3 * heads:]
    step = pl.program_id(0)
    whole = jnp.concatenate([p[0] for p in parts], axis=1)
    ng_ref[0] = mm(whole, w_ref[...], NT).astype(bf16)
    add = mm(x_ref[0].T, whole)
    sums = jnp.sum(whole.astype(f32), axis=0, keepdims=True)

    @pl.when(step == 0)
    def _():
        acc_ref[...] = add
        bg_ref[...] = sums

    @pl.when(step > 0)
    def _():
        acc_ref[...] += add
        bg_ref[...] += sums

    @pl.when(step == pl.num_programs(0) - 1)
    def _():
        wg_ref[...] = acc_ref[...].astype(bf16)


def close(x, w, grads, order, heads):
    sets, rows, d = x.shape
    width = w.shape[1]
    return pl.pallas_call(
        partial(close_kernel, heads=heads),
        out_shape=(
            jax.ShapeDtypeStruct((sets, rows, d), bf16),
            jax.ShapeDtypeStruct((d, width), bf16),
            jax.ShapeDtypeStruct((1, width), f32),
        ),
        grid_spec=pltpu.PrefetchScalarGridSpec(
            num_scalar_prefetch=1,
            grid=(sets,),
            in_specs=[
                pl.BlockSpec((1, rows, d), lambda i, o: (i, 0, 0)),
                pl.BlockSpec(w.shape, lambda i, o: (0, 0)),
            ] + [pl.BlockSpec((1, rows, 128), lambda i, o: (0, o[i], 0))] * (3 * heads),
            out_specs=[
                pl.BlockSpec((1, rows, d), lambda i, o: (i, 0, 0)),
                pl.BlockSpec((d, width), lambda i, o: (0, 0)),
                pl.BlockSpec((1, width), lambda i, o: (0, 0)),
            ],
            scratch_shapes=[pltpu.VMEM((d, width), f32)],
        ),
        compiler_params=pltpu.CompilerParams(vmem_limit_bytes=VMEM_BYTES),
        cost_estimate=pl.CostEstimate(flops=4 * sets * rows * d * width, bytes_accessed=2 * sets * rows * (2 * d + width), transcendentals=0),
        name="close",
    )(order, x, w, *grads)


def pairs_of(shape, move):
    nf, nc, nt = shape["fsdp"], shape["ctx"], shape["tp"]
    out = []
    for f in range(nf):
        for z in range(nc):
            for t in range(nt):
                g, w, u = move(f, z, t)
                out.append(((f * nc + z) * nt + t, (g * nc + w) * nt + u))
    return out


AXES = ("fsdp", "ctx", "tp")


def grouped(
    shape,
    images,
    norm1_gain,
    norm1_bias,
    qkv_weight,
    qv_bias,
    rel_pos_h,
    rel_pos_w,
    proj_weight,
    proj_bias,
    norm2_gain,
    norm2_bias,
    up_weight,
    up_bias,
    down_weight,
    down_bias,
    out_cotangent,
):
    nf, nc, nt = shape["fsdp"], shape["ctx"], shape["tp"]
    batch, quarter, d = images.shape
    sets = 2 * nt
    chunk = quarter // sets
    rows = nc * chunk
    tokens = sets * rows
    half = qkv_weight.shape[2]
    width = half // 2
    heads = width // HD
    depth = qkv_weight.shape[1]
    blocks = nf * nc
    half_ff = up_weight.shape[1]
    fi, z, t = lax.axis_index("fsdp"), lax.axis_index("ctx"), lax.axis_index("tp")
    c = fi % 2
    me = 2 * t + c

    def send(x, move):
        return lax.ppermute(x, AXES, pairs_of(shape, move))

    core = lambda x: send(x, lambda f, w, u: (f ^ 1, w, u))
    across = lambda x: send(x, lambda f, w, u: (f, w, u ^ 1))
    diagonal = lambda x: send(x, lambda f, w, u: (f ^ 1, w, u ^ 1))
    xswap = lambda x: send(x, lambda f, w, u: (f ^ 2, w, u))
    zswap = lambda x, k: send(x, lambda f, w, u: (f, w ^ k, u))

    def pick(x, i, axis=0):
        return lax.dynamic_index_in_dim(x, i, axis, keepdims=False)

    def ordered(bit, mine, other, axis=0):
        return jnp.where(bit == 0, jnp.concatenate([mine, other], axis), jnp.concatenate([other, mine], axis))

    f = lambda v: v.astype(f32)

    packed = lax.all_gather(
        jnp.concatenate([up_weight, down_weight, proj_weight], axis=1), AXES, axis=0, tiled=False
    ).reshape(blocks, nt, depth, 2 * half_ff + half)

    def scatter_tokens(x):
        parts = x.reshape(batch, sets, chunk, d)
        four = ordered(c, pick(parts, me, 1), core(pick(parts, me ^ 1, 1)))
        return lax.all_to_all(four, "ctx", 0, 0, tiled=True).reshape(rows, d)

    def gather_tokens(x):
        four = lax.all_to_all(x.reshape(nc, chunk, d), "ctx", 0, 0, tiled=True).reshape(2, batch, 1, chunk, d)
        mine = ordered(c, pick(four, c), core(pick(four, 1 - c)), 1)
        return ordered(t, mine, across(mine), 1).reshape(batch, quarter, d)

    src = scatter_tokens(images)
    normed_f, unit1, inverse1 = norm(f(src), f(norm1_gain), f(norm1_bias))
    normed = normed_f.astype(bf16)
    other = across(normed)
    near = core(jnp.stack([normed, other]))
    all_normed = jnp.stack([normed, near[0], other, near[1]])
    order = jnp.arange(sets, dtype=jnp.int32) ^ me

    cols = qkv_weight.reshape(3, depth, 2, width)
    w = ordered(c, pick(cols, c, 2)[None], core(pick(cols, 1 - c, 2))[None])
    step = 1
    w = w[None]
    while step < nc:
        w = ordered((z // step) % 2, w, zswap(w, step))
        step *= 2
    w = w[None]
    w = ordered(fi // 2, w, xswap(w))
    w = w.transpose(0, 2, 1, 4, 3, 5).reshape(d, 3, heads, HD)
    w = jnp.pad(w, ((0, 0), (0, 0), (0, 0), (0, HD))).reshape(d, 3 * heads * 2 * HD)
    bias = pick(qv_bias.reshape(2, 2, heads, HD), c, 1)
    bias = jnp.stack([bias[0], jnp.zeros_like(bias[0]), bias[1]])
    bias = jnp.pad(f(bias), ((0, 0), (0, 0), (0, HD))).reshape(1, -1)

    flip = lambda v: jnp.pad(v[::-1].T, ((0, HD), (0, 128 - (2 * G - 1))))
    plain = lambda v: jnp.pad(v.T, ((0, HD), (0, 128 - (2 * G - 1))))
    tab = jnp.concatenate([flip(rel_pos_h), flip(rel_pos_w)], axis=1)
    tab_back = jnp.concatenate([flip(rel_pos_h), plain(rel_pos_w)], axis=1)
    place = np.array([w_ * quarter + s * chunk + i for s in range(sets) for w_ in range(nc) for i in range(chunk)])
    at = np.arange(tokens)
    hot = np.zeros((tokens, 256), np.float32)
    for base, index in ((LH, place // G), (LW, place % G), (160, place // G), (208, place % G)):
        hot[at, base + index] = 1
    turn = np.zeros((G, tokens), np.float32)
    turn[G - 1 - place % G, at] = 1
    hot = jnp.asarray(hot.astype(ml_dtypes.bfloat16).reshape(sets, rows, 256))
    turn = jnp.asarray(turn.astype(ml_dtypes.bfloat16))

    q, k, v = prep(all_normed, w, bias, tab, hot, order, heads, nc)
    forward = [attend(q, k, v, h, 3, 256) for h in range(heads)]

    def swap_blocks(x):
        got = jnp.stack([pick(x, me), core(pick(x, me ^ 1)), across(pick(x, me ^ 2)), diagonal(pick(x, me ^ 3))])
        return jnp.stack([pick(got, i ^ me) for i in range(sets)])

    mixed = jnp.concatenate([m[1][0] for m in forward], axis=1).reshape(sets, rows, width)
    mixed = swap_blocks(mixed).transpose(1, 0, 2).reshape(rows, d)

    top = scatter_tokens(out_cotangent)
    full_bias = f(jnp.where(t == 0, jnp.concatenate([up_bias, up_bias]), jnp.concatenate([up_bias, up_bias])))
    other_bias = f(across(up_bias))
    full_bias = ordered(t, f(up_bias), other_bias)[None]
    vecs = jnp.stack([f(proj_bias), f(norm2_gain), f(norm2_bias), f(down_bias)])
    result, active, hidden_grad, normed2, middle_grad, branch, mixed_grad, up_bias_grad, vec_grads = mlp(
        mixed, src, top, packed, full_bias, vecs, half_ff, 512
    )
    big = wgrad(normed2, top, branch, hidden_grad, active, mixed, blocks, nt)
    big = lax.psum_scatter(big.reshape(blocks * nt, depth, -1), AXES, scatter_dimension=0, tiled=True)
    big = f(big.reshape(depth, -1))

    back = swap_blocks(mixed_grad.reshape(rows, sets, width).transpose(1, 0, 2))
    back = back.reshape(tokens, heads, HD).transpose(1, 0, 2)
    grads = [
        attend_back(forward[h][2], k, v, back[h:h + 1], forward[h][0], tab_back, turn, h, 3, 256, sets, nc)
        for h in range(heads)
    ]
    tables = sum(
        lax.dot_general(g[3][0], q[h, :, :HD], (((0,), (0,)), ((), ())), preferred_element_type=f32)
        for h, g in enumerate(grads)
    ) * HD ** 0.5
    small_part, weight_part, sums = close(
        all_normed, w, [g[j] for j in range(3) for g in grads], order, heads
    )

    got = core(jnp.stack([small_part[1], small_part[3]]))
    normed_grad = f(small_part[0]) + f(got[0]) + f(across((f(small_part[2]) + f(got[1])).astype(bf16)))
    input_grad = (middle_grad + norm_back(normed_grad, unit1, inverse1, f(norm1_gain))).astype(bf16)
    result = gather_tokens(result)
    input_grad = gather_tokens(input_grad)

    wg = weight_part.reshape(nf // 2, 2, nc, depth, 3, heads, 2 * HD)[..., :HD].reshape(nf // 2, 2, nc, depth, 3, width)
    wg = wg.transpose(0, 2, 1, 4, 3, 5)
    wg = f(pick(wg, fi // 2)) + f(xswap(pick(wg, 1 - fi // 2)))
    step = nc // 2
    while step:
        bit = (z // step) % 2
        wg = wg.reshape((2, step) + wg.shape[1:])
        wg = pick(wg, bit) + f(zswap(pick(wg, 1 - bit).astype(bf16), step))
        step //= 2
    wg = wg[0].astype(bf16)
    wg = f(ordered(c, pick(wg, c)[:, :, None], core(pick(wg, 1 - c))[:, :, None], 2).reshape(3, depth, half))

    def total(x):
        for move in (core, across, xswap):
            x = x + move(x)
        step = 1
        while step < nc:
            x = x + zswap(x, step)
            step *= 2
        return x

    sums = sums.reshape(3, heads, 2 * HD)[:, :, :HD].reshape(3, width)[::2]
    sums = jnp.where(jnp.arange(sets)[:, None, None] == me, sums[None], 0.0)
    sums = sums.transpose(1, 0, 2).reshape(2, d)
    vectors = jnp.concatenate(
        [
            jnp.sum(normed_grad * unit1, axis=0),
            jnp.sum(normed_grad, axis=0),
            vec_grads.reshape(-1),
            sums.reshape(-1),
            up_bias_grad.reshape(-1),
            tables.reshape(-1),
        ]
    )
    vectors = total(vectors.reshape(-1, 128)).reshape(-1)
    at = 0
    cut = []
    for size in (d, d, d, d, d, d, 2 * d, nt * half_ff, 256 * HD):
        cut.append(lax.slice(vectors, (at,), (at + size,)))
        at += size
    g1, b1, pb, g2, b2, db, qv, ub, tg = cut
    tg = tg.reshape(256, HD)
    return (
        result,
        input_grad,
        g1,
        b1,
        wg,
        pick(qv.reshape(2, nt, half), t, 1),
        tg[: 2 * G - 1][::-1],
        tg[128 : 128 + 2 * G - 1],
        big[:, 2 * half_ff :],
        pb,
        g2,
        b2,
        big[:, :half_ff],
        pick(ub.reshape(nt, half_ff), t),
        big[:, half_ff : 2 * half_ff],
        db,
    )


def layer_norm(values, gain_vec, shift_vec):
    centered = values - jnp.mean(values, axis=-1, keepdims=True)
    inverse = lax.rsqrt(jnp.mean(centered * centered, axis=-1, keepdims=True) + eps)
    standard = centered * inverse
    return (standard * gain_vec + shift_vec, standard, inverse)


def norm_back_plain(upstream, standard, inverse, gain_vec):
    scaled = upstream * gain_vec
    mean_term = jnp.mean(scaled, axis=-1, keepdims=True)
    proj_term = jnp.mean(scaled * standard, axis=-1, keepdims=True)
    return inverse * (scaled - mean_term - standard * proj_term)


def exact_gelu(values):
    return jax.nn.gelu(values, approximate=False)


def table_rows(pos_table, first_row, num_rows):
    table_len = pos_table.shape[0]
    grid_side = (table_len + 1) // 2
    query_row = first_row + lax.broadcasted_iota(jnp.int32, (num_rows, grid_side, table_len), 0)
    key_row = lax.broadcasted_iota(jnp.int32, (num_rows, grid_side, table_len), 1)
    entry_idx = lax.broadcasted_iota(jnp.int32, (num_rows, grid_side, table_len), 2)
    chooser = (query_row - key_row + grid_side - 1 == entry_idx).astype(jnp.float32)
    chooser = chooser.reshape(num_rows * grid_side, table_len)
    picked = jnp.dot(chooser, pos_table, precision=highest)
    return (picked.reshape(num_rows, grid_side, -1), chooser)


def rel_terms(query_f, row_first, rel_h, rel_w):
    grid_rows = query_f.shape[0] // G
    head_count = query_f.shape[1]
    near_h, pick_h = table_rows(rel_h, row_first, grid_rows)
    near_w, pick_w = table_rows(rel_w, 0, G)
    shaped = query_f.reshape(grid_rows, G, head_count, query_f.shape[2])
    term_h = jnp.einsum("awhc,akc->awhk", shaped, near_h, precision=highest)
    term_w = jnp.einsum("awhc,wkc->awhk", shaped, near_w, precision=highest)
    return (
        term_h.reshape(-1, head_count, G),
        term_w.reshape(-1, head_count, G),
        near_h,
        near_w,
        pick_h,
        pick_w,
    )


def piece_scores(query, key_h, term_h, term_w, factor):
    num_keys = key_h.shape[0]
    products = jnp.einsum("rhc,nhc->rhn", query, key_h, preferred_element_type=jnp.float32)
    position = (term_h[..., :, None] + term_w[..., None, :]).reshape(
        term_h.shape[0], term_h.shape[1], num_keys
    )
    return products * factor + position


def attend_step(running, pieces, offset, query, term_h, term_w, factor):
    run_max, run_sum, accumulated = running
    key_piece, value_piece = pieces
    num_keys = key_piece.shape[0]
    head_count = query.shape[1]
    key_h = key_piece.reshape(num_keys, head_count, -1)
    value_h = value_piece.reshape(num_keys, head_count, -1)
    scores = piece_scores(query, key_h, term_h, term_w, factor)
    new_max = jnp.maximum(run_max, jnp.max(scores, axis=-1))
    weights_p = jnp.exp(scores - new_max[..., None])
    run_sum = jnp.sum(weights_p, axis=-1)
    accumulated = jnp.einsum(
        "rhn,nhc->rhc", weights_p.astype(jnp.bfloat16), value_h, preferred_element_type=jnp.float32
    )
    return (new_max, run_sum, accumulated)


def grad_step(running, pieces, offset, query, out_grad, log_total, row_dot, term_h, term_w, factor):
    key_piece, value_piece = pieces
    num_keys = key_piece.shape[0]
    num_rows, head_count, head_size = query.shape
    key_h = key_piece.reshape(num_keys, head_count, head_size)
    value_h = value_piece.reshape(num_keys, head_count, head_size)
    scores = piece_scores(query, key_h, term_h, term_w, factor)
    weights_p = jnp.exp(scores - log_total[..., None])
    prob_grad = jnp.einsum("rhc,nhc->rhn", out_grad, value_h, preferred_element_type=jnp.float32)
    score_grad = (weights_p * (prob_grad - row_dot[..., None])).astype(jnp.bfloat16)
    query_acc = jnp.einsum("rhn,nhc->rhc", score_grad, key_h, preferred_element_type=jnp.float32)
    key_grad = (
        jnp.einsum("rhn,rhc->nhc", score_grad, query, preferred_element_type=jnp.float32) * factor
    )
    value_grad = jnp.einsum(
        "rhn,rhc->nhc", weights_p.astype(jnp.bfloat16), out_grad, preferred_element_type=jnp.float32
    )
    joined = jnp.concatenate(
        [key_grad.reshape(num_keys, -1), value_grad.reshape(num_keys, -1)], axis=1
    )
    grid_grad = score_grad.reshape(num_rows, head_count, num_keys // G, G)
    part_h = jnp.sum(grid_grad, axis=-1, dtype=jnp.float32)
    grad_w = jnp.sum(grid_grad, axis=-2, dtype=jnp.float32)
    return (query_acc, joined, part_h, grad_w)


def tensor_total(partial_sum):
    return lax.psum(partial_sum.astype(jnp.bfloat16), "tp").astype(jnp.float32)


def contract_last(left_mat, right_mat):
    return lax.dot_general(
        left_mat, right_mat, (((1,), (1,)), ((), ())), preferred_element_type=jnp.float32
    )


def micro_step(weights_full, picture, cotangent, params):
    (
        gain_one,
        shift_one,
        qv_shift,
        rel_h,
        rel_w,
        proj_shift,
        gain_two,
        shift_two,
        up_shift,
        down_shift,
    ) = params
    qkv_full, proj_full, up_full, down_full = weights_full
    rows_dev = picture.shape[0]
    half_width = qkv_full.shape[2]
    head_count = half_width // HD
    grid_rows = rows_dev // G
    row_first = lax.axis_index("ctx") * grid_rows
    factor = HD ** (-0.5)
    source = picture.astype(jnp.float32)
    normed_f, standard_one, inverse_one = layer_norm(source, gain_one, shift_one)
    normed = normed_f.astype(jnp.bfloat16)
    projected = jnp.einsum("rd,jde->jre", normed, qkv_full, preferred_element_type=jnp.float32)
    query_flat = (projected[0] + qv_shift[0]).astype(jnp.bfloat16)
    key_flat = projected[1].astype(jnp.bfloat16)
    value_flat = (projected[2] + qv_shift[1]).astype(jnp.bfloat16)
    query = query_flat.reshape(rows_dev, head_count, HD)
    query_f = query.astype(jnp.float32)
    term_h, term_w, near_h, near_w, pick_h, pick_w = rel_terms(query_f, row_first, rel_h, rel_w)
    start_state = (
        jnp.full((rows_dev, head_count), -1e30, jnp.float32),
        jnp.zeros((rows_dev, head_count), jnp.float32),
        jnp.zeros((rows_dev, head_count, HD), jnp.float32),
    )
    forward_fn = partial(attend_step, query=query, term_h=term_h, term_w=term_w, factor=factor)
    run_max, run_sum, accumulated = forward_fn(
        start_state,
        (
            lax.all_gather(key_flat, "ctx", axis=0, tiled=True),
            lax.all_gather(value_flat, "ctx", axis=0, tiled=True),
        ),
        jnp.int32(0),
    )
    attended = accumulated / run_sum[..., None]
    log_total = run_max + jnp.log(run_sum)
    mixed = attended.reshape(rows_dev, half_width).astype(jnp.bfloat16)
    middle = source + tensor_total(contract_last(mixed, proj_full)) + proj_shift
    normed2_f, standard_two, inverse_two = layer_norm(middle, gain_two, shift_two)
    normed2 = normed2_f.astype(jnp.bfloat16)
    hidden = jnp.dot(normed2, up_full, preferred_element_type=jnp.float32) + up_shift
    active, gelu_back = jax.vjp(exact_gelu, hidden)
    active_low = active.astype(jnp.bfloat16)
    result = (middle + tensor_total(contract_last(active_low, down_full)) + down_shift).astype(
        jnp.bfloat16
    )
    top_f = cotangent.astype(jnp.float32)
    down_grad = jnp.einsum("rd,rf->df", cotangent, active_low, preferred_element_type=jnp.float32)
    down_shift_grad = jnp.sum(top_f, axis=0)
    active_grad = jnp.dot(cotangent, down_full, preferred_element_type=jnp.float32)
    hidden_grad = gelu_back(active_grad)[0].astype(jnp.bfloat16)
    up_grad = jnp.einsum("rd,rf->df", normed2, hidden_grad, preferred_element_type=jnp.float32)
    up_shift_grad = jnp.sum(hidden_grad, axis=0, dtype=jnp.float32)
    normed2_grad = lax.psum(contract_last(hidden_grad, up_full).astype(jnp.bfloat16), "tp").astype(
        jnp.float32
    )
    middle_grad = top_f + norm_back_plain(normed2_grad, standard_two, inverse_two, gain_two)
    gain_two_grad = jnp.sum(normed2_grad * standard_two, axis=0)
    shift_two_grad = jnp.sum(normed2_grad, axis=0)
    branch_grad = middle_grad.astype(jnp.bfloat16)
    proj_grad = jnp.einsum("rd,re->de", branch_grad, mixed, preferred_element_type=jnp.float32)
    proj_shift_grad = jnp.sum(branch_grad, axis=0, dtype=jnp.float32)
    mixed_grad = (
        jnp.dot(branch_grad, proj_full, preferred_element_type=jnp.float32)
        .astype(jnp.bfloat16)
        .reshape(rows_dev, head_count, HD)
    )
    row_dot = jnp.sum(mixed_grad.astype(jnp.float32) * attended, axis=-1)
    ctx_count = lax.axis_size("ctx")
    start_back = (
        jnp.zeros((rows_dev, head_count, HD), jnp.float32),
        jnp.zeros((rows_dev * ctx_count, 2 * half_width), jnp.float32),
        jnp.zeros((rows_dev, head_count, G), jnp.float32),
        jnp.zeros((rows_dev, head_count, G), jnp.float32),
    )
    back_fn = partial(
        grad_step,
        query=query,
        out_grad=mixed_grad,
        log_total=log_total,
        row_dot=row_dot,
        term_h=term_h,
        term_w=term_w,
        factor=factor,
    )
    query_acc, key_value_acc, grad_h, grad_w = back_fn(
        start_back,
        (
            lax.all_gather(key_flat, "ctx", axis=0, tiled=True),
            lax.all_gather(value_flat, "ctx", axis=0, tiled=True),
        ),
        jnp.int32(0),
    )
    key_value_mine = lax.psum_scatter(
        key_value_acc.astype(jnp.bfloat16), "ctx", scatter_dimension=0, tiled=True
    ).astype(jnp.float32)
    grid_h = grad_h.reshape(grid_rows, G, head_count, G)
    grid_w = grad_w.reshape(grid_rows, G, head_count, G)
    shaped_q = query_f.reshape(grid_rows, G, head_count, HD)
    rel_query = jnp.einsum("awhk,akc->awhc", grid_h, near_h, precision=highest) + jnp.einsum(
        "awhk,wkc->awhc", grid_w, near_w, precision=highest
    )
    query_grad = (
        (query_acc * factor + rel_query.reshape(rows_dev, head_count, HD))
        .reshape(rows_dev, half_width)
        .astype(jnp.bfloat16)
    )
    key_grad = key_value_mine[:, :half_width].astype(jnp.bfloat16)
    value_grad = key_value_mine[:, half_width:].astype(jnp.bfloat16)
    table_h_part = jnp.dot(
        pick_h.T,
        jnp.einsum("awhk,awhc->akc", grid_h, shaped_q, precision=highest).reshape(-1, HD),
        precision=highest,
    )
    table_w_part = jnp.dot(
        pick_w.T,
        jnp.einsum("awhk,awhc->wkc", grid_w, shaped_q, precision=highest).reshape(-1, HD),
        precision=highest,
    )
    stacked = jnp.stack([query_grad, key_grad, value_grad])
    qkv_grad = jnp.einsum("rd,jre->jde", normed, stacked, preferred_element_type=jnp.float32)
    qv_shift_grad = jnp.stack(
        [
            jnp.sum(query_grad, axis=0, dtype=jnp.float32),
            jnp.sum(value_grad, axis=0, dtype=jnp.float32),
        ]
    )
    normed_part = jnp.einsum("jre,jde->rd", stacked, qkv_full, preferred_element_type=jnp.float32)
    normed_grad, table_h_grad, table_w_grad = (
        lax.psum(normed_part.astype(jnp.bfloat16), "tp").astype(jnp.float32),
        lax.psum(table_h_part.astype(jnp.bfloat16), "tp").astype(jnp.float32),
        lax.psum(table_w_part.astype(jnp.bfloat16), "tp").astype(jnp.float32),
    )
    input_grad = (middle_grad + norm_back_plain(normed_grad, standard_one, inverse_one, gain_one)).astype(
        jnp.bfloat16
    )
    gain_one_grad = jnp.sum(normed_grad * standard_one, axis=0)
    shift_one_grad = jnp.sum(normed_grad, axis=0)
    big_grads = (qkv_grad, proj_grad, up_grad, down_grad)
    small_grads = (
        gain_one_grad,
        shift_one_grad,
        qv_shift_grad,
        table_h_grad,
        table_w_grad,
        proj_shift_grad,
        gain_two_grad,
        shift_two_grad,
        up_shift_grad,
        down_shift_grad,
    )
    return (result, input_grad, big_grads, small_grads)


def add_trees(first_tree, second_tree):
    return jax.tree.map(lambda first_v, second_v: first_v + second_v, first_tree, second_tree)


def zeros_like_tree(tree):
    return jax.tree.map(lambda member: jnp.zeros(member.shape, jnp.float32), tree)


def local(
    images,
    norm1_gain,
    norm1_bias,
    qkv_weight,
    qv_bias,
    rel_pos_h,
    rel_pos_w,
    proj_weight,
    proj_bias,
    norm2_gain,
    norm2_bias,
    up_weight,
    up_bias,
    down_weight,
    down_bias,
    out_cotangent,
):
    params = tuple(
        (
            member.astype(jnp.float32)
            for member in (
                norm1_gain,
                norm1_bias,
                qv_bias,
                rel_pos_h,
                rel_pos_w,
                proj_bias,
                norm2_gain,
                norm2_bias,
                up_bias,
                down_bias,
            )
        )
    )
    small_start = zeros_like_tree(params)

    def per_batch(totals, pair):
        weights_full = (
            lax.all_gather(qkv_weight, ("fsdp", "ctx"), axis=1, tiled=True),
            lax.all_gather(proj_weight, ("fsdp", "ctx"), axis=0, tiled=True),
            lax.all_gather(up_weight, ("fsdp", "ctx"), axis=0, tiled=True),
            lax.all_gather(down_weight, ("fsdp", "ctx"), axis=0, tiled=True),
        )
        result, input_grad, big_grads, small_grads = micro_step(
            weights_full, pair[0], pair[1], params
        )
        shards = (
            lax.psum_scatter(big_grads[0], ("fsdp", "ctx"), scatter_dimension=1, tiled=True),
            lax.psum_scatter(big_grads[1], ("fsdp", "ctx"), scatter_dimension=0, tiled=True),
            lax.psum_scatter(big_grads[2], ("fsdp", "ctx"), scatter_dimension=0, tiled=True),
            lax.psum_scatter(big_grads[3], ("fsdp", "ctx"), scatter_dimension=0, tiled=True),
        )
        return (add_trees(totals, (shards, small_grads)), (result, input_grad))

    shard_start = zeros_like_tree((qkv_weight, proj_weight, up_weight, down_weight))
    (shard_totals, small_totals), (outputs, input_grads) = lax.scan(
        per_batch, (shard_start, small_start), (images, out_cotangent)
    )
    small_final = lax.psum(small_totals, ("fsdp", "ctx"))
    return (
        outputs,
        input_grads,
        small_final[0],
        small_final[1],
        shard_totals[0],
        small_final[2],
        small_final[3],
        small_final[4],
        shard_totals[1],
        small_final[5],
        small_final[6],
        small_final[7],
        shard_totals[2],
        small_final[8],
        shard_totals[3],
        small_final[9],
    )


def solution(mesh):
    shape = dict(mesh.shape)
    body = partial(grouped, shape) if shape["fsdp"] == 4 and shape["ctx"] == 4 and shape["tp"] == 2 else local
    placed = (
        P("fsdp", "ctx", None),
        P(),
        P(),
        P(None, ("fsdp", "ctx"), "tp"),
        P(None, "tp"),
        P(),
        P(),
        P(("fsdp", "ctx"), "tp"),
        P(),
        P(),
        P(),
        P(("fsdp", "ctx"), "tp"),
        P("tp"),
        P(("fsdp", "ctx"), "tp"),
        P(),
        P("fsdp", "ctx", None),
    )
    return jax.shard_map(
        body,
        mesh=mesh,
        in_specs=placed,
        out_specs=(
            P("fsdp", "ctx", None),
            P("fsdp", "ctx", None),
            P(),
            P(),
            P(None, ("fsdp", "ctx"), "tp"),
            P(None, "tp"),
            P(),
            P(),
            P(("fsdp", "ctx"), "tp"),
            P(),
            P(),
            P(),
            P(("fsdp", "ctx"), "tp"),
            P("tp"),
            P(("fsdp", "ctx"), "tp"),
            P(),
        ),
        check_vma=False,
    )
```

```python
from functools import partial

import jax
import jax.numpy as jnp
import ml_dtypes
import numpy as np
from jax import lax
from jax.experimental import pallas as pl
from jax.experimental.pallas import tpu as pltpu
from jax.sharding import PartitionSpec as P

G = 48
HD = 64


eps = 1e-06
highest = lax.Precision.HIGHEST
bf16, f32 = jnp.bfloat16, jnp.float32
VMEM_BYTES = 56 * 1024 * 1024
NN = (((1,), (0,)), ((), ()))
NT = (((1,), (1,)), ((), ()))
TN = (((0,), (0,)), ((), ()))
LH, LW = 64, 112
ANY = pl.BlockSpec(memory_space=pl.ANY)
PEAK = 1.0e15


def mm(a, b, dims=NN):
    return lax.dot_general(a, b, dims, preferred_element_type=f32)


def roll(x, shift, stride=None):
    extra = {} if stride is None else dict(stride=stride, stride_axis=0)
    return pltpu.roll(x, shift, 1, **extra)


def lane_iota(shape):
    return lax.broadcasted_iota(jnp.int32, shape, 1)


def struct(shape, dtype=bf16):
    return jax.ShapeDtypeStruct(shape, dtype)


def whole(shape):
    return pl.BlockSpec(shape, lambda *_: (0,) * len(shape))


def call(kernel, name, us, grid, prefetch, ins, in_specs, outs, out_specs, scratch=(), aliases=None):
    return pl.pallas_call(
        kernel,
        out_shape=outs,
        grid_spec=pltpu.PrefetchScalarGridSpec(
            num_scalar_prefetch=1, grid=grid, in_specs=in_specs, out_specs=out_specs, scratch_shapes=list(scratch)
        ),
        input_output_aliases=aliases or {},
        compiler_params=pltpu.CompilerParams(vmem_limit_bytes=VMEM_BYTES),
        cost_estimate=pl.CostEstimate(flops=int(us * 1e-6 * PEAK), bytes_accessed=0, transcendentals=0),
        name=name,
    )(prefetch, *ins)


def columns(w_ref, side):
    width = w_ref.shape[2] // 2
    parts = [jnp.where(side == 0, w_ref[j, :, :width], w_ref[j, :, width:]) for j in range(3)]
    return jnp.concatenate([p[:, :128] for p in parts] + [p[:, 128:] for p in parts], axis=1)


def pack_kernel(at_ref, image_ref, w_ref, out_ref):
    rows = image_ref.shape[1]
    depth = w_ref.shape[1]
    out_ref[:rows] = image_ref[0]
    out_ref[rows:] = jnp.zeros((depth, out_ref.shape[1]), bf16)
    out_ref[rows:, :576] = columns(w_ref, 1 - at_ref[0])


def pack(at, images, w):
    batch, quarter, d = images.shape
    rows = quarter // 2
    out = (rows + w.shape[1], d)
    return call(
        pack_kernel, "pack", 2, (1,), at, [images, w],
        [pl.BlockSpec((1, rows, d), lambda i, o: (o[1], 1 - o[0], 0)), whole(w.shape)], struct(out), whole(out),
    )


def route_kernel(at_ref, image_ref, got_ref, w_ref, ub_ref, qvb_ref, gain_ref, bias_ref, near_ref, normed_ref, far_ref, w_out_ref):
    rows = image_ref.shape[1]
    depth = w_ref.shape[1]
    same = at_ref[0] == at_ref[2]
    own, got = image_ref[0], got_ref[:rows]
    near = jnp.where(same, own, got)
    near_ref[...] = near
    far_ref[...] = jnp.where(same, got, own)
    normed_ref[...] = norm(near.astype(f32), gain_ref[...], bias_ref[...])[0].astype(bf16)
    w_out_ref[...] = jnp.zeros(w_out_ref.shape, bf16)
    w_out_ref[:depth, :576] = columns(w_ref, at_ref[0])
    w_out_ref[depth:2 * depth] = got_ref[rows:]
    d = image_ref.shape[2]
    w_out_ref[2 * depth:2 * depth + 1] = ub_ref[:, :d]
    w_out_ref[2 * depth + 1:2 * depth + 2] = ub_ref[:, d:]
    w_out_ref[2 * depth + 2:2 * depth + 3] = qvb_ref[...]


def route(at, images, got, w, up_bias, qv_bias, gain, bias):
    batch, quarter, d = images.shape
    rows = quarter // 2
    half = (rows, d)
    out = (2 * w.shape[1] + 16, d)
    return call(
        route_kernel, "route", 3, (1,), at, [images, got, w, up_bias, qv_bias, gain, bias],
        [pl.BlockSpec((1, rows, d), lambda i, o: (o[1], o[0], 0))] + [whole(v.shape) for v in (got, w, up_bias, qv_bias, gain, bias)],
        (struct(half), struct(half), struct(half), struct(out)), [whole(half)] * 3 + [whole(out)],
    )


def norm_kernel(_, x_ref, gain_ref, bias_ref, out_ref):
    out_ref[...] = norm(x_ref[...].astype(f32), gain_ref[...], bias_ref[...])[0].astype(bf16)


def norm_low(at, x, gain, bias):
    return call(
        norm_kernel, "norm_low", 1, (1,), at, [x, gain, bias], [whole(v.shape) for v in (x, gain, bias)], struct(x.shape), whole(x.shape)
    )


def arrange_kernel(me_ref, *refs):
    pieces, out_ref = refs[:-1], refs[-1]
    depth = pieces[0].shape[0] // 2
    out_ref[:, 576:] = jnp.zeros((out_ref.shape[0], 64), bf16)
    for dx in range(2):
        for dz in range(4):
            for dc in range(2):
                ref, lo = (pieces[dz], dc) if dx == 0 else (pieces[4], dz * 2 + dc)
                at = (dx * 8 + dc * 4 + dz) ^ me_ref[0]
                out_ref[pl.ds(pl.multiple_of(at * depth, 16), depth), :576] = ref[lo * depth:(lo + 1) * depth]


def arrange(me, pieces, rows):
    return call(
        arrange_kernel, "arrange", 2, (1,), me, pieces, [whole(p.shape) for p in pieces],
        struct((rows, 640)), whole((rows, 640)),
    )


def prep_kernel(order_ref, *refs):
    xs, refs = refs[:4], refs[4:]
    w_ref, b_ref, tab_ref, hot_ref = refs[:4]
    q_ref, k_ref, v_ref, n_ref = refs[-4:]
    step = pl.program_id(0)
    rows = q_ref.shape[1]

    def work(x):
        first_row = order_ref[4 + step]
        n_ref[...] = x
        qkv = (mm(x, w_ref[...]) + b_ref[...]).astype(bf16).astype(f32)
        lane = lane_iota((G, 128))
        lane_all = lane_iota((rows, 128))
        hot_a = hot_ref[0, :, :128].astype(f32)
        hot_b = hot_ref[0, :, 128:]
        cols = [qkv[:, i * 128:(i + 1) * 128] for i in range(5)]
        back = [roll(v, 64) for v in cols[:4]]
        for h, (q, k, v) in enumerate(
            ((cols[0], cols[1], cols[2]), (back[0], back[1], back[2]), (cols[3], back[3], cols[4]))
        ):
            k_ref[h, :, :128] = jnp.where(lane_all < 64, k, hot_a).astype(bf16)
            k_ref[h, :, 128:] = hot_b
            v_ref[h] = jnp.where(lane_all < 64, v, jnp.where(lane_all < 67, 1.0, 0.0)).astype(bf16)
            turned = mm(q.astype(bf16), tab_ref[...])
            qf = q * (HD ** -0.5)
            for g in range(rows // G):
                r = first_row + g
                along_h = turned[g * G:(g + 1) * G, :128]
                along_w = turned[g * G:(g + 1) * G, 128:]
                h_a = roll(along_h, (LH - (G - 1) + 128 + r) % 128)
                h_b = roll(along_h, (32 - (G - 1) + 128 + r) % 128)
                w_a = roll(along_w, (LW - (G - 1)) % 128, 1)
                w_b = roll(along_w, (80 - (G - 1)) % 128, 1)
                h_lo = h_b - h_b.astype(bf16).astype(f32)
                w_lo = w_b - w_b.astype(bf16).astype(f32)
                first = jnp.where(lane < LH, qf[g * G:(g + 1) * G], jnp.where(lane < LW, h_a, w_a))
                second = jnp.where(lane < 32, w_a, jnp.where(lane < 80, h_lo, w_lo))
                q_ref[h, g * G:(g + 1) * G, :128] = first.astype(bf16)
                q_ref[h, g * G:(g + 1) * G, 128:] = second.astype(bf16)

    for k in range(4):
        @pl.when(step == k)
        def _(k=k):
            work(xs[k][...])


def prep(order, xs, w, b, tab, hot, heads, before, group):
    rows, d = xs[0].shape
    tokens = len(xs) * 2 * rows
    outs = (struct((heads, tokens, 256)), struct((heads, tokens, 256)), struct((heads, tokens, 128)), struct((tokens, d)))
    return call(
        prep_kernel, "prep", 7, (len(xs),), order, list(xs) + [w, b, tab, hot] + list(before),
        [whole(x.shape) for x in xs] + [whole(w.shape), whole(b.shape), whole(tab.shape)]
        + [pl.BlockSpec((1, rows, 256), lambda i, o: (o[i], 0, 0))] + [ANY] * len(before),
        outs,
        [
            pl.BlockSpec((heads, rows, 256), lambda i, o: (0, 2 * i + group, 0)),
            pl.BlockSpec((heads, rows, 256), lambda i, o: (0, 2 * i + group, 0)),
            pl.BlockSpec((heads, rows, 128), lambda i, o: (0, 2 * i + group, 0)),
            pl.BlockSpec((rows, d), lambda i, o: (2 * i + group, 0)),
        ],
        aliases={9 + i: i for i in range(len(before))},
    )


def attend_kernel(order_ref, q_ref, k_ref, v_ref, *refs, tiles):
    att_ref, q2_ref, mix_ref = refs[-3:]
    head = pl.program_id(0)
    start = 0
    for tile in tiles:
        at = pl.ds(start, tile)
        start += tile
        lane = lane_iota((tile, 128))
        q = q_ref[0, at, :]
        s = mm(q, k_ref[0], NT)
        m = jnp.max(s, axis=1, keepdims=True)
        p = jnp.exp(s - m)
        o = mm(p.astype(bf16), v_ref[0])
        total = o[:, 64:65]
        att = o / total
        lse = m + jnp.log(total)
        att_ref[0, at, :] = att
        low_att = att[:, :64].astype(bf16)
        for h in range(3):
            @pl.when(head == h)
            def _(h=h):
                mix_ref[at, h * 64:(h + 1) * 64] = low_att
        a = q[:, :128].astype(f32)
        b = q[:, 128:].astype(f32)
        full = a + roll(b, 32) - lse
        high = full.astype(bf16)
        low = roll(full - high.astype(f32), 96)
        q2_ref[0, at, :128] = jnp.where((lane >= LH) & (lane < LW), high.astype(f32), a).astype(bf16)
        q2_ref[0, at, 128:] = jnp.where((lane >= 32) & (lane < 80), low, b).astype(bf16)


def attend(q, k, v, side):
    heads, tokens, _ = q.shape
    rows = tokens // 2
    tiles = (256,) * (rows // 256) + ((rows % 256,) if rows % 256 else ())
    return call(
        partial(attend_kernel, tiles=tiles), "attend", 19, (heads,), jnp.zeros((1,), jnp.int32), [q, k, v],
        [
            pl.BlockSpec((1, rows, 256), lambda h, o: (h, side, 0)),
            pl.BlockSpec((1, tokens, 256), lambda h, o: (h, 0, 0)),
            pl.BlockSpec((1, tokens, 128), lambda h, o: (h, 0, 0)),
        ],
        (struct((heads, rows, 128), f32), struct((heads, rows, 256)), struct((rows, heads * HD))),
        [pl.BlockSpec((1, rows, 128), lambda h, o: (h, 0, 0)), pl.BlockSpec((1, rows, 256), lambda h, o: (h, 0, 0)), whole((rows, heads * HD))],
    )


def back_kernel(order_ref, qa_ref, qb_ref, k_ref, v_ref, atta_ref, attb_ref, g0, g1, g2, g3, tab_ref, turn_ref,
                d_ref, table_ref, q_ref, go_ref, kt_ref, acc_ref, hi_ref, lo_ref, *, tile, sets, first, count):
    head, step = pl.program_id(0), pl.program_id(1)
    last = pl.num_programs(1) - 1
    tokens = k_ref.shape[1]
    rows = tokens // sets
    wide = count * 64

    @pl.when(step == 0)
    def _():
        lane = lane_iota((rows, 128))
        for n, ref in enumerate((g0, g1, g2, g3)):
            at = pl.ds(n * rows, rows)
            for h in range(count):
                @pl.when(head == h)
                def _(ref=ref, at=at, h=h):
                    lo = (first + h) * 64
                    go_ref[at, :64] = ref[:, lo:lo + 64]
        go = go_ref[...].astype(f32)
        lane = lane_iota(go.shape)
        go = jnp.where(lane < 64, go, 0.0)
        att = jnp.concatenate([atta_ref[0], attb_ref[0]], axis=0)
        q_ref[:tokens // 2] = qa_ref[0]
        q_ref[tokens // 2:] = qb_ref[0]
        dot = jnp.sum(jnp.where(lane < 64, go * att, 0.0), axis=1, keepdims=True)
        high = dot.astype(bf16).astype(f32)
        mid = (dot - high).astype(bf16).astype(f32)
        low = dot - high - mid
        go_ref[...] = jnp.where(lane < 64, go, jnp.where(lane == 64, -high, jnp.where(lane == 65, -mid, jnp.where(lane == 66, -low, 0.0)))).astype(bf16)
        acc_ref[...] = jnp.zeros_like(acc_ref)
        kt_ref[:LW] = k_ref[0, :, :128].T[:LW]
        kt_ref[LW:] = turn_ref[...]

    keys = tokens // pl.num_programs(1)
    for i in range(keys // tile):
        at = pl.ds(pl.multiple_of(step * keys + i * tile, tile), tile)
        s = mm(k_ref[0, at, :], q_ref[...], NT)
        p = jnp.exp(s)
        pb = p.astype(bf16)
        d = (p * mm(v_ref[0, at, :], go_ref[...], NT)).astype(bf16)
        dv = mm(pb, go_ref[...]).astype(bf16)
        dk = mm(d, q_ref[:, :128]).astype(bf16)
        for h in range(count):
            @pl.when(head == h)
            def _(h=h):
                d_ref[at, 2 * wide + h * 64:2 * wide + (h + 1) * 64] = dv[:, :64]
                d_ref[at, wide + h * 64:wide + (h + 1) * 64] = dk[:, :64]
        acc_ref[...] += mm(kt_ref[:, at], d)

    @pl.when(step == last)
    def _():
        small = lane_iota((G, 128))
        a = acc_ref[:128].T
        b = jnp.concatenate([acc_ref[128:160], jnp.zeros((96, tokens), f32)], axis=0).T
        for g in range(tokens // G):
            block, inner = divmod(g, rows // 2 // G)
            r = order_ref[block] + inner
            ag = a[g * G:(g + 1) * G]
            bg = b[g * G:(g + 1) * G]
            along_h = jnp.where((small >= LH) & (small < LW), ag, 0.0)
            along_w = jnp.where(small >= LW, ag, jnp.where(small < 32, bg, 0.0))
            along_h = roll(along_h, (256 + G - 1 - LH - r) % 128)
            along_w = roll(along_w, (128 - LW) % 128, 1)
            h_hi = along_h.astype(bf16)
            w_hi = along_w.astype(bf16)
            hi_ref[g * G:(g + 1) * G, :128] = h_hi
            hi_ref[g * G:(g + 1) * G, 128:] = w_hi
            lo_ref[g * G:(g + 1) * G, :128] = (along_h - h_hi.astype(f32)).astype(bf16)
            lo_ref[g * G:(g + 1) * G, 128:] = (along_w - w_hi.astype(f32)).astype(bf16)
        turned = mm(hi_ref[...], tab_ref[...], NT) + mm(lo_ref[...], tab_ref[...], NT)
        dq = (a * (HD ** -0.5) + turned).astype(bf16)
        for h in range(count):
            @pl.when(head == h)
            def _(h=h):
                d_ref[:, h * 64:(h + 1) * 64] = dq[:, :64]
        tables = mm(hi_ref[...], q_ref[:, :128], TN)

        @pl.when(head == 0)
        def _():
            table_ref[...] = tables

        @pl.when(head > 0)
        def _():
            table_ref[...] += tables


def attend_back(order, q2, k, v, att, grads, tab, turn, first, count, steps, tile, sets):
    _, tokens, _ = k.shape
    at = lambda h, i, o: (first + h, 0, 0)
    wide = 3 * count * HD
    per_head = lambda a: pl.BlockSpec((1,) + a.shape[1:], at)
    return call(
        partial(back_kernel, tile=tile, sets=sets, first=first, count=count), "attend_back", 21 * count,
        (count, steps), order, list(q2) + [k, v] + list(att) + list(grads) + [tab, turn],
        [per_head(a) for a in list(q2) + [k, v] + list(att)] + [whole(g.shape) for g in grads] + [whole(tab.shape), whole(turn.shape)],
        (struct((tokens, wide)), struct((256, 128), f32)),
        [whole((tokens, wide)), whole((256, 128))],
        [
            pltpu.VMEM((tokens, 256), bf16),
            pltpu.VMEM((tokens, 128), bf16),
            pltpu.VMEM((160, tokens), bf16),
            pltpu.VMEM((160, tokens), f32),
            pltpu.VMEM((tokens, 256), bf16),
            pltpu.VMEM((tokens, 256), bf16),
        ],
    )


def norm(v, gain, bias):
    mean = jnp.mean(v, axis=1, keepdims=True)
    centered = v - mean
    inverse = lax.rsqrt(jnp.mean(centered * centered, axis=1, keepdims=True) + eps)
    unit = centered * inverse
    return unit * gain + bias, unit, inverse


def norm_back(upstream, unit, inverse, gain):
    scaled = upstream * gain
    return inverse * (scaled - jnp.mean(scaled, axis=1, keepdims=True) - unit * jnp.mean(scaled * unit, axis=1, keepdims=True))


def mlp_kernel(order_ref, m0, m1, m2, m3, src0, src1, top0, top1, up_ref, down_ref, proj_ref, ub_ref, vec_ref,
               out0, out1, act_ref, hg_ref, n2_ref, mg_ref, br_ref, mix_ref, d0, d1, d2, d3, ubg_ref, vg_ref,
               mid_ref, unit_ref, inv_ref, acc_ref, ng_ref, quad_ref, top_ref):
    step = pl.program_id(0)
    last = pl.num_programs(0) - 1
    part, d = src0.shape
    half = proj_ref.shape[3]
    width = m0.shape[1]

    def proj(i):
        return proj_ref[:, i].reshape(d, half)

    @pl.when(step == 0)
    def _():
        for k, ref in enumerate((m0, m1, m2, m3)):
            quad_ref[order_ref[k]] = ref[...]
        for i in range(4):
            mix_ref[:, i * width:(i + 1) * width] = quad_ref[i]
        top_ref[:part] = top0[...]
        top_ref[part:] = top1[...]
        mid = jnp.concatenate([src0[...], src1[...]], axis=0).astype(f32) + vec_ref[0:1] + mm(mix_ref[:, :half], proj(0), NT) + mm(mix_ref[:, half:], proj(1), NT)
        normed, unit, inverse = norm(mid, vec_ref[1:2], vec_ref[2:3])
        mid_ref[...] = mid
        unit_ref[...] = unit
        inv_ref[...] = inverse
        n2_ref[...] = normed.astype(bf16)

    tile = up_ref.shape[3]
    up = up_ref[:, 0].reshape(d, tile)
    down = down_ref[:, 0].reshape(d, tile)
    hidden = mm(n2_ref[...], up) + ub_ref[...]
    phi_all = 0.5 + 0.5 * lax.erf(hidden * (0.5 ** 0.5))
    slope = phi_all + hidden * (jnp.exp(-0.5 * hidden * hidden) * 0.3989422804014327)
    active = (hidden * phi_all).astype(bf16)
    hg = (mm(top_ref[...], down) * slope).astype(bf16)
    act_ref[...] = active
    hg_ref[...] = hg
    ubg_ref[...] = jnp.sum(hg.astype(f32), axis=0, keepdims=True)
    out = mm(active, down, NT)
    ng = mm(hg, up, NT)

    @pl.when(step == 0)
    def _():
        acc_ref[...] = out
        ng_ref[...] = ng

    @pl.when(step > 0)
    def _():
        acc_ref[...] += out
        ng_ref[...] += ng

    @pl.when(step == last)
    def _():
        top = top_ref[...].astype(f32)
        grad = ng_ref[...]
        unit = unit_ref[...]
        out = (mid_ref[...] + acc_ref[...] + vec_ref[3:4]).astype(bf16)
        out0[...] = out[:part]
        out1[...] = out[part:]
        middle = top + norm_back(grad, unit, inv_ref[...], vec_ref[1:2])
        branch = middle.astype(bf16)
        mg_ref[...] = middle
        br_ref[...] = branch
        for i in range(2):
            piece = mm(branch, proj(i)).astype(bf16)
            quad_ref[2 * i] = piece[:, :width]
            quad_ref[2 * i + 1] = piece[:, width:]
        for k, ref in enumerate((d0, d1, d2, d3)):
            ref[...] = quad_ref[order_ref[k]]
        vg_ref[0:1] = jnp.sum(branch.astype(f32), axis=0, keepdims=True)
        vg_ref[1:2] = jnp.sum(grad * unit, axis=0, keepdims=True)
        vg_ref[2:3] = jnp.sum(grad, axis=0, keepdims=True)
        vg_ref[3:4] = jnp.sum(top, axis=0, keepdims=True)


def mlp(order, mixed, src, top, packed, up_bias, vecs, half_ff, tile):
    part, d = src[0].shape
    rows = 2 * part
    blocks, halves, depth, _ = packed.shape
    per = half_ff // tile
    half = d // halves
    ff = halves * half_ff
    by_tile = pl.BlockSpec((rows, tile), lambda i, o: (0, i))
    row_tile = pl.BlockSpec((1, tile), lambda i, o: (0, i))
    full = whole((rows, d))
    piece = whole((part, d))
    return call(
        mlp_kernel, "mlp", 24, (halves * per,), order,
        list(mixed) + list(src) + list(top) + [packed, packed, packed, up_bias, vecs],
        [whole(m.shape) for m in mixed] + [
            piece, piece, piece, piece,
            pl.BlockSpec((blocks, 1, depth, tile), lambda i, o: (0, i // per, 0, i % per)),
            pl.BlockSpec((blocks, 1, depth, tile), lambda i, o: (0, i // per, 0, per + i % per)),
            pl.BlockSpec((blocks, halves, depth, half), lambda i, o: (0, 0, 0, 2 * half_ff // half)),
            row_tile, whole(vecs.shape),
        ],
        (struct((part, d)), struct((part, d)), struct((rows, ff)), struct((rows, ff)), struct((rows, d)), struct((rows, d), f32), struct((rows, d)), struct((rows, d)))
        + (struct(mixed[0].shape),) * 4 + (struct((1, ff), f32), struct((4, d), f32)),
        [piece, piece, by_tile, by_tile, full, full, full, full] + [whole(mixed[0].shape)] * 4 + [row_tile, whole((4, d))],
        [
            pltpu.VMEM((rows, d), f32),
            pltpu.VMEM((rows, d), f32),
            pltpu.VMEM((rows, 1), f32),
            pltpu.VMEM((rows, d), f32),
            pltpu.VMEM((rows, d), f32),
            pltpu.VMEM((4,) + mixed[0].shape, bf16),
            pltpu.VMEM((rows, d), bf16),
        ],
    )


def wgrad_kernel(_, n2_ref, top0, top1, br_ref, hg_ref, act_ref, mix_ref, out_ref, left_ref, *, per):
    half, block = pl.program_id(0), pl.program_id(1)
    blocks, depth = out_ref.shape[0], out_ref.shape[2]

    @pl.when((half == 0) & (block == 0))
    def _():
        left_ref[0] = n2_ref[...].T
        left_ref[1] = jnp.concatenate([top0[...], top1[...]], axis=0).T
        left_ref[2] = br_ref[...].T

    def put(i, right):
        out_ref[:, 0] = mm(left_ref[i], right[...]).astype(bf16).reshape(blocks, depth, -1)

    @pl.when(block < per)
    def _():
        put(0, hg_ref)

    @pl.when((block >= per) & (block < 2 * per))
    def _():
        put(1, act_ref)

    @pl.when(block == 2 * per)
    def _():
        put(2, mix_ref)


def wgrad(n2, top, branch, hg, active, mixed, blocks, halves):
    rows, d = n2.shape
    ff = hg.shape[1]
    tile = d // halves
    per = ff // halves // tile
    depth = d // blocks
    return call(
        partial(wgrad_kernel, per=per), "wgrad", 20, (halves, 2 * per + 1), jnp.zeros((1,), jnp.int32),
        [n2, top[0], top[1], branch, hg, active, mixed],
        [whole((rows, d)), whole(top[0].shape), whole(top[1].shape), whole((rows, d))] + [
            pl.BlockSpec((rows, tile), lambda s, j, o: (0, s * per + jnp.minimum(j, per - 1))),
            pl.BlockSpec((rows, tile), lambda s, j, o: (0, s * per + jnp.clip(j - per, 0, per - 1))),
            pl.BlockSpec((rows, tile), lambda s, j, o: (0, s)),
        ],
        struct((blocks, halves, depth, (2 * per + 1) * tile)),
        pl.BlockSpec((blocks, 1, depth, tile), lambda s, j, o: (0, s, 0, j)),
        [pltpu.VMEM((3, d, rows), bf16)],
    )


def down_kernel(_, a_ref, b_ref, w_ref, ng_ref):
    both = jnp.concatenate([a_ref[...], b_ref[...]], axis=1)
    ng_ref[0] = mm(both, w_ref[:, :both.shape[1]], NT).astype(bf16)


def grad_down(sets, grads, w, rows):
    d = w.shape[0]
    return call(
        down_kernel, "grad_down", 4, (2,), jnp.zeros((1,), jnp.int32), list(grads) + [w],
        [pl.BlockSpec((rows, g.shape[1]), lambda i, o: (2 * i + sets, 0)) for g in grads] + [whole(w.shape)],
        struct((2, rows, d)), pl.BlockSpec((1, rows, d), lambda i, o: (i, 0, 0)),
    )


def qkv_grad_kernel(_, x_ref, a_ref, b_ref, w_ref, wg_ref, bg_ref, ng_ref, acc_ref):
    step = pl.program_id(0)
    width = wg_ref.shape[-1]
    both = jnp.concatenate([a_ref[...], b_ref[...]], axis=1)
    add = mm(x_ref[...].T, both)
    sums = jnp.sum(both.astype(f32), axis=0, keepdims=True)

    @pl.when(step == 0)
    def _():
        acc_ref[...] = add
        bg_ref[...] = sums

    @pl.when(step > 0)
    def _():
        acc_ref[...] += add
        bg_ref[...] += sums

    @pl.when(step == pl.num_programs(0) - 1)
    def _():
        full = acc_ref[...]
        wg_ref[...] = full.astype(bf16).reshape(wg_ref.shape)
        w = w_ref[:, :width].astype(f32)
        lane = lane_iota(ng_ref.shape)
        a = jnp.sum(full * w, axis=1, keepdims=True)
        b = jnp.sum(bg_ref[...] * w, axis=1, keepdims=True)
        ng_ref[...] = jnp.where(lane == 0, a, jnp.where(lane == 1, b, 0.0))


def qkv_grad(x, grads, w, steps, blocks):
    tokens, d = x.shape
    rows = tokens // steps
    width = sum(g.shape[1] for g in grads)
    by_rows = lambda n: pl.BlockSpec((rows, n), lambda i, o: (i, 0))
    return call(
        qkv_grad_kernel, "qkv_grad", 5, (steps,), jnp.zeros((1,), jnp.int32), [x] + list(grads) + [w],
        [by_rows(d)] + [by_rows(g.shape[1]) for g in grads] + [whole(w.shape)],
        (struct((blocks, d // blocks, width)), struct((1, width), f32), struct((d, 128), f32)),
        [whole((blocks, d // blocks, width)), whole((1, width)), whole((d, 128))],
        [pltpu.VMEM((d, width), f32)],
    )


def finish_kernel(_, kept_ref, got_ref, passed_ref, middle_ref, src_ref, gain_ref, out_ref):
    grad = kept_ref[0].astype(f32) + got_ref[0].astype(f32) + passed_ref[...].astype(f32)
    _, unit, inverse = norm(src_ref[...].astype(f32), 1.0, 0.0)
    out_ref[...] = (middle_ref[...] + norm_back(grad, unit, inverse, gain_ref[...])).astype(bf16)


def finish(at, kept, got, passed, middle, src, gain, group):
    part, d = src.shape
    first = pl.BlockSpec((1, part, d), lambda i, o: (0, group, 0))
    return call(
        finish_kernel, "finish", 2, (1,), at, [kept, got, passed, middle, src, gain],
        [first, first, whole((part, d)), pl.BlockSpec((part, d), lambda i, o: (group, 0)), whole((part, d)), whole(gain.shape)],
        struct((part, d)), whole((part, d)),
    )


AXES = ("fsdp", "ctx", "tp")


def pairs_of(shape, move):
    nf, nc, nt = shape["fsdp"], shape["ctx"], shape["tp"]
    flat = lambda f, z, t: (f * nc + z) * nt + t
    return [(flat(f, z, t), flat(*move(f, z, t))) for f in range(nf) for z in range(nc) for t in range(nt)]


def grouped(
    shape,
    images,
    norm1_gain,
    norm1_bias,
    qkv_weight,
    qv_bias,
    rel_pos_h,
    rel_pos_w,
    proj_weight,
    proj_bias,
    norm2_gain,
    norm2_bias,
    up_weight,
    up_bias,
    down_weight,
    down_bias,
    out_cotangent,
):
    nf, nc, nt = shape["fsdp"], shape["ctx"], shape["tp"]
    batch, quarter, d = images.shape
    sets = 4
    part = quarter // 2
    rows = 2 * part
    tokens = sets * rows
    half = qkv_weight.shape[2]
    width = half // 2
    heads = width // HD
    depth = qkv_weight.shape[1]
    blocks = nf * nc
    half_ff = up_weight.shape[1]
    fi, z, t = lax.axis_index("fsdp"), lax.axis_index("ctx"), lax.axis_index("tp")
    x, c = fi // 2, fi % 2
    zi, zp = z // 2, z % 2
    me = 2 * zp + c

    def send(v, move):
        return lax.ppermute(v, AXES, pairs_of(shape, move))

    core = lambda v: send(v, lambda f, w, u: (f ^ 1, w, u))
    tpswap = lambda v: send(v, lambda f, w, u: (f, w, u ^ 1))
    xswap = lambda v: send(v, lambda f, w, u: (f ^ 2, w, u))
    zswap = lambda v, k: send(v, lambda f, w, u: (f, w ^ k, u))
    beside = lambda v: zswap(v, 1)
    diagonal = lambda v: send(v, lambda f, w, u: (f ^ 1, w ^ 1, u))

    def pick(v, i, axis=0):
        return lax.dynamic_index_in_dim(v, i, axis, keepdims=False)

    def ordered(bit, mine, other, axis=0):
        return jnp.where(bit == 0, jnp.concatenate([mine, other], axis), jnp.concatenate([other, mine], axis))

    f = lambda v: v.astype(f32)
    ints = lambda *v: jnp.stack([jnp.asarray(i, jnp.int32) for i in v])
    place = ints(c, t, zi, zp)
    gain1, bias1 = f(norm1_gain)[None], f(norm1_bias)[None]

    got = core(pack(place, images, qkv_weight))
    near, normed_near, far, w_own = route(place, images, got, qkv_weight, up_bias[None], qv_bias.reshape(1, d), gain1, bias1)
    w_other = tpswap(w_own)
    far = zswap(far, 2)
    mine, yours = w_own[: 2 * depth, :576], w_other[: 2 * depth, :576]
    keep = jnp.where(t == zp, mine, yours)
    give = jnp.where(t == zp, yours, mine)
    w_z = [keep, zswap(give, 1), zswap(keep, 2), zswap(give, 3)]
    w = arrange(ints(fi * nc + z), w_z + [xswap(jnp.concatenate(w_z, axis=0))], d)
    near_sets = [normed_near, core(normed_near), beside(normed_near)]
    near_sets.append(core(near_sets[2]))
    normed_far = norm_low(place, far, gain1, bias1)
    far_sets = [normed_far, core(normed_far), beside(normed_far)]
    far_sets.append(core(far_sets[2]))

    bias = jnp.where(t == zp, qv_bias, w_other[2 * depth + 2].reshape(2, half))
    bias = pick(bias.reshape(2, 2, width), c, 1)
    bias = jnp.stack([bias[0], jnp.zeros_like(bias[0]), bias[1]])
    bias = f(jnp.concatenate([bias[:, :128].reshape(-1), bias[:, 128:].reshape(-1), jnp.zeros((64,), bf16)]))[None]
    flip = lambda v: jnp.pad(v[::-1].T, ((0, HD), (0, 128 - (2 * G - 1))))
    plain = lambda v: jnp.pad(v.T, ((0, HD), (0, 128 - (2 * G - 1))))
    tab = jnp.concatenate([flip(rel_pos_h), flip(rel_pos_w)], axis=1)
    tab_back = jnp.concatenate([flip(rel_pos_h), plain(rel_pos_w)], axis=1)
    block_rows = part // G
    first_of = lambda m, s_: (2 * m + s_ // 2) * (quarter // G) + (s_ % 2) * block_rows
    spot = np.concatenate([first_of(m, s_) * G + np.arange(part) for m in range(2) for s_ in range(sets)])
    at = np.arange(tokens)
    hot = np.zeros((tokens, 256), np.float32)
    for base, index in ((LH, spot // G), (LW, spot % G), (160, spot // G), (208, spot % G)):
        hot[at, base + index] = 1
    turn = np.zeros((G, tokens), np.float32)
    turn[G - 1 - at % G, at] = 1
    hot = jnp.asarray(hot.astype(ml_dtypes.bfloat16).reshape(2 * sets, part, 256))
    turn = jnp.asarray(turn.astype(ml_dtypes.bfloat16))

    order = [me ^ k for k in range(sets)]
    qkv = ()
    for g, group in enumerate((near_sets, far_sets)):
        m = zi ^ g
        spots = ints(*[m * sets + s for s in order], *[first_of(m, s) for s in order])
        qkv = prep(spots, group, w, bias, tab, hot, heads, qkv, g)
    q, k, v, normed = qkv

    packed = lax.all_gather(
        jnp.concatenate([up_weight, down_weight, proj_weight], axis=1), AXES, axis=0, tiled=False
    ).reshape(blocks, nt, depth, 2 * half_ff + half)

    att_far, q_far, mix_far = attend(q, k, v, 1)
    mix2, mix3 = beside(mix_far[:rows]), diagonal(mix_far[rows:])
    att_near, q_near, mix_near = attend(q, k, v, 0)
    mix0, mix1 = mix_near[:rows], core(mix_near[rows:])
    att, q2 = (att_near, att_far), (q_near, q_far)

    out_cotangent, _ = lax.optimization_barrier((out_cotangent, k))
    top_own = lax.dynamic_index_in_dim(out_cotangent, t, 0, False).reshape(2, part, d)
    top_got = core(pick(top_own, 1 - c))
    top_own = pick(top_own, c)
    top = [jnp.where(c == zi, top_own, top_got), zswap(jnp.where(c == zi, top_got, top_own), 2)]
    other_up = w_other[2 * depth : 2 * depth + 2].reshape(-1)[:half_ff]
    full_bias = f(ordered(t, up_bias, other_up))[None]
    vecs = jnp.stack([f(proj_bias), f(norm2_gain), f(norm2_bias), f(down_bias)])
    (out0, out1, active, hidden_grad, normed2, middle_grad, branch, mixed, back0, back1, back2, back3, up_bias_grad, vec_grads) = mlp(
        ints(*order), [mix0, mix1, mix2, mix3], [near, far], top, packed, full_bias, vecs, half_ff, 768
    )
    back = [back0, core(back1), beside(back2), diagonal(back3)]
    big = wgrad(normed2, top, branch, hidden_grad, active, mixed, blocks, nt)
    big = lax.psum_scatter(big.reshape(blocks * nt, depth, -1), AXES, scatter_dimension=0, tiled=True)
    big = f(big.reshape(depth, -1))

    def give_back(own, own_other, home, home_other):
        a = jnp.stack([own, own_other])
        b = jnp.stack([home, home_other])
        keep_, pass_ = jnp.where(c == zi, a, b), jnp.where(c == zi, b, a)
        both = ordered(c, keep_, core(pass_), 1)
        return jnp.where(t == 0, both, both[::-1])

    out_home, out_own = zswap(out1, 2), tpswap(out0)
    back, out_home, out_own = lax.optimization_barrier((back, out_home, out_own))

    spots = ints(*[first_of(zi ^ g, s) for s in order for g in range(2)])
    a_back, a_tables = attend_back(spots, q2, k, v, att, back, tab_back, turn, 0, 2, 3, 256, sets)
    home_other = tpswap(out_home)
    q2, home_other, a_back = lax.optimization_barrier((q2, home_other, a_back))
    result = give_back(out0, out_own, out_home, home_other)
    b_back, b_tables = attend_back(spots, q2, k, v, att, back, tab_back, turn, 2, 1, 3, 256, sets)
    tables = (a_tables + b_tables)[:, :HD] * HD ** 0.5
    grads = [a_back, b_back]
    result, b_back = lax.optimization_barrier((result, b_back))
    grads = [a_back, b_back]
    got = core(grad_down(1, grads, w, rows))
    kept = grad_down(0, grads, w, rows)

    passed = (f(kept[1]) + f(got[1])).astype(bf16)
    passed1 = beside(passed[part:])
    grad1 = finish(place, kept, got, passed1, middle_grad, far, gain1, 1)
    passed0 = beside(passed[:part])
    grad0 = finish(place, kept, got, passed0, middle_grad, near, gain1, 0)
    home = zswap(grad1, 2)
    input_grad = give_back(grad0, tpswap(grad0), home, tpswap(home))

    wg, sums, ng = qkv_grad(normed, grads, w, 3, blocks)
    wg = wg.reshape(2, 2, 2, 2, depth, 3 * width)
    wg = f(pick(wg, x)) + f(xswap(pick(wg, 1 - x)))
    wg_low = wg.astype(bf16)
    wg = pick(wg, zi, 1) + f(zswap(pick(wg_low, 1 - zi, 1), 2))
    wg_low = wg.astype(bf16)
    wg = pick(wg, t, 1) + f(tpswap(pick(wg_low, 1 - t, 1)))
    wg = wg.astype(bf16)
    wg = send(wg, lambda f_, w_, u: (f_, (w_ // 2) * 2 + u, w_ % 2))
    wg = f(ordered(c, pick(wg, c)[None], core(pick(wg, 1 - c))[None]))
    wg = jnp.concatenate([wg[..., :384].reshape(2, depth, 3, 128), wg[..., 384:].reshape(2, depth, 3, 64)], axis=-1)
    wg = wg.transpose(2, 1, 0, 3).reshape(3, depth, half)

    def total(v):
        for move in (core, beside, tpswap, xswap):
            v = v + move(v)
        return v + zswap(v, 2)

    def cut(v, sizes):
        at, out = 0, []
        v = v.reshape(-1)
        for size in sizes:
            out.append(lax.slice(v, (at,), (at + size,)))
            at += size
        return out

    sums = sums[0]
    qv = jnp.stack([jnp.concatenate([sums[i:i + 128], sums[j:j + 64]]) for i, j in ((0, 384), (256, 512))])
    qv = jnp.where(jnp.arange(sets)[:, None, None] == me, qv[None], 0.0).transpose(1, 0, 2).reshape(-1)
    small = total(
        jnp.concatenate(
            [vec_grads.reshape(-1), up_bias_grad.reshape(-1), ng[:, 0], ng[:, 1], qv, tables.reshape(-1)]
        ).reshape(-1, 128)
    )
    pb, g2, b2, db, ub, g1, b1, qv, tg = cut(small, (d, d, d, d, nt * half_ff, d, d, 2 * d, 256 * HD))
    g1 = (g1 - b1 * f(norm1_bias)) / f(norm1_gain)
    tg = tg.reshape(256, HD)
    return (
        result.reshape(batch, quarter, d),
        input_grad.reshape(batch, quarter, d),
        g1,
        b1,
        wg,
        pick(qv.reshape(2, nt, half), t, 1),
        tg[: 2 * G - 1][::-1],
        tg[128 : 128 + 2 * G - 1],
        big[:, 2 * half_ff :],
        pb,
        g2,
        b2,
        big[:, :half_ff],
        pick(ub.reshape(nt, half_ff), t),
        big[:, half_ff : 2 * half_ff],
        db,
    )


def layer_norm(values, gain_vec, shift_vec):
    centered = values - jnp.mean(values, axis=-1, keepdims=True)
    inverse = lax.rsqrt(jnp.mean(centered * centered, axis=-1, keepdims=True) + eps)
    standard = centered * inverse
    return (standard * gain_vec + shift_vec, standard, inverse)


def norm_back_plain(upstream, standard, inverse, gain_vec):
    scaled = upstream * gain_vec
    mean_term = jnp.mean(scaled, axis=-1, keepdims=True)
    proj_term = jnp.mean(scaled * standard, axis=-1, keepdims=True)
    return inverse * (scaled - mean_term - standard * proj_term)


def exact_gelu(values):
    return jax.nn.gelu(values, approximate=False)


def table_rows(pos_table, first_row, num_rows):
    table_len = pos_table.shape[0]
    grid_side = (table_len + 1) // 2
    query_row = first_row + lax.broadcasted_iota(jnp.int32, (num_rows, grid_side, table_len), 0)
    key_row = lax.broadcasted_iota(jnp.int32, (num_rows, grid_side, table_len), 1)
    entry_idx = lax.broadcasted_iota(jnp.int32, (num_rows, grid_side, table_len), 2)
    chooser = (query_row - key_row + grid_side - 1 == entry_idx).astype(jnp.float32)
    chooser = chooser.reshape(num_rows * grid_side, table_len)
    picked = jnp.dot(chooser, pos_table, precision=highest)
    return (picked.reshape(num_rows, grid_side, -1), chooser)


def rel_terms(query_f, row_first, rel_h, rel_w):
    grid_rows = query_f.shape[0] // G
    head_count = query_f.shape[1]
    near_h, pick_h = table_rows(rel_h, row_first, grid_rows)
    near_w, pick_w = table_rows(rel_w, 0, G)
    shaped = query_f.reshape(grid_rows, G, head_count, query_f.shape[2])
    term_h = jnp.einsum("awhc,akc->awhk", shaped, near_h, precision=highest)
    term_w = jnp.einsum("awhc,wkc->awhk", shaped, near_w, precision=highest)
    return (
        term_h.reshape(-1, head_count, G),
        term_w.reshape(-1, head_count, G),
        near_h,
        near_w,
        pick_h,
        pick_w,
    )


def piece_scores(query, key_h, term_h, term_w, factor):
    num_keys = key_h.shape[0]
    products = jnp.einsum("rhc,nhc->rhn", query, key_h, preferred_element_type=jnp.float32)
    position = (term_h[..., :, None] + term_w[..., None, :]).reshape(
        term_h.shape[0], term_h.shape[1], num_keys
    )
    return products * factor + position


def attend_step(running, pieces, offset, query, term_h, term_w, factor):
    run_max, run_sum, accumulated = running
    key_piece, value_piece = pieces
    num_keys = key_piece.shape[0]
    head_count = query.shape[1]
    key_h = key_piece.reshape(num_keys, head_count, -1)
    value_h = value_piece.reshape(num_keys, head_count, -1)
    scores = piece_scores(query, key_h, term_h, term_w, factor)
    new_max = jnp.maximum(run_max, jnp.max(scores, axis=-1))
    weights_p = jnp.exp(scores - new_max[..., None])
    run_sum = jnp.sum(weights_p, axis=-1)
    accumulated = jnp.einsum(
        "rhn,nhc->rhc", weights_p.astype(jnp.bfloat16), value_h, preferred_element_type=jnp.float32
    )
    return (new_max, run_sum, accumulated)


def grad_step(running, pieces, offset, query, out_grad, log_total, row_dot, term_h, term_w, factor):
    key_piece, value_piece = pieces
    num_keys = key_piece.shape[0]
    num_rows, head_count, head_size = query.shape
    key_h = key_piece.reshape(num_keys, head_count, head_size)
    value_h = value_piece.reshape(num_keys, head_count, head_size)
    scores = piece_scores(query, key_h, term_h, term_w, factor)
    weights_p = jnp.exp(scores - log_total[..., None])
    prob_grad = jnp.einsum("rhc,nhc->rhn", out_grad, value_h, preferred_element_type=jnp.float32)
    score_grad = (weights_p * (prob_grad - row_dot[..., None])).astype(jnp.bfloat16)
    query_acc = jnp.einsum("rhn,nhc->rhc", score_grad, key_h, preferred_element_type=jnp.float32)
    key_grad = (
        jnp.einsum("rhn,rhc->nhc", score_grad, query, preferred_element_type=jnp.float32) * factor
    )
    value_grad = jnp.einsum(
        "rhn,rhc->nhc", weights_p.astype(jnp.bfloat16), out_grad, preferred_element_type=jnp.float32
    )
    joined = jnp.concatenate(
        [key_grad.reshape(num_keys, -1), value_grad.reshape(num_keys, -1)], axis=1
    )
    grid_grad = score_grad.reshape(num_rows, head_count, num_keys // G, G)
    part_h = jnp.sum(grid_grad, axis=-1, dtype=jnp.float32)
    grad_w = jnp.sum(grid_grad, axis=-2, dtype=jnp.float32)
    return (query_acc, joined, part_h, grad_w)


def tensor_total(partial_sum):
    return lax.psum(partial_sum.astype(jnp.bfloat16), "tp").astype(jnp.float32)


def contract_last(left_mat, right_mat):
    return lax.dot_general(
        left_mat, right_mat, (((1,), (1,)), ((), ())), preferred_element_type=jnp.float32
    )


def micro_step(weights_full, picture, cotangent, params):
    (
        gain_one,
        shift_one,
        qv_shift,
        rel_h,
        rel_w,
        proj_shift,
        gain_two,
        shift_two,
        up_shift,
        down_shift,
    ) = params
    qkv_full, proj_full, up_full, down_full = weights_full
    rows_dev = picture.shape[0]
    half_width = qkv_full.shape[2]
    head_count = half_width // HD
    grid_rows = rows_dev // G
    row_first = lax.axis_index("ctx") * grid_rows
    factor = HD ** (-0.5)
    source = picture.astype(jnp.float32)
    normed_f, standard_one, inverse_one = layer_norm(source, gain_one, shift_one)
    normed = normed_f.astype(jnp.bfloat16)
    projected = jnp.einsum("rd,jde->jre", normed, qkv_full, preferred_element_type=jnp.float32)
    query_flat = (projected[0] + qv_shift[0]).astype(jnp.bfloat16)
    key_flat = projected[1].astype(jnp.bfloat16)
    value_flat = (projected[2] + qv_shift[1]).astype(jnp.bfloat16)
    query = query_flat.reshape(rows_dev, head_count, HD)
    query_f = query.astype(jnp.float32)
    term_h, term_w, near_h, near_w, pick_h, pick_w = rel_terms(query_f, row_first, rel_h, rel_w)
    start_state = (
        jnp.full((rows_dev, head_count), -1e30, jnp.float32),
        jnp.zeros((rows_dev, head_count), jnp.float32),
        jnp.zeros((rows_dev, head_count, HD), jnp.float32),
    )
    forward_fn = partial(attend_step, query=query, term_h=term_h, term_w=term_w, factor=factor)
    run_max, run_sum, accumulated = forward_fn(
        start_state,
        (
            lax.all_gather(key_flat, "ctx", axis=0, tiled=True),
            lax.all_gather(value_flat, "ctx", axis=0, tiled=True),
        ),
        jnp.int32(0),
    )
    attended = accumulated / run_sum[..., None]
    log_total = run_max + jnp.log(run_sum)
    mixed = attended.reshape(rows_dev, half_width).astype(jnp.bfloat16)
    middle = source + tensor_total(contract_last(mixed, proj_full)) + proj_shift
    normed2_f, standard_two, inverse_two = layer_norm(middle, gain_two, shift_two)
    normed2 = normed2_f.astype(jnp.bfloat16)
    hidden = jnp.dot(normed2, up_full, preferred_element_type=jnp.float32) + up_shift
    active, gelu_back = jax.vjp(exact_gelu, hidden)
    active_low = active.astype(jnp.bfloat16)
    result = (middle + tensor_total(contract_last(active_low, down_full)) + down_shift).astype(
        jnp.bfloat16
    )
    top_f = cotangent.astype(jnp.float32)
    down_grad = jnp.einsum("rd,rf->df", cotangent, active_low, preferred_element_type=jnp.float32)
    down_shift_grad = jnp.sum(top_f, axis=0)
    active_grad = jnp.dot(cotangent, down_full, preferred_element_type=jnp.float32)
    hidden_grad = gelu_back(active_grad)[0].astype(jnp.bfloat16)
    up_grad = jnp.einsum("rd,rf->df", normed2, hidden_grad, preferred_element_type=jnp.float32)
    up_shift_grad = jnp.sum(hidden_grad, axis=0, dtype=jnp.float32)
    normed2_grad = lax.psum(contract_last(hidden_grad, up_full).astype(jnp.bfloat16), "tp").astype(
        jnp.float32
    )
    middle_grad = top_f + norm_back_plain(normed2_grad, standard_two, inverse_two, gain_two)
    gain_two_grad = jnp.sum(normed2_grad * standard_two, axis=0)
    shift_two_grad = jnp.sum(normed2_grad, axis=0)
    branch_grad = middle_grad.astype(jnp.bfloat16)
    proj_grad = jnp.einsum("rd,re->de", branch_grad, mixed, preferred_element_type=jnp.float32)
    proj_shift_grad = jnp.sum(branch_grad, axis=0, dtype=jnp.float32)
    mixed_grad = (
        jnp.dot(branch_grad, proj_full, preferred_element_type=jnp.float32)
        .astype(jnp.bfloat16)
        .reshape(rows_dev, head_count, HD)
    )
    row_dot = jnp.sum(mixed_grad.astype(jnp.float32) * attended, axis=-1)
    ctx_count = lax.axis_size("ctx")
    start_back = (
        jnp.zeros((rows_dev, head_count, HD), jnp.float32),
        jnp.zeros((rows_dev * ctx_count, 2 * half_width), jnp.float32),
        jnp.zeros((rows_dev, head_count, G), jnp.float32),
        jnp.zeros((rows_dev, head_count, G), jnp.float32),
    )
    back_fn = partial(
        grad_step,
        query=query,
        out_grad=mixed_grad,
        log_total=log_total,
        row_dot=row_dot,
        term_h=term_h,
        term_w=term_w,
        factor=factor,
    )
    query_acc, key_value_acc, grad_h, grad_w = back_fn(
        start_back,
        (
            lax.all_gather(key_flat, "ctx", axis=0, tiled=True),
            lax.all_gather(value_flat, "ctx", axis=0, tiled=True),
        ),
        jnp.int32(0),
    )
    key_value_mine = lax.psum_scatter(
        key_value_acc.astype(jnp.bfloat16), "ctx", scatter_dimension=0, tiled=True
    ).astype(jnp.float32)
    grid_h = grad_h.reshape(grid_rows, G, head_count, G)
    grid_w = grad_w.reshape(grid_rows, G, head_count, G)
    shaped_q = query_f.reshape(grid_rows, G, head_count, HD)
    rel_query = jnp.einsum("awhk,akc->awhc", grid_h, near_h, precision=highest) + jnp.einsum(
        "awhk,wkc->awhc", grid_w, near_w, precision=highest
    )
    query_grad = (
        (query_acc * factor + rel_query.reshape(rows_dev, head_count, HD))
        .reshape(rows_dev, half_width)
        .astype(jnp.bfloat16)
    )
    key_grad = key_value_mine[:, :half_width].astype(jnp.bfloat16)
    value_grad = key_value_mine[:, half_width:].astype(jnp.bfloat16)
    table_h_part = jnp.dot(
        pick_h.T,
        jnp.einsum("awhk,awhc->akc", grid_h, shaped_q, precision=highest).reshape(-1, HD),
        precision=highest,
    )
    table_w_part = jnp.dot(
        pick_w.T,
        jnp.einsum("awhk,awhc->wkc", grid_w, shaped_q, precision=highest).reshape(-1, HD),
        precision=highest,
    )
    stacked = jnp.stack([query_grad, key_grad, value_grad])
    qkv_grad = jnp.einsum("rd,jre->jde", normed, stacked, preferred_element_type=jnp.float32)
    qv_shift_grad = jnp.stack(
        [
            jnp.sum(query_grad, axis=0, dtype=jnp.float32),
            jnp.sum(value_grad, axis=0, dtype=jnp.float32),
        ]
    )
    normed_part = jnp.einsum("jre,jde->rd", stacked, qkv_full, preferred_element_type=jnp.float32)
    normed_grad, table_h_grad, table_w_grad = (
        lax.psum(normed_part.astype(jnp.bfloat16), "tp").astype(jnp.float32),
        lax.psum(table_h_part.astype(jnp.bfloat16), "tp").astype(jnp.float32),
        lax.psum(table_w_part.astype(jnp.bfloat16), "tp").astype(jnp.float32),
    )
    input_grad = (middle_grad + norm_back_plain(normed_grad, standard_one, inverse_one, gain_one)).astype(
        jnp.bfloat16
    )
    gain_one_grad = jnp.sum(normed_grad * standard_one, axis=0)
    shift_one_grad = jnp.sum(normed_grad, axis=0)
    big_grads = (qkv_grad, proj_grad, up_grad, down_grad)
    small_grads = (
        gain_one_grad,
        shift_one_grad,
        qv_shift_grad,
        table_h_grad,
        table_w_grad,
        proj_shift_grad,
        gain_two_grad,
        shift_two_grad,
        up_shift_grad,
        down_shift_grad,
    )
    return (result, input_grad, big_grads, small_grads)


def add_trees(first_tree, second_tree):
    return jax.tree.map(lambda first_v, second_v: first_v + second_v, first_tree, second_tree)


def zeros_like_tree(tree):
    return jax.tree.map(lambda member: jnp.zeros(member.shape, jnp.float32), tree)


def local(
    images,
    norm1_gain,
    norm1_bias,
    qkv_weight,
    qv_bias,
    rel_pos_h,
    rel_pos_w,
    proj_weight,
    proj_bias,
    norm2_gain,
    norm2_bias,
    up_weight,
    up_bias,
    down_weight,
    down_bias,
    out_cotangent,
):
    params = tuple(
        (
            member.astype(jnp.float32)
            for member in (
                norm1_gain,
                norm1_bias,
                qv_bias,
                rel_pos_h,
                rel_pos_w,
                proj_bias,
                norm2_gain,
                norm2_bias,
                up_bias,
                down_bias,
            )
        )
    )
    small_start = zeros_like_tree(params)

    def per_batch(totals, pair):
        weights_full = (
            lax.all_gather(qkv_weight, ("fsdp", "ctx"), axis=1, tiled=True),
            lax.all_gather(proj_weight, ("fsdp", "ctx"), axis=0, tiled=True),
            lax.all_gather(up_weight, ("fsdp", "ctx"), axis=0, tiled=True),
            lax.all_gather(down_weight, ("fsdp", "ctx"), axis=0, tiled=True),
        )
        result, input_grad, big_grads, small_grads = micro_step(
            weights_full, pair[0], pair[1], params
        )
        shards = (
            lax.psum_scatter(big_grads[0], ("fsdp", "ctx"), scatter_dimension=1, tiled=True),
            lax.psum_scatter(big_grads[1], ("fsdp", "ctx"), scatter_dimension=0, tiled=True),
            lax.psum_scatter(big_grads[2], ("fsdp", "ctx"), scatter_dimension=0, tiled=True),
            lax.psum_scatter(big_grads[3], ("fsdp", "ctx"), scatter_dimension=0, tiled=True),
        )
        return (add_trees(totals, (shards, small_grads)), (result, input_grad))

    shard_start = zeros_like_tree((qkv_weight, proj_weight, up_weight, down_weight))
    (shard_totals, small_totals), (outputs, input_grads) = lax.scan(
        per_batch, (shard_start, small_start), (images, out_cotangent)
    )
    small_final = lax.psum(small_totals, ("fsdp", "ctx"))
    return (
        outputs,
        input_grads,
        small_final[0],
        small_final[1],
        shard_totals[0],
        small_final[2],
        small_final[3],
        small_final[4],
        shard_totals[1],
        small_final[5],
        small_final[6],
        small_final[7],
        shard_totals[2],
        small_final[8],
        shard_totals[3],
        small_final[9],
    )


def solution(mesh):
    shape = dict(mesh.shape)
    body = partial(grouped, shape) if shape == {"fsdp": 4, "ctx": 4, "tp": 2} else local
    placed = (
        P("fsdp", "ctx", None),
        P(),
        P(),
        P(None, ("fsdp", "ctx"), "tp"),
        P(None, "tp"),
        P(),
        P(),
        P(("fsdp", "ctx"), "tp"),
        P(),
        P(),
        P(),
        P(("fsdp", "ctx"), "tp"),
        P("tp"),
        P(("fsdp", "ctx"), "tp"),
        P(),
        P("fsdp", "ctx", None),
    )
    return jax.shard_map(
        body,
        mesh=mesh,
        in_specs=placed,
        out_specs=(
            P("fsdp", "ctx", None),
            P("fsdp", "ctx", None),
            P(),
            P(),
            P(None, ("fsdp", "ctx"), "tp"),
            P(None, "tp"),
            P(),
            P(),
            P(("fsdp", "ctx"), "tp"),
            P(),
            P(),
            P(),
            P(("fsdp", "ctx"), "tp"),
            P("tp"),
            P(("fsdp", "ctx"), "tp"),
            P(),
        ),
        check_vma=False,
    )
```

```python
from functools import partial

import jax
import jax.numpy as jnp
import ml_dtypes
import numpy as np
from jax import lax
from jax.experimental import pallas as pl
from jax.experimental.pallas import tpu as pltpu
from jax.sharding import PartitionSpec as P

G = 48
HD = 64


eps = 1e-06
highest = lax.Precision.HIGHEST
bf16, f32 = jnp.bfloat16, jnp.float32
VMEM_BYTES = 56 * 1024 * 1024
NN = (((1,), (0,)), ((), ()))
NT = (((1,), (1,)), ((), ()))
TN = (((0,), (0,)), ((), ()))
LH, LW = 64, 112
ANY = pl.BlockSpec(memory_space=pl.ANY)
PEAK = 1.0e15


def mm(a, b, dims=NN):
    return lax.dot_general(a, b, dims, preferred_element_type=f32)


def roll(x, shift, stride=None):
    extra = {} if stride is None else dict(stride=stride, stride_axis=0)
    return pltpu.roll(x, shift, 1, **extra)


def lane_iota(shape):
    return lax.broadcasted_iota(jnp.int32, shape, 1)


def struct(shape, dtype=bf16):
    return jax.ShapeDtypeStruct(shape, dtype)


def whole(shape):
    return pl.BlockSpec(shape, lambda *_: (0,) * len(shape))


def call(kernel, name, us, grid, prefetch, ins, in_specs, outs, out_specs, scratch=(), aliases=None):
    return pl.pallas_call(
        kernel,
        out_shape=outs,
        grid_spec=pltpu.PrefetchScalarGridSpec(
            num_scalar_prefetch=1, grid=grid, in_specs=in_specs, out_specs=out_specs, scratch_shapes=list(scratch)
        ),
        input_output_aliases=aliases or {},
        compiler_params=pltpu.CompilerParams(vmem_limit_bytes=VMEM_BYTES),
        cost_estimate=pl.CostEstimate(flops=int(us * 1e-6 * PEAK), bytes_accessed=0, transcendentals=0),
        name=name,
    )(prefetch, *ins)


def columns(w_ref, side):
    width = w_ref.shape[2] // 2
    parts = [jnp.where(side == 0, w_ref[j, :, :width], w_ref[j, :, width:]) for j in range(3)]
    return jnp.concatenate([p[:, :128] for p in parts] + [p[:, 128:] for p in parts], axis=1)


def pack_kernel(at_ref, image_ref, w_ref, out_ref):
    rows = image_ref.shape[1]
    depth = w_ref.shape[1]
    out_ref[:rows] = image_ref[0]
    out_ref[rows:] = jnp.zeros((depth, out_ref.shape[1]), bf16)
    out_ref[rows:, :576] = columns(w_ref, 1 - at_ref[0])


def pack(at, images, w):
    batch, quarter, d = images.shape
    rows = quarter // 2
    out = (rows + w.shape[1], d)
    return call(
        pack_kernel, "pack", 2, (1,), at, [images, w],
        [pl.BlockSpec((1, rows, d), lambda i, o: (o[1], 1 - o[0], 0)), whole(w.shape)], struct(out), whole(out),
    )


def route_kernel(at_ref, image_ref, got_ref, w_ref, ub_ref, qvb_ref, gain_ref, bias_ref, near_ref, normed_ref, w_out_ref):
    rows = image_ref.shape[1]
    depth = w_ref.shape[1]
    same = at_ref[0] == at_ref[2]
    own, got = image_ref[0], got_ref[:rows]
    near = jnp.where(same, own, got)
    near_ref[...] = near
    normed_ref[...] = norm(near.astype(f32), gain_ref[...], bias_ref[...])[0].astype(bf16)
    w_out_ref[...] = jnp.zeros(w_out_ref.shape, bf16)
    w_out_ref[:depth, :576] = columns(w_ref, at_ref[0])
    w_out_ref[depth:2 * depth] = got_ref[rows:]
    d = image_ref.shape[2]
    w_out_ref[2 * depth:2 * depth + 1] = ub_ref[:, :d]
    w_out_ref[2 * depth + 1:2 * depth + 2] = ub_ref[:, d:]
    w_out_ref[2 * depth + 2:2 * depth + 3] = qvb_ref[...]


def route(at, images, got, w, up_bias, qv_bias, gain, bias):
    batch, quarter, d = images.shape
    rows = quarter // 2
    half = (rows, d)
    out = (2 * w.shape[1] + 16, d)
    return call(
        route_kernel, "route", 3, (1,), at, [images, got, w, up_bias, qv_bias, gain, bias],
        [pl.BlockSpec((1, rows, d), lambda i, o: (o[1], o[0], 0))] + [whole(v.shape) for v in (got, w, up_bias, qv_bias, gain, bias)],
        (struct(half), struct(half), struct(out)), [whole(half)] * 2 + [whole(out)],
    )


def far_kernel(at_ref, a_ref, b_ref, gain_ref, bias_ref, *refs):
    far_ref, out_ref = refs[-2:]
    far = jnp.where(at_ref[0] == at_ref[2], a_ref[...], b_ref[...])
    far_ref[...] = far
    out_ref[...] = norm(far.astype(f32), gain_ref[...], bias_ref[...])[0].astype(bf16)


def take_far(at, a, b, gain, bias, after):
    return call(
        far_kernel, "take_far", 2, (1,), at, [a, b, gain, bias] + after, [whole(v.shape) for v in (a, b, gain, bias)] + [ANY] * len(after),
        (struct(a.shape), struct(a.shape)), [whole(a.shape)] * 2,
    )


def arrange_kernel(me_ref, *refs):
    pieces, out_ref = refs[:-1], refs[-1]
    depth = pieces[0].shape[0] // 2
    out_ref[:, 576:] = jnp.zeros((out_ref.shape[0], 64), bf16)
    for dx in range(2):
        for dz in range(4):
            for dc in range(2):
                ref, lo = (pieces[dz], dc) if dx == 0 else (pieces[4], dz * 2 + dc)
                at = (dx * 8 + dc * 4 + dz) ^ me_ref[0]
                out_ref[pl.ds(pl.multiple_of(at * depth, 16), depth), :576] = ref[lo * depth:(lo + 1) * depth]


def arrange(me, pieces, rows):
    return call(
        arrange_kernel, "arrange", 2, (1,), me, pieces, [whole(p.shape) for p in pieces],
        struct((rows, 640)), whole((rows, 640)),
    )


def prep_kernel(order_ref, *refs):
    xs, refs = refs[:4], refs[4:]
    w_ref, b_ref, tab_ref, hot_ref = refs[:4]
    q_ref, k_ref, v_ref, n_ref = refs[-4:]
    step = pl.program_id(0)
    rows = q_ref.shape[1]

    def work(x):
        first_row = order_ref[4 + step]
        n_ref[...] = x
        qkv = (mm(x, w_ref[...]) + b_ref[...]).astype(bf16).astype(f32)
        lane = lane_iota((G, 128))
        lane_all = lane_iota((rows, 128))
        hot_a = hot_ref[0, :, :128].astype(f32)
        hot_b = hot_ref[0, :, 128:]
        cols = [qkv[:, i * 128:(i + 1) * 128] for i in range(5)]
        back = [roll(v, 64) for v in cols[:4]]
        for h, (q, k, v) in enumerate(
            ((cols[0], cols[1], cols[2]), (back[0], back[1], back[2]), (cols[3], back[3], cols[4]))
        ):
            k_ref[h, :, :128] = jnp.where(lane_all < 64, k, hot_a).astype(bf16)
            k_ref[h, :, 128:] = hot_b
            v_ref[h] = jnp.where(lane_all < 64, v, jnp.where(lane_all < 67, 1.0, 0.0)).astype(bf16)
            turned = mm(q.astype(bf16), tab_ref[...])
            qf = q * (HD ** -0.5)
            for g in range(rows // G):
                r = first_row + g
                along_h = turned[g * G:(g + 1) * G, :128]
                along_w = turned[g * G:(g + 1) * G, 128:]
                h_a = roll(along_h, (LH - (G - 1) + 128 + r) % 128)
                h_b = roll(along_h, (32 - (G - 1) + 128 + r) % 128)
                w_a = roll(along_w, (LW - (G - 1)) % 128, 1)
                w_b = roll(along_w, (80 - (G - 1)) % 128, 1)
                h_lo = h_b - h_b.astype(bf16).astype(f32)
                w_lo = w_b - w_b.astype(bf16).astype(f32)
                first = jnp.where(lane < LH, qf[g * G:(g + 1) * G], jnp.where(lane < LW, h_a, w_a))
                second = jnp.where(lane < 32, w_a, jnp.where(lane < 80, h_lo, w_lo))
                q_ref[h, g * G:(g + 1) * G, :128] = first.astype(bf16)
                q_ref[h, g * G:(g + 1) * G, 128:] = second.astype(bf16)

    for k in range(4):
        @pl.when(step == k)
        def _(k=k):
            work(xs[k][...])


def prep(order, xs, w, b, tab, hot, heads, before, group):
    rows, d = xs[0].shape
    tokens = len(xs) * 2 * rows
    outs = (struct((heads, tokens, 256)), struct((heads, tokens, 256)), struct((heads, tokens, 128)), struct((tokens, d)))
    return call(
        prep_kernel, "prep", 7, (len(xs),), order, list(xs) + [w, b, tab, hot] + list(before),
        [whole(x.shape) for x in xs] + [whole(w.shape), whole(b.shape), whole(tab.shape)]
        + [pl.BlockSpec((1, rows, 256), lambda i, o: (o[i], 0, 0))] + [ANY] * len(before),
        outs,
        [
            pl.BlockSpec((heads, rows, 256), lambda i, o: (0, 2 * i + group, 0)),
            pl.BlockSpec((heads, rows, 256), lambda i, o: (0, 2 * i + group, 0)),
            pl.BlockSpec((heads, rows, 128), lambda i, o: (0, 2 * i + group, 0)),
            pl.BlockSpec((rows, d), lambda i, o: (2 * i + group, 0)),
        ],
        aliases={9 + i: i for i in range(len(before))},
    )


def attend_kernel(order_ref, q_ref, k_ref, v_ref, *refs, tiles):
    att_ref, q2_ref, mix_ref = refs[-3:]
    head = pl.program_id(0)
    start = 0
    for tile in tiles:
        at = pl.ds(start, tile)
        start += tile
        lane = lane_iota((tile, 128))
        q = q_ref[0, at, :]
        s = mm(q, k_ref[0], NT)
        m = jnp.max(s, axis=1, keepdims=True)
        p = jnp.exp(s - m)
        o = mm(p.astype(bf16), v_ref[0])
        total = o[:, 64:65]
        att = o / total
        lse = m + jnp.log(total)
        att_ref[0, at, :] = att
        low_att = att[:, :64].astype(bf16)
        for h in range(3):
            @pl.when(head == h)
            def _(h=h):
                mix_ref[at, h * 64:(h + 1) * 64] = low_att
        a = q[:, :128].astype(f32)
        b = q[:, 128:].astype(f32)
        full = a + roll(b, 32) - lse
        high = full.astype(bf16)
        low = roll(full - high.astype(f32), 96)
        q2_ref[0, at, :128] = jnp.where((lane >= LH) & (lane < LW), high.astype(f32), a).astype(bf16)
        q2_ref[0, at, 128:] = jnp.where((lane >= 32) & (lane < 80), low, b).astype(bf16)


def attend(q, k, v, side):
    heads, tokens, _ = q.shape
    rows = tokens // 2
    tiles = (256,) * (rows // 256) + ((rows % 256,) if rows % 256 else ())
    return call(
        partial(attend_kernel, tiles=tiles), "attend", 19, (heads,), jnp.zeros((1,), jnp.int32), [q, k, v],
        [
            pl.BlockSpec((1, rows, 256), lambda h, o: (h, side, 0)),
            pl.BlockSpec((1, tokens, 256), lambda h, o: (h, 0, 0)),
            pl.BlockSpec((1, tokens, 128), lambda h, o: (h, 0, 0)),
        ],
        (struct((heads, rows, 128), f32), struct((heads, rows, 256)), struct((rows, heads * HD))),
        [pl.BlockSpec((1, rows, 128), lambda h, o: (h, 0, 0)), pl.BlockSpec((1, rows, 256), lambda h, o: (h, 0, 0)), whole((rows, heads * HD))],
    )


def back_kernel(order_ref, qa_ref, qb_ref, k_ref, v_ref, atta_ref, attb_ref, own_ref, beside_ref, core_ref, tab_ref, turn_ref,
                d_ref, table_ref, q_ref, go_ref, kt_ref, acc_ref, hi_ref, lo_ref, *, tile, sets, first, count):
    head, step = pl.program_id(0), pl.program_id(1)
    last = pl.num_programs(1) - 1
    tokens = k_ref.shape[1]
    rows = tokens // sets
    wide = count * 64

    @pl.when(step == 0)
    def _():
        lane = lane_iota((rows, 128))
        for n, (ref, from_row) in enumerate(((own_ref, 0), (core_ref, 0), (beside_ref, 0), (core_ref, rows))):
            at = pl.ds(n * rows, rows)
            for h in range(count):
                @pl.when(head == h)
                def _(ref=ref, at=at, h=h, from_row=from_row):
                    lo = (first + h) * 64
                    go_ref[at, :64] = ref[from_row:from_row + rows, lo:lo + 64]
        go = go_ref[...].astype(f32)
        lane = lane_iota(go.shape)
        go = jnp.where(lane < 64, go, 0.0)
        att = jnp.concatenate([atta_ref[0], attb_ref[0]], axis=0)
        q_ref[:tokens // 2] = qa_ref[0]
        q_ref[tokens // 2:] = qb_ref[0]
        dot = jnp.sum(jnp.where(lane < 64, go * att, 0.0), axis=1, keepdims=True)
        high = dot.astype(bf16).astype(f32)
        mid = (dot - high).astype(bf16).astype(f32)
        low = dot - high - mid
        go_ref[...] = jnp.where(lane < 64, go, jnp.where(lane == 64, -high, jnp.where(lane == 65, -mid, jnp.where(lane == 66, -low, 0.0)))).astype(bf16)
        acc_ref[...] = jnp.zeros_like(acc_ref)
        kt_ref[:LW] = k_ref[0, :, :128].T[:LW]
        kt_ref[LW:] = turn_ref[...]

    keys = tokens // pl.num_programs(1)
    for i in range(keys // tile):
        at = pl.ds(pl.multiple_of(step * keys + i * tile, tile), tile)
        s = mm(k_ref[0, at, :], q_ref[...], NT)
        p = jnp.exp(s)
        pb = p.astype(bf16)
        d = (p * mm(v_ref[0, at, :], go_ref[...], NT)).astype(bf16)
        dv = mm(pb, go_ref[...]).astype(bf16)
        dk = mm(d, q_ref[:, :128]).astype(bf16)
        for h in range(count):
            @pl.when(head == h)
            def _(h=h):
                d_ref[at, 2 * wide + h * 64:2 * wide + (h + 1) * 64] = dv[:, :64]
                d_ref[at, wide + h * 64:wide + (h + 1) * 64] = dk[:, :64]
        acc_ref[...] += mm(kt_ref[:, at], d)

    @pl.when(step == last)
    def _():
        small = lane_iota((G, 128))
        a = acc_ref[:128].T
        b = jnp.concatenate([acc_ref[128:160], jnp.zeros((96, tokens), f32)], axis=0).T
        for g in range(tokens // G):
            block, inner = divmod(g, rows // 2 // G)
            r = order_ref[block] + inner
            ag = a[g * G:(g + 1) * G]
            bg = b[g * G:(g + 1) * G]
            along_h = jnp.where((small >= LH) & (small < LW), ag, 0.0)
            along_w = jnp.where(small >= LW, ag, jnp.where(small < 32, bg, 0.0))
            along_h = roll(along_h, (256 + G - 1 - LH - r) % 128)
            along_w = roll(along_w, (128 - LW) % 128, 1)
            h_hi = along_h.astype(bf16)
            w_hi = along_w.astype(bf16)
            hi_ref[g * G:(g + 1) * G, :128] = h_hi
            hi_ref[g * G:(g + 1) * G, 128:] = w_hi
            lo_ref[g * G:(g + 1) * G, :128] = (along_h - h_hi.astype(f32)).astype(bf16)
            lo_ref[g * G:(g + 1) * G, 128:] = (along_w - w_hi.astype(f32)).astype(bf16)
        turned = mm(hi_ref[...], tab_ref[...], NT) + mm(lo_ref[...], tab_ref[...], NT)
        dq = (a * (HD ** -0.5) + turned).astype(bf16)
        for h in range(count):
            @pl.when(head == h)
            def _(h=h):
                d_ref[:, h * 64:(h + 1) * 64] = dq[:, :64]
        tables = mm(hi_ref[...], q_ref[:, :128], TN)

        @pl.when(head == 0)
        def _():
            table_ref[...] = tables

        @pl.when(head > 0)
        def _():
            table_ref[...] += tables


def attend_back(order, q2, k, v, att, grads, tab, turn, first, count, steps, tile, sets):
    _, tokens, _ = k.shape
    at = lambda h, i, o: (first + h, 0, 0)
    wide = 3 * count * HD
    per_head = lambda a: pl.BlockSpec((1,) + a.shape[1:], at)
    return call(
        partial(back_kernel, tile=tile, sets=sets, first=first, count=count), "attend_back", 21 * count,
        (count, steps), order, list(q2) + [k, v] + list(att) + list(grads) + [tab, turn],
        [per_head(a) for a in list(q2) + [k, v] + list(att)] + [whole(g.shape) for g in grads] + [whole(tab.shape), whole(turn.shape)],
        (struct((tokens, wide)), struct((256, 128), f32)),
        [whole((tokens, wide)), whole((256, 128))],
        [
            pltpu.VMEM((tokens, 256), bf16),
            pltpu.VMEM((tokens, 128), bf16),
            pltpu.VMEM((160, tokens), bf16),
            pltpu.VMEM((160, tokens), f32),
            pltpu.VMEM((tokens, 256), bf16),
            pltpu.VMEM((tokens, 256), bf16),
        ],
    )


def norm(v, gain, bias):
    mean = jnp.mean(v, axis=1, keepdims=True)
    centered = v - mean
    inverse = lax.rsqrt(jnp.mean(centered * centered, axis=1, keepdims=True) + eps)
    unit = centered * inverse
    return unit * gain + bias, unit, inverse


def norm_back(upstream, unit, inverse, gain):
    scaled = upstream * gain
    return inverse * (scaled - jnp.mean(scaled, axis=1, keepdims=True) - unit * jnp.mean(scaled * unit, axis=1, keepdims=True))


def mlp_kernel(order_ref, near_ref, beside_ref, core_ref, src0, src1, top0, top1, up_ref, down_ref, proj_ref, ub_ref, vec_ref,
               out0, out1, act_ref, hg_ref, n2_ref, mg_ref, br_ref, mix_ref, back_ref, ubg_ref, vg_ref,
               mid_ref, unit_ref, inv_ref, acc_ref, ng_ref, quad_ref, top_ref):
    step = pl.program_id(0)
    last = pl.num_programs(0) - 1
    part, d = src0.shape
    half = proj_ref.shape[3]
    width = near_ref.shape[1]

    def proj(i):
        return proj_ref[:, i].reshape(d, half)

    @pl.when(step == 0)
    def _():
        rows = near_ref.shape[0] // 2
        for k, piece in enumerate((near_ref[:rows], core_ref[:rows], beside_ref[:rows], core_ref[rows:])):
            quad_ref[order_ref[k]] = piece
        for i in range(4):
            mix_ref[:, i * width:(i + 1) * width] = quad_ref[i]
        top_ref[:part] = top0[...]
        top_ref[part:] = top1[...]
        mid = jnp.concatenate([src0[...], src1[...]], axis=0).astype(f32) + vec_ref[0:1] + mm(mix_ref[:, :half], proj(0), NT) + mm(mix_ref[:, half:], proj(1), NT)
        normed, unit, inverse = norm(mid, vec_ref[1:2], vec_ref[2:3])
        mid_ref[...] = mid
        unit_ref[...] = unit
        inv_ref[...] = inverse
        n2_ref[...] = normed.astype(bf16)

    tile = up_ref.shape[3]
    up = up_ref[:, 0].reshape(d, tile)
    down = down_ref[:, 0].reshape(d, tile)
    hidden = mm(n2_ref[...], up) + ub_ref[...]
    phi_all = 0.5 + 0.5 * lax.erf(hidden * (0.5 ** 0.5))
    slope = phi_all + hidden * (jnp.exp(-0.5 * hidden * hidden) * 0.3989422804014327)
    active = (hidden * phi_all).astype(bf16)
    hg = (mm(top_ref[...], down) * slope).astype(bf16)
    act_ref[...] = active
    hg_ref[...] = hg
    ubg_ref[...] = jnp.sum(hg.astype(f32), axis=0, keepdims=True)
    out = mm(active, down, NT)
    ng = mm(hg, up, NT)

    @pl.when(step == 0)
    def _():
        acc_ref[...] = out
        ng_ref[...] = ng

    @pl.when(step > 0)
    def _():
        acc_ref[...] += out
        ng_ref[...] += ng

    @pl.when(step == last)
    def _():
        top = top_ref[...].astype(f32)
        grad = ng_ref[...]
        unit = unit_ref[...]
        out = (mid_ref[...] + acc_ref[...] + vec_ref[3:4]).astype(bf16)
        out0[...] = out[:part]
        out1[...] = out[part:]
        middle = top + norm_back(grad, unit, inv_ref[...], vec_ref[1:2])
        branch = middle.astype(bf16)
        mg_ref[...] = middle
        br_ref[...] = branch
        for i in range(2):
            piece = mm(branch, proj(i)).astype(bf16)
            quad_ref[2 * i] = piece[:, :width]
            quad_ref[2 * i + 1] = piece[:, width:]
        for k in range(4):
            back_ref[k] = quad_ref[order_ref[k]]
        vg_ref[0:1] = jnp.sum(branch.astype(f32), axis=0, keepdims=True)
        vg_ref[1:2] = jnp.sum(grad * unit, axis=0, keepdims=True)
        vg_ref[2:3] = jnp.sum(grad, axis=0, keepdims=True)
        vg_ref[3:4] = jnp.sum(top, axis=0, keepdims=True)


def mlp(order, mixed, src, top, packed, up_bias, vecs, half_ff, tile):
    part, d = src[0].shape
    rows = 2 * part
    blocks, halves, depth, _ = packed.shape
    per = half_ff // tile
    half = d // halves
    quad = (4, rows, mixed[0].shape[1])
    ff = halves * half_ff
    by_tile = pl.BlockSpec((rows, tile), lambda i, o: (0, i))
    row_tile = pl.BlockSpec((1, tile), lambda i, o: (0, i))
    full = whole((rows, d))
    piece = whole((part, d))
    return call(
        mlp_kernel, "mlp", 24, (halves * per,), order,
        list(mixed) + list(src) + list(top) + [packed, packed, packed, up_bias, vecs],
        [whole(m.shape) for m in mixed] + [
            piece, piece, piece, piece,
            pl.BlockSpec((blocks, 1, depth, tile), lambda i, o: (0, i // per, 0, i % per)),
            pl.BlockSpec((blocks, 1, depth, tile), lambda i, o: (0, i // per, 0, per + i % per)),
            pl.BlockSpec((blocks, halves, depth, half), lambda i, o: (0, 0, 0, 2 * half_ff // half)),
            row_tile, whole(vecs.shape),
        ],
        (struct((part, d)), struct((part, d)), struct((rows, ff)), struct((rows, ff)), struct((rows, d)), struct((rows, d), f32), struct((rows, d)), struct((rows, d)))
        + (struct(quad),) + (struct((1, ff), f32), struct((4, d), f32)),
        [piece, piece, by_tile, by_tile, full, full, full, full] + [whole(quad)] + [row_tile, whole((4, d))],
        [
            pltpu.VMEM((rows, d), f32),
            pltpu.VMEM((rows, d), f32),
            pltpu.VMEM((rows, 1), f32),
            pltpu.VMEM((rows, d), f32),
            pltpu.VMEM((rows, d), f32),
            pltpu.VMEM(quad, bf16),
            pltpu.VMEM((rows, d), bf16),
        ],
    )


def wgrad_kernel(_, n2_ref, top0, top1, br_ref, hg_ref, act_ref, mix_ref, out_ref, left_ref):
    half, third = pl.program_id(0), pl.program_id(1)
    blocks, depth, tile = out_ref.shape

    @pl.when((half == 0) & (third == 0))
    def _():
        left_ref[0] = n2_ref[...].T
        left_ref[1] = jnp.concatenate([top0[...], top1[...]], axis=0).T
        left_ref[2] = br_ref[...].T

    at = 0
    for i, ref in enumerate((hg_ref, act_ref, mix_ref)):
        width = ref.shape[1]
        for k in range(3):
            lo, hi = max(at, k * tile), min(at + width, (k + 1) * tile)
            if lo < hi:
                @pl.when(third == k)
                def _(i=i, k=k, ref=ref, lo=lo, hi=hi, at=at):
                    part = mm(left_ref[i], ref[:, lo - at:hi - at]).astype(bf16)
                    out_ref[:, :, lo - k * tile:hi - k * tile] = part.reshape(blocks, depth, hi - lo)
        at += width


def wgrad(n2, top, branch, hg, active, mixed, blocks, halves):
    rows, d = n2.shape
    half_ff, half = hg.shape[1] // halves, d // halves
    depth = d // blocks
    total = 2 * half_ff + half
    by_half = lambda n: pl.BlockSpec((rows, n), lambda s, j, o: (0, s))
    return call(
        wgrad_kernel, "wgrad", 18, (halves, 3), jnp.zeros((1,), jnp.int32),
        [n2, top[0], top[1], branch, hg, active, mixed],
        [whole((rows, d)), whole(top[0].shape), whole(top[1].shape), whole((rows, d)), by_half(half_ff), by_half(half_ff), by_half(half)],
        struct((blocks, depth, halves * total)),
        pl.BlockSpec((blocks, depth, total // 3), lambda s, j, o: (0, 0, 3 * s + j)),
        [pltpu.VMEM((3, d, rows), bf16)],
    )


def down_kernel(_, a_ref, b_ref, w_ref, ng_ref):
    both = jnp.concatenate([a_ref[...], b_ref[...]], axis=1)
    ng_ref[0] = mm(both, w_ref[:, :both.shape[1]], NT).astype(bf16)


def grad_down(sets, grads, w, rows):
    d = w.shape[0]
    return call(
        down_kernel, "grad_down", 4, (2,), jnp.zeros((1,), jnp.int32), list(grads) + [w],
        [pl.BlockSpec((rows, g.shape[1]), lambda i, o: (2 * i + sets, 0)) for g in grads] + [whole(w.shape)],
        struct((2, rows, d)), pl.BlockSpec((1, rows, d), lambda i, o: (i, 0, 0)),
    )


def qkv_grad_kernel(_, x_ref, a_ref, b_ref, w_ref, wg_ref, bg_ref, ng_ref, acc_ref):
    step = pl.program_id(0)
    width = wg_ref.shape[-1]
    both = jnp.concatenate([a_ref[...], b_ref[...]], axis=1)
    add = mm(x_ref[...].T, both)
    sums = jnp.sum(both.astype(f32), axis=0, keepdims=True)

    @pl.when(step == 0)
    def _():
        acc_ref[...] = add
        bg_ref[...] = sums

    @pl.when(step > 0)
    def _():
        acc_ref[...] += add
        bg_ref[...] += sums

    @pl.when(step == pl.num_programs(0) - 1)
    def _():
        full = acc_ref[...]
        wg_ref[...] = full.astype(bf16).reshape(wg_ref.shape)
        w = w_ref[:, :width].astype(f32)
        lane = lane_iota(ng_ref.shape)
        a = jnp.sum(full * w, axis=1, keepdims=True)
        b = jnp.sum(bg_ref[...] * w, axis=1, keepdims=True)
        ng_ref[...] = jnp.where(lane == 0, a, jnp.where(lane == 1, b, 0.0))


def qkv_grad(x, grads, w, steps, blocks):
    tokens, d = x.shape
    rows = tokens // steps
    width = sum(g.shape[1] for g in grads)
    by_rows = lambda n: pl.BlockSpec((rows, n), lambda i, o: (i, 0))
    return call(
        qkv_grad_kernel, "qkv_grad", 5, (steps,), jnp.zeros((1,), jnp.int32), [x] + list(grads) + [w],
        [by_rows(d)] + [by_rows(g.shape[1]) for g in grads] + [whole(w.shape)],
        (struct((blocks, d // blocks, width)), struct((1, width), f32), struct((d, 128), f32)),
        [whole((blocks, d // blocks, width)), whole((1, width)), whole((d, 128))],
        [pltpu.VMEM((d, width), f32)],
    )


def finish_kernel(_, kept_ref, got_ref, passed_ref, middle_ref, src_ref, gain_ref, *refs):
    out_ref = refs[-1]
    grad = kept_ref[0].astype(f32) + got_ref[0].astype(f32) + passed_ref[...].astype(f32)
    _, unit, inverse = norm(src_ref[...].astype(f32), 1.0, 0.0)
    out_ref[...] = (middle_ref[...] + norm_back(grad, unit, inverse, gain_ref[...])).astype(bf16)


def finish(at, kept, got, passed, middle, src, gain, group, after=()):
    part, d = src.shape
    first = pl.BlockSpec((1, part, d), lambda i, o: (0, group, 0))
    return call(
        finish_kernel, "finish", 2, (1,), at, [kept, got, passed, middle, src, gain, *after],
        [first, first, whole((part, d)), pl.BlockSpec((part, d), lambda i, o: (group, 0)), whole((part, d)), whole(gain.shape)] + [ANY] * len(after),
        struct((part, d)), whole((part, d)),
    )


def assemble_kernel(at_ref, own_ref, other_ref, home_ref, home_other_ref, got_ref, out_ref):
    part = own_ref.shape[0]
    mine = pl.ds(pl.multiple_of(at_ref[0] * part, 16), part)
    other = pl.ds(pl.multiple_of((1 - at_ref[0]) * part, 16), part)
    same = at_ref[0] == at_ref[2]
    out_ref[at_ref[1], mine] = jnp.where(same, own_ref[...], home_ref[...])
    out_ref[1 - at_ref[1], mine] = jnp.where(same, other_ref[...], home_other_ref[...])
    out_ref[at_ref[1], other] = got_ref[0]
    out_ref[1 - at_ref[1], other] = got_ref[1]


def assemble(place, own, own_other, home, home_other, got):
    part, d = own.shape
    ins = [own, own_other, home, home_other, got]
    return call(
        assemble_kernel, "assemble", 3, (1,), place, ins, [whole(v.shape) for v in ins],
        struct((2, 2 * part, d)), whole((2, 2 * part, d)),
    )


AXES = ("fsdp", "ctx", "tp")


def pairs_of(shape, move):
    nf, nc, nt = shape["fsdp"], shape["ctx"], shape["tp"]
    flat = lambda f, z, t: (f * nc + z) * nt + t
    return [(flat(f, z, t), flat(*move(f, z, t))) for f in range(nf) for z in range(nc) for t in range(nt)]


def grouped(
    shape,
    images,
    norm1_gain,
    norm1_bias,
    qkv_weight,
    qv_bias,
    rel_pos_h,
    rel_pos_w,
    proj_weight,
    proj_bias,
    norm2_gain,
    norm2_bias,
    up_weight,
    up_bias,
    down_weight,
    down_bias,
    out_cotangent,
):
    nf, nc, nt = shape["fsdp"], shape["ctx"], shape["tp"]
    batch, quarter, d = images.shape
    sets = 4
    part = quarter // 2
    rows = 2 * part
    tokens = sets * rows
    half = qkv_weight.shape[2]
    width = half // 2
    heads = width // HD
    depth = qkv_weight.shape[1]
    blocks = nf * nc
    half_ff = up_weight.shape[1]
    fi, z, t = lax.axis_index("fsdp"), lax.axis_index("ctx"), lax.axis_index("tp")
    x, c = fi // 2, fi % 2
    zi, zp = z // 2, z % 2
    me = 2 * zp + c

    def send(v, move):
        return lax.ppermute(v, AXES, pairs_of(shape, move))

    core = lambda v: send(v, lambda f, w, u: (f ^ 1, w, u))
    tpswap = lambda v: send(v, lambda f, w, u: (f, w, u ^ 1))
    xswap = lambda v: send(v, lambda f, w, u: (f ^ 2, w, u))
    zswap = lambda v, k: send(v, lambda f, w, u: (f, w ^ k, u))
    beside = lambda v: zswap(v, 1)
    diagonal = lambda v: send(v, lambda f, w, u: (f ^ 1, w ^ 1, u))

    def pick(v, i, axis=0):
        return lax.dynamic_index_in_dim(v, i, axis, keepdims=False)

    def ordered(bit, mine, other, axis=0):
        return jnp.where(bit == 0, jnp.concatenate([mine, other], axis), jnp.concatenate([other, mine], axis))

    f = lambda v: v.astype(f32)
    tied = lambda *v: lax.optimization_barrier(v)
    ints = lambda *v: jnp.stack([jnp.asarray(i, jnp.int32) for i in v])
    place = ints(c, t, zi, zp)
    gain1, bias1 = f(norm1_gain)[None], f(norm1_bias)[None]

    image = lax.dynamic_index_in_dim(images, t, 0, False).reshape(2, part, d)
    is_far = lambda f, w: f % 2 != w // 2
    some = lambda v, move: lax.ppermute(
        v, AXES, [p for p in pairs_of(shape, move) if is_far(p[0] // (nc * nt), p[0] // nt % nc)]
    )
    far_a = some(pick(image, c), lambda f, w, u: (f, w ^ 2, u))
    far_b = some(pick(image, 1 - c), lambda f, w, u: (f ^ 1, w ^ 2, u))
    got = core(pack(place, images, qkv_weight))
    near, normed_near, w_own = route(place, images, got, qkv_weight, up_bias[None], qv_bias.reshape(1, d), gain1, bias1)
    w_other = tpswap(w_own)
    mine, yours = w_own[: 2 * depth, :576], w_other[: 2 * depth, :576]
    keep = jnp.where(t == zp, mine, yours)
    give = jnp.where(t == zp, yours, mine)
    w_z = [keep, zswap(give, 1), zswap(keep, 2), zswap(give, 3)]
    w = arrange(ints(fi * nc + z), w_z + [xswap(jnp.concatenate(w_z, axis=0))], d)
    near_sets = [normed_near, core(normed_near), beside(normed_near)]
    near_sets.append(core(near_sets[2]))
    far, normed_far = take_far(place, far_a, far_b, gain1, bias1, w_z[1:])

    own_w = jnp.concatenate([up_weight, down_weight, proj_weight], axis=1)
    own_w, normed_far = tied(own_w, normed_far)
    packed = lax.all_gather(own_w, AXES, axis=0, tiled=False).reshape(blocks, nt, depth, 2 * half_ff + half)

    far_sets = [normed_far, core(normed_far), beside(normed_far)]
    far_sets.append(core(far_sets[2]))

    bias = jnp.where(t == zp, qv_bias, w_other[2 * depth + 2].reshape(2, half))
    bias = pick(bias.reshape(2, 2, width), c, 1)
    bias = jnp.stack([bias[0], jnp.zeros_like(bias[0]), bias[1]])
    bias = f(jnp.concatenate([bias[:, :128].reshape(-1), bias[:, 128:].reshape(-1), jnp.zeros((64,), bf16)]))[None]
    flip = lambda v: jnp.pad(v[::-1].T, ((0, HD), (0, 128 - (2 * G - 1))))
    plain = lambda v: jnp.pad(v.T, ((0, HD), (0, 128 - (2 * G - 1))))
    tab = jnp.concatenate([flip(rel_pos_h), flip(rel_pos_w)], axis=1)
    tab_back = jnp.concatenate([flip(rel_pos_h), plain(rel_pos_w)], axis=1)
    block_rows = part // G
    first_of = lambda m, s_: (2 * m + s_ // 2) * (quarter // G) + (s_ % 2) * block_rows
    spot = np.concatenate([first_of(m, s_) * G + np.arange(part) for m in range(2) for s_ in range(sets)])
    at = np.arange(tokens)
    hot = np.zeros((tokens, 256), np.float32)
    for base, index in ((LH, spot // G), (LW, spot % G), (160, spot // G), (208, spot % G)):
        hot[at, base + index] = 1
    turn = np.zeros((G, tokens), np.float32)
    turn[G - 1 - at % G, at] = 1
    hot = jnp.asarray(hot.astype(ml_dtypes.bfloat16).reshape(2 * sets, part, 256))
    turn = jnp.asarray(turn.astype(ml_dtypes.bfloat16))

    order = [me ^ k for k in range(sets)]
    qkv = ()
    for g, group in enumerate((near_sets, far_sets)):
        m = zi ^ g
        spots = ints(*[m * sets + s for s in order], *[first_of(m, s) for s in order])
        qkv = prep(spots, group, w, bias, tab, hot, heads, qkv, g)
    q, k, v, normed = qkv

    normed, out_cotangent = tied(normed, out_cotangent)
    top_own = lax.dynamic_index_in_dim(out_cotangent, t, 0, False).reshape(2, part, d)
    top_got = core(pick(top_own, 1 - c))
    top_own = pick(top_own, c)
    top_near, top_far = jnp.where(c == zi, top_own, top_got), jnp.where(c == zi, top_got, top_own)
    q, top_near, top_far = tied(q, top_near, top_far)
    top_far = zswap(top_far, 2)
    att_far, q_far, mix_far = attend(q, k, v, 1)
    from_beside = beside(mix_far)
    att_near, q_near, mix_near = attend(q, k, v, 0)
    mix_near, from_beside, top_far = tied(mix_near, from_beside, top_far)
    top = [top_near, top_far]
    from_core = core(jnp.concatenate([mix_near[rows:], from_beside[rows:]], axis=0))
    att, q2 = (att_near, att_far), (q_near, q_far)

    other_up = w_other[2 * depth : 2 * depth + 2].reshape(-1)[:half_ff]
    full_bias = f(ordered(t, up_bias, other_up))[None]
    vecs = jnp.stack([f(proj_bias), f(norm2_gain), f(norm2_bias), f(down_bias)])
    (out0, out1, active, hidden_grad, normed2, middle_grad, branch, mixed, back, up_bias_grad, vec_grads) = mlp(
        ints(*order), [mix_near, from_beside, from_core], [near, far], top, packed, full_bias, vecs, half_ff, 768
    )
    back_beside = beside(back[2:].reshape(2 * rows, width))
    big = wgrad(normed2, top, branch, hidden_grad, active, mixed, blocks, nt)
    big, back_beside = tied(big, back_beside)
    back_core = core(jnp.concatenate([back[1], back_beside[rows:]], axis=0))
    back = [back[0], back_beside, back_core]
    big = lax.psum_scatter(big.reshape(d, -1), ("fsdp", "ctx"), scatter_dimension=0, tiled=True)
    big = big.reshape(depth, nt, -1)
    big = f(pick(big, t, 1)) + f(tpswap(pick(big, 1 - t, 1)))

    def give_back(own, own_other, home, home_other):
        a = jnp.stack([own, own_other])
        b = jnp.stack([home, home_other])
        return own, own_other, home, home_other, core(jnp.where(c == zi, b, a))

    out_home, out_own = zswap(out1, 2), tpswap(out0)

    spots = ints(*[first_of(zi ^ g, s) for s in order for g in range(2)])
    b_back, b_tables = attend_back(spots, q2, k, v, att, back, tab_back, turn, 2, 1, 3, 256, sets)
    q2, b_back, out_home, out_own = tied(q2, b_back, out_home, out_own)
    home_other = tpswap(out_home)
    a_back, a_tables = attend_back(spots, q2, k, v, att, back, tab_back, turn, 0, 2, 3, 256, sets)
    home_other, a_back = tied(home_other, a_back)
    result = (out0, out_own, out_home, home_other)
    grads = [a_back, b_back]

    to_core = grad_down(1, grads, w, rows)
    w, to_core = tied(w, to_core)
    got = core(to_core)
    kept = grad_down(0, grads, w, rows)
    passed = (f(kept[1]) + f(got[1])).astype(bf16)
    normed, passed = tied(normed, passed)
    passed1, passed0 = beside(passed[part:]), beside(passed[:part])
    wg, sums, ng = qkv_grad(normed, grads, w, 3, blocks)
    grad1 = finish(place, kept, got, passed1, middle_grad, far, gain1, 1)
    wg = wg.reshape(2, 2, 2, 2, depth, 3 * width)
    wg_x = xswap(pick(wg, 1 - x))
    tables = (a_tables + b_tables)[:, :HD] * HD ** 0.5
    home = zswap(grad1, 2)
    grad0 = finish(place, kept, got, passed0, middle_grad, near, gain1, 0, [grad1])
    grad_other = tpswap(grad0)

    def cut(v, sizes):
        at, out = 0, []
        v = v.reshape(-1)
        for size in sizes:
            out.append(lax.slice(v, (at,), (at + size,)))
            at += size
        return out

    grad1_, wg_x, tables, sums, ng, result = tied(grad1, wg_x, tables, sums, ng, result)
    sums = sums[0]
    qv = jnp.stack([jnp.concatenate([sums[i:i + 128], sums[j:j + 64]]) for i, j in ((0, 384), (256, 512))])
    qv = jnp.where(jnp.arange(sets)[:, None, None] == me, qv[None], 0.0).transpose(1, 0, 2).reshape(-1)
    small = jnp.concatenate(
        [vec_grads.reshape(-1), up_bias_grad.reshape(-1), ng[:, 0], ng[:, 1], qv, tables.reshape(-1)]
    ).reshape(-1, 128)
    for move in (core, tpswap, xswap):
        small = small + move(small)

    wg = f(pick(wg, x)) + f(wg_x)
    wg_low = wg.astype(bf16)
    wg = pick(wg, t, 2) + f(tpswap(pick(wg_low, 1 - t, 2)))
    result = assemble(place, *give_back(*result))
    grad1_, home, wg, small, result = tied(grad1_, home, wg, small, result)
    input_grad = assemble(place, *give_back(grad0, grad_other, home, tpswap(home)))
    wg_low = wg.astype(bf16)
    wg = pick(wg, zi, 1) + f(zswap(pick(wg_low, 1 - zi, 1), 2))
    wg = wg.astype(bf16)
    wg = send(wg, lambda f_, w_, u: (f_, (w_ // 2) * 2 + u, w_ % 2))
    wg = f(ordered(c, pick(wg, c)[None], core(pick(wg, 1 - c))[None]))
    wg = jnp.concatenate([wg[..., :384].reshape(2, depth, 3, 128), wg[..., 384:].reshape(2, depth, 3, 64)], axis=-1)
    wg = wg.transpose(2, 1, 0, 3).reshape(3, depth, half)

    for distance in (1, 2):
        small = small + zswap(small, distance)
    pb, g2, b2, db, ub, g1, b1, qv, tg = cut(small, (d, d, d, d, nt * half_ff, d, d, 2 * d, 256 * HD))
    g1 = (g1 - b1 * f(norm1_bias)) / f(norm1_gain)
    tg = tg.reshape(256, HD)
    return (
        result,
        input_grad,
        g1,
        b1,
        wg,
        pick(qv.reshape(2, nt, half), t, 1),
        tg[: 2 * G - 1][::-1],
        tg[128 : 128 + 2 * G - 1],
        big[:, 2 * half_ff :],
        pb,
        g2,
        b2,
        big[:, :half_ff],
        pick(ub.reshape(nt, half_ff), t),
        big[:, half_ff : 2 * half_ff],
        db,
    )


def layer_norm(values, gain_vec, shift_vec):
    centered = values - jnp.mean(values, axis=-1, keepdims=True)
    inverse = lax.rsqrt(jnp.mean(centered * centered, axis=-1, keepdims=True) + eps)
    standard = centered * inverse
    return (standard * gain_vec + shift_vec, standard, inverse)


def norm_back_plain(upstream, standard, inverse, gain_vec):
    scaled = upstream * gain_vec
    mean_term = jnp.mean(scaled, axis=-1, keepdims=True)
    proj_term = jnp.mean(scaled * standard, axis=-1, keepdims=True)
    return inverse * (scaled - mean_term - standard * proj_term)


def exact_gelu(values):
    return jax.nn.gelu(values, approximate=False)


def table_rows(pos_table, first_row, num_rows):
    table_len = pos_table.shape[0]
    grid_side = (table_len + 1) // 2
    query_row = first_row + lax.broadcasted_iota(jnp.int32, (num_rows, grid_side, table_len), 0)
    key_row = lax.broadcasted_iota(jnp.int32, (num_rows, grid_side, table_len), 1)
    entry_idx = lax.broadcasted_iota(jnp.int32, (num_rows, grid_side, table_len), 2)
    chooser = (query_row - key_row + grid_side - 1 == entry_idx).astype(jnp.float32)
    chooser = chooser.reshape(num_rows * grid_side, table_len)
    picked = jnp.dot(chooser, pos_table, precision=highest)
    return (picked.reshape(num_rows, grid_side, -1), chooser)


def rel_terms(query_f, row_first, rel_h, rel_w):
    grid_rows = query_f.shape[0] // G
    head_count = query_f.shape[1]
    near_h, pick_h = table_rows(rel_h, row_first, grid_rows)
    near_w, pick_w = table_rows(rel_w, 0, G)
    shaped = query_f.reshape(grid_rows, G, head_count, query_f.shape[2])
    term_h = jnp.einsum("awhc,akc->awhk", shaped, near_h, precision=highest)
    term_w = jnp.einsum("awhc,wkc->awhk", shaped, near_w, precision=highest)
    return (
        term_h.reshape(-1, head_count, G),
        term_w.reshape(-1, head_count, G),
        near_h,
        near_w,
        pick_h,
        pick_w,
    )


def piece_scores(query, key_h, term_h, term_w, factor):
    num_keys = key_h.shape[0]
    products = jnp.einsum("rhc,nhc->rhn", query, key_h, preferred_element_type=jnp.float32)
    position = (term_h[..., :, None] + term_w[..., None, :]).reshape(
        term_h.shape[0], term_h.shape[1], num_keys
    )
    return products * factor + position


def attend_step(running, pieces, offset, query, term_h, term_w, factor):
    run_max, run_sum, accumulated = running
    key_piece, value_piece = pieces
    num_keys = key_piece.shape[0]
    head_count = query.shape[1]
    key_h = key_piece.reshape(num_keys, head_count, -1)
    value_h = value_piece.reshape(num_keys, head_count, -1)
    scores = piece_scores(query, key_h, term_h, term_w, factor)
    new_max = jnp.maximum(run_max, jnp.max(scores, axis=-1))
    weights_p = jnp.exp(scores - new_max[..., None])
    run_sum = jnp.sum(weights_p, axis=-1)
    accumulated = jnp.einsum(
        "rhn,nhc->rhc", weights_p.astype(jnp.bfloat16), value_h, preferred_element_type=jnp.float32
    )
    return (new_max, run_sum, accumulated)


def grad_step(running, pieces, offset, query, out_grad, log_total, row_dot, term_h, term_w, factor):
    key_piece, value_piece = pieces
    num_keys = key_piece.shape[0]
    num_rows, head_count, head_size = query.shape
    key_h = key_piece.reshape(num_keys, head_count, head_size)
    value_h = value_piece.reshape(num_keys, head_count, head_size)
    scores = piece_scores(query, key_h, term_h, term_w, factor)
    weights_p = jnp.exp(scores - log_total[..., None])
    prob_grad = jnp.einsum("rhc,nhc->rhn", out_grad, value_h, preferred_element_type=jnp.float32)
    score_grad = (weights_p * (prob_grad - row_dot[..., None])).astype(jnp.bfloat16)
    query_acc = jnp.einsum("rhn,nhc->rhc", score_grad, key_h, preferred_element_type=jnp.float32)
    key_grad = (
        jnp.einsum("rhn,rhc->nhc", score_grad, query, preferred_element_type=jnp.float32) * factor
    )
    value_grad = jnp.einsum(
        "rhn,rhc->nhc", weights_p.astype(jnp.bfloat16), out_grad, preferred_element_type=jnp.float32
    )
    joined = jnp.concatenate(
        [key_grad.reshape(num_keys, -1), value_grad.reshape(num_keys, -1)], axis=1
    )
    grid_grad = score_grad.reshape(num_rows, head_count, num_keys // G, G)
    part_h = jnp.sum(grid_grad, axis=-1, dtype=jnp.float32)
    grad_w = jnp.sum(grid_grad, axis=-2, dtype=jnp.float32)
    return (query_acc, joined, part_h, grad_w)


def tensor_total(partial_sum):
    return lax.psum(partial_sum.astype(jnp.bfloat16), "tp").astype(jnp.float32)


def contract_last(left_mat, right_mat):
    return lax.dot_general(
        left_mat, right_mat, (((1,), (1,)), ((), ())), preferred_element_type=jnp.float32
    )


def micro_step(weights_full, picture, cotangent, params):
    (
        gain_one,
        shift_one,
        qv_shift,
        rel_h,
        rel_w,
        proj_shift,
        gain_two,
        shift_two,
        up_shift,
        down_shift,
    ) = params
    qkv_full, proj_full, up_full, down_full = weights_full
    rows_dev = picture.shape[0]
    half_width = qkv_full.shape[2]
    head_count = half_width // HD
    grid_rows = rows_dev // G
    row_first = lax.axis_index("ctx") * grid_rows
    factor = HD ** (-0.5)
    source = picture.astype(jnp.float32)
    normed_f, standard_one, inverse_one = layer_norm(source, gain_one, shift_one)
    normed = normed_f.astype(jnp.bfloat16)
    projected = jnp.einsum("rd,jde->jre", normed, qkv_full, preferred_element_type=jnp.float32)
    query_flat = (projected[0] + qv_shift[0]).astype(jnp.bfloat16)
    key_flat = projected[1].astype(jnp.bfloat16)
    value_flat = (projected[2] + qv_shift[1]).astype(jnp.bfloat16)
    query = query_flat.reshape(rows_dev, head_count, HD)
    query_f = query.astype(jnp.float32)
    term_h, term_w, near_h, near_w, pick_h, pick_w = rel_terms(query_f, row_first, rel_h, rel_w)
    start_state = (
        jnp.full((rows_dev, head_count), -1e30, jnp.float32),
        jnp.zeros((rows_dev, head_count), jnp.float32),
        jnp.zeros((rows_dev, head_count, HD), jnp.float32),
    )
    forward_fn = partial(attend_step, query=query, term_h=term_h, term_w=term_w, factor=factor)
    run_max, run_sum, accumulated = forward_fn(
        start_state,
        (
            lax.all_gather(key_flat, "ctx", axis=0, tiled=True),
            lax.all_gather(value_flat, "ctx", axis=0, tiled=True),
        ),
        jnp.int32(0),
    )
    attended = accumulated / run_sum[..., None]
    log_total = run_max + jnp.log(run_sum)
    mixed = attended.reshape(rows_dev, half_width).astype(jnp.bfloat16)
    middle = source + tensor_total(contract_last(mixed, proj_full)) + proj_shift
    normed2_f, standard_two, inverse_two = layer_norm(middle, gain_two, shift_two)
    normed2 = normed2_f.astype(jnp.bfloat16)
    hidden = jnp.dot(normed2, up_full, preferred_element_type=jnp.float32) + up_shift
    active, gelu_back = jax.vjp(exact_gelu, hidden)
    active_low = active.astype(jnp.bfloat16)
    result = (middle + tensor_total(contract_last(active_low, down_full)) + down_shift).astype(
        jnp.bfloat16
    )
    top_f = cotangent.astype(jnp.float32)
    down_grad = jnp.einsum("rd,rf->df", cotangent, active_low, preferred_element_type=jnp.float32)
    down_shift_grad = jnp.sum(top_f, axis=0)
    active_grad = jnp.dot(cotangent, down_full, preferred_element_type=jnp.float32)
    hidden_grad = gelu_back(active_grad)[0].astype(jnp.bfloat16)
    up_grad = jnp.einsum("rd,rf->df", normed2, hidden_grad, preferred_element_type=jnp.float32)
    up_shift_grad = jnp.sum(hidden_grad, axis=0, dtype=jnp.float32)
    normed2_grad = lax.psum(contract_last(hidden_grad, up_full).astype(jnp.bfloat16), "tp").astype(
        jnp.float32
    )
    middle_grad = top_f + norm_back_plain(normed2_grad, standard_two, inverse_two, gain_two)
    gain_two_grad = jnp.sum(normed2_grad * standard_two, axis=0)
    shift_two_grad = jnp.sum(normed2_grad, axis=0)
    branch_grad = middle_grad.astype(jnp.bfloat16)
    proj_grad = jnp.einsum("rd,re->de", branch_grad, mixed, preferred_element_type=jnp.float32)
    proj_shift_grad = jnp.sum(branch_grad, axis=0, dtype=jnp.float32)
    mixed_grad = (
        jnp.dot(branch_grad, proj_full, preferred_element_type=jnp.float32)
        .astype(jnp.bfloat16)
        .reshape(rows_dev, head_count, HD)
    )
    row_dot = jnp.sum(mixed_grad.astype(jnp.float32) * attended, axis=-1)
    ctx_count = lax.axis_size("ctx")
    start_back = (
        jnp.zeros((rows_dev, head_count, HD), jnp.float32),
        jnp.zeros((rows_dev * ctx_count, 2 * half_width), jnp.float32),
        jnp.zeros((rows_dev, head_count, G), jnp.float32),
        jnp.zeros((rows_dev, head_count, G), jnp.float32),
    )
    back_fn = partial(
        grad_step,
        query=query,
        out_grad=mixed_grad,
        log_total=log_total,
        row_dot=row_dot,
        term_h=term_h,
        term_w=term_w,
        factor=factor,
    )
    query_acc, key_value_acc, grad_h, grad_w = back_fn(
        start_back,
        (
            lax.all_gather(key_flat, "ctx", axis=0, tiled=True),
            lax.all_gather(value_flat, "ctx", axis=0, tiled=True),
        ),
        jnp.int32(0),
    )
    key_value_mine = lax.psum_scatter(
        key_value_acc.astype(jnp.bfloat16), "ctx", scatter_dimension=0, tiled=True
    ).astype(jnp.float32)
    grid_h = grad_h.reshape(grid_rows, G, head_count, G)
    grid_w = grad_w.reshape(grid_rows, G, head_count, G)
    shaped_q = query_f.reshape(grid_rows, G, head_count, HD)
    rel_query = jnp.einsum("awhk,akc->awhc", grid_h, near_h, precision=highest) + jnp.einsum(
        "awhk,wkc->awhc", grid_w, near_w, precision=highest
    )
    query_grad = (
        (query_acc * factor + rel_query.reshape(rows_dev, head_count, HD))
        .reshape(rows_dev, half_width)
        .astype(jnp.bfloat16)
    )
    key_grad = key_value_mine[:, :half_width].astype(jnp.bfloat16)
    value_grad = key_value_mine[:, half_width:].astype(jnp.bfloat16)
    table_h_part = jnp.dot(
        pick_h.T,
        jnp.einsum("awhk,awhc->akc", grid_h, shaped_q, precision=highest).reshape(-1, HD),
        precision=highest,
    )
    table_w_part = jnp.dot(
        pick_w.T,
        jnp.einsum("awhk,awhc->wkc", grid_w, shaped_q, precision=highest).reshape(-1, HD),
        precision=highest,
    )
    stacked = jnp.stack([query_grad, key_grad, value_grad])
    qkv_grad = jnp.einsum("rd,jre->jde", normed, stacked, preferred_element_type=jnp.float32)
    qv_shift_grad = jnp.stack(
        [
            jnp.sum(query_grad, axis=0, dtype=jnp.float32),
            jnp.sum(value_grad, axis=0, dtype=jnp.float32),
        ]
    )
    normed_part = jnp.einsum("jre,jde->rd", stacked, qkv_full, preferred_element_type=jnp.float32)
    normed_grad, table_h_grad, table_w_grad = (
        lax.psum(normed_part.astype(jnp.bfloat16), "tp").astype(jnp.float32),
        lax.psum(table_h_part.astype(jnp.bfloat16), "tp").astype(jnp.float32),
        lax.psum(table_w_part.astype(jnp.bfloat16), "tp").astype(jnp.float32),
    )
    input_grad = (middle_grad + norm_back_plain(normed_grad, standard_one, inverse_one, gain_one)).astype(
        jnp.bfloat16
    )
    gain_one_grad = jnp.sum(normed_grad * standard_one, axis=0)
    shift_one_grad = jnp.sum(normed_grad, axis=0)
    big_grads = (qkv_grad, proj_grad, up_grad, down_grad)
    small_grads = (
        gain_one_grad,
        shift_one_grad,
        qv_shift_grad,
        table_h_grad,
        table_w_grad,
        proj_shift_grad,
        gain_two_grad,
        shift_two_grad,
        up_shift_grad,
        down_shift_grad,
    )
    return (result, input_grad, big_grads, small_grads)


def add_trees(first_tree, second_tree):
    return jax.tree.map(lambda first_v, second_v: first_v + second_v, first_tree, second_tree)


def zeros_like_tree(tree):
    return jax.tree.map(lambda member: jnp.zeros(member.shape, jnp.float32), tree)


def local(
    images,
    norm1_gain,
    norm1_bias,
    qkv_weight,
    qv_bias,
    rel_pos_h,
    rel_pos_w,
    proj_weight,
    proj_bias,
    norm2_gain,
    norm2_bias,
    up_weight,
    up_bias,
    down_weight,
    down_bias,
    out_cotangent,
):
    params = tuple(
        (
            member.astype(jnp.float32)
            for member in (
                norm1_gain,
                norm1_bias,
                qv_bias,
                rel_pos_h,
                rel_pos_w,
                proj_bias,
                norm2_gain,
                norm2_bias,
                up_bias,
                down_bias,
            )
        )
    )
    small_start = zeros_like_tree(params)

    def per_batch(totals, pair):
        weights_full = (
            lax.all_gather(qkv_weight, ("fsdp", "ctx"), axis=1, tiled=True),
            lax.all_gather(proj_weight, ("fsdp", "ctx"), axis=0, tiled=True),
            lax.all_gather(up_weight, ("fsdp", "ctx"), axis=0, tiled=True),
            lax.all_gather(down_weight, ("fsdp", "ctx"), axis=0, tiled=True),
        )
        result, input_grad, big_grads, small_grads = micro_step(
            weights_full, pair[0], pair[1], params
        )
        shards = (
            lax.psum_scatter(big_grads[0], ("fsdp", "ctx"), scatter_dimension=1, tiled=True),
            lax.psum_scatter(big_grads[1], ("fsdp", "ctx"), scatter_dimension=0, tiled=True),
            lax.psum_scatter(big_grads[2], ("fsdp", "ctx"), scatter_dimension=0, tiled=True),
            lax.psum_scatter(big_grads[3], ("fsdp", "ctx"), scatter_dimension=0, tiled=True),
        )
        return (add_trees(totals, (shards, small_grads)), (result, input_grad))

    shard_start = zeros_like_tree((qkv_weight, proj_weight, up_weight, down_weight))
    (shard_totals, small_totals), (outputs, input_grads) = lax.scan(
        per_batch, (shard_start, small_start), (images, out_cotangent)
    )
    small_final = lax.psum(small_totals, ("fsdp", "ctx"))
    return (
        outputs,
        input_grads,
        small_final[0],
        small_final[1],
        shard_totals[0],
        small_final[2],
        small_final[3],
        small_final[4],
        shard_totals[1],
        small_final[5],
        small_final[6],
        small_final[7],
        shard_totals[2],
        small_final[8],
        shard_totals[3],
        small_final[9],
    )


def solution(mesh):
    shape = dict(mesh.shape)
    body = partial(grouped, shape) if shape == {"fsdp": 4, "ctx": 4, "tp": 2} else local
    placed = (
        P("fsdp", "ctx", None),
        P(),
        P(),
        P(None, ("fsdp", "ctx"), "tp"),
        P(None, "tp"),
        P(),
        P(),
        P(("fsdp", "ctx"), "tp"),
        P(),
        P(),
        P(),
        P(("fsdp", "ctx"), "tp"),
        P("tp"),
        P(("fsdp", "ctx"), "tp"),
        P(),
        P("fsdp", "ctx", None),
    )
    return jax.shard_map(
        body,
        mesh=mesh,
        in_specs=placed,
        out_specs=(
            P("fsdp", "ctx", None),
            P("fsdp", "ctx", None),
            P(),
            P(),
            P(None, ("fsdp", "ctx"), "tp"),
            P(None, "tp"),
            P(),
            P(),
            P(("fsdp", "ctx"), "tp"),
            P(),
            P(),
            P(),
            P(("fsdp", "ctx"), "tp"),
            P("tp"),
            P(("fsdp", "ctx"), "tp"),
            P(),
        ),
        check_vma=False,
    )
```

```python
from functools import partial

import jax
import jax.numpy as jnp
import ml_dtypes
import numpy as np
from jax import lax
from jax.experimental import pallas as pl
from jax.experimental.pallas import tpu as pltpu
from jax.sharding import PartitionSpec as P

G = 48
HD = 64


eps = 1e-06
highest = lax.Precision.HIGHEST
bf16, f32 = jnp.bfloat16, jnp.float32
VMEM_BYTES = 56 * 1024 * 1024
NN = (((1,), (0,)), ((), ()))
NT = (((1,), (1,)), ((), ()))
TN = (((0,), (0,)), ((), ()))
LH, LW = 64, 112
ANY = pl.BlockSpec(memory_space=pl.ANY)
PEAK = 5.0e15


def mm(a, b, dims=NN):
    return lax.dot_general(a, b, dims, preferred_element_type=f32)


def roll(x, shift, stride=None):
    extra = {} if stride is None else dict(stride=stride, stride_axis=0)
    return pltpu.roll(x, shift, 1, **extra)


def lane_iota(shape):
    return lax.broadcasted_iota(jnp.int32, shape, 1)


def struct(shape, dtype=bf16):
    return jax.ShapeDtypeStruct(shape, dtype)


def whole(shape):
    return pl.BlockSpec(shape, lambda *_: (0,) * len(shape))


def call(kernel, name, us, grid, prefetch, ins, in_specs, outs, out_specs, scratch=(), aliases=None):
    return pl.pallas_call(
        kernel,
        out_shape=outs,
        grid_spec=pltpu.PrefetchScalarGridSpec(
            num_scalar_prefetch=1, grid=grid, in_specs=in_specs, out_specs=out_specs, scratch_shapes=list(scratch)
        ),
        input_output_aliases=aliases or {},
        compiler_params=pltpu.CompilerParams(vmem_limit_bytes=VMEM_BYTES),
        cost_estimate=pl.CostEstimate(flops=int(us * 1e-6 * PEAK), bytes_accessed=0, transcendentals=0),
        name=name,
    )(prefetch, *ins)


def columns(w_ref, side):
    width = w_ref.shape[2] // 2
    parts = [jnp.where(side == 0, w_ref[j, :, :width], w_ref[j, :, width:]) for j in range(3)]
    return jnp.concatenate([p[:, :128] for p in parts] + [p[:, 128:] for p in parts], axis=1)


def pack_kernel(at_ref, image_ref, w_ref, out_ref):
    rows = image_ref.shape[1]
    depth = w_ref.shape[1]
    out_ref[:rows] = image_ref[0]
    out_ref[rows:] = jnp.zeros((depth, out_ref.shape[1]), bf16)
    out_ref[rows:, :576] = columns(w_ref, 1 - at_ref[0])


def pack(at, images, w):
    batch, quarter, d = images.shape
    rows = quarter // 2
    out = (rows + w.shape[1], d)
    return call(
        pack_kernel, "pack", 2, (1,), at, [images, w],
        [pl.BlockSpec((1, rows, d), lambda i, o: (o[1], 1 - o[0], 0)), whole(w.shape)], struct(out), whole(out),
    )


def route_kernel(at_ref, image_ref, got_ref, w_ref, ub_ref, qvb_ref, gain_ref, bias_ref, near_ref, normed_ref, w_out_ref):
    rows = image_ref.shape[1]
    depth = w_ref.shape[1]
    same = at_ref[0] == at_ref[2]
    own, got = image_ref[0], got_ref[:rows]
    near = jnp.where(same, own, got)
    near_ref[...] = near
    normed_ref[...] = norm(near.astype(f32), gain_ref[...], bias_ref[...])[0].astype(bf16)
    w_out_ref[...] = jnp.zeros(w_out_ref.shape, bf16)
    w_out_ref[:depth, :576] = columns(w_ref, at_ref[0])
    w_out_ref[depth:2 * depth] = got_ref[rows:]
    d = image_ref.shape[2]
    w_out_ref[2 * depth:2 * depth + 1] = ub_ref[:, :d]
    w_out_ref[2 * depth + 1:2 * depth + 2] = ub_ref[:, d:]
    w_out_ref[2 * depth + 2:2 * depth + 3] = qvb_ref[...]


def route(at, images, got, w, up_bias, qv_bias, gain, bias):
    batch, quarter, d = images.shape
    rows = quarter // 2
    half = (rows, d)
    out = (2 * w.shape[1] + 16, d)
    return call(
        route_kernel, "route", 3, (1,), at, [images, got, w, up_bias, qv_bias, gain, bias],
        [pl.BlockSpec((1, rows, d), lambda i, o: (o[1], o[0], 0))] + [whole(v.shape) for v in (got, w, up_bias, qv_bias, gain, bias)],
        (struct(half), struct(half), struct(out)), [whole(half)] * 2 + [whole(out)],
    )


def far_kernel(at_ref, a_ref, b_ref, gain_ref, bias_ref, *refs):
    far_ref, out_ref = refs[-2:]
    far = jnp.where(at_ref[0] == at_ref[2], a_ref[...], b_ref[...])
    far_ref[...] = far
    out_ref[...] = norm(far.astype(f32), gain_ref[...], bias_ref[...])[0].astype(bf16)


def take_far(at, a, b, gain, bias, after):
    return call(
        far_kernel, "take_far", 2, (1,), at, [a, b, gain, bias] + after, [whole(v.shape) for v in (a, b, gain, bias)] + [ANY] * len(after),
        (struct(a.shape), struct(a.shape)), [whole(a.shape)] * 2,
    )


def arrange_kernel(me_ref, *refs):
    pieces, out_ref = refs[:-1], refs[-1]
    depth = pieces[0].shape[0] // 2
    out_ref[:, 576:] = jnp.zeros((out_ref.shape[0], 64), bf16)
    for dx in range(2):
        for dz in range(4):
            for dc in range(2):
                ref, lo = (pieces[dz], dc) if dx == 0 else (pieces[4], dz * 2 + dc)
                at = (dx * 8 + dc * 4 + dz) ^ me_ref[0]
                out_ref[pl.ds(pl.multiple_of(at * depth, 16), depth), :576] = ref[lo * depth:(lo + 1) * depth]


def arrange(me, pieces, rows):
    return call(
        arrange_kernel, "arrange", 2, (1,), me, pieces, [whole(p.shape) for p in pieces],
        struct((rows, 640)), whole((rows, 640)),
    )


def prep_kernel(order_ref, *refs):
    xs, refs = refs[:4], refs[4:]
    w_ref, b_ref, tab_ref, hot_ref = refs[:4]
    q_ref, k_ref, v_ref, n_ref = refs[-4:]
    step = pl.program_id(0)
    rows = q_ref.shape[1]

    def work(x):
        first_row = order_ref[4 + step]
        n_ref[...] = x
        qkv = (mm(x, w_ref[...]) + b_ref[...]).astype(bf16).astype(f32)
        lane = lane_iota((G, 128))
        lane_all = lane_iota((rows, 128))
        hot_a = hot_ref[0, :, :128].astype(f32)
        hot_b = hot_ref[0, :, 128:]
        cols = [qkv[:, i * 128:(i + 1) * 128] for i in range(5)]
        back = [roll(v, 64) for v in cols[:4]]
        for h, (q, k, v) in enumerate(
            ((cols[0], cols[1], cols[2]), (back[0], back[1], back[2]), (cols[3], back[3], cols[4]))
        ):
            k_ref[h, :, :128] = jnp.where(lane_all < 64, k, hot_a).astype(bf16)
            k_ref[h, :, 128:] = hot_b
            v_ref[h] = jnp.where(lane_all < 64, v, jnp.where(lane_all < 67, 1.0, 0.0)).astype(bf16)
            turned = mm(q.astype(bf16), tab_ref[...])
            qf = q * (HD ** -0.5)
            for g in range(rows // G):
                r = first_row + g
                along_h = turned[g * G:(g + 1) * G, :128]
                along_w = turned[g * G:(g + 1) * G, 128:]
                h_a = roll(along_h, (LH - (G - 1) + 128 + r) % 128)
                h_b = roll(along_h, (32 - (G - 1) + 128 + r) % 128)
                w_a = roll(along_w, (LW - (G - 1)) % 128, 1)
                w_b = roll(along_w, (80 - (G - 1)) % 128, 1)
                h_lo = h_b - h_b.astype(bf16).astype(f32)
                w_lo = w_b - w_b.astype(bf16).astype(f32)
                first = jnp.where(lane < LH, qf[g * G:(g + 1) * G], jnp.where(lane < LW, h_a, w_a))
                second = jnp.where(lane < 32, w_a, jnp.where(lane < 80, h_lo, w_lo))
                q_ref[h, g * G:(g + 1) * G, :128] = first.astype(bf16)
                q_ref[h, g * G:(g + 1) * G, 128:] = second.astype(bf16)

    for k in range(4):
        @pl.when(step == k)
        def _(k=k):
            work(xs[k][...])


def prep(order, xs, w, b, tab, hot, heads, before, group):
    rows, d = xs[0].shape
    tokens = len(xs) * 2 * rows
    outs = (struct((heads, tokens, 256)), struct((heads, tokens, 256)), struct((heads, tokens, 128)), struct((tokens, d)))
    return call(
        prep_kernel, "prep", 7, (len(xs),), order, list(xs) + [w, b, tab, hot] + list(before),
        [whole(x.shape) for x in xs] + [whole(w.shape), whole(b.shape), whole(tab.shape)]
        + [pl.BlockSpec((1, rows, 256), lambda i, o: (o[i], 0, 0))] + [ANY] * len(before),
        outs,
        [
            pl.BlockSpec((heads, rows, 256), lambda i, o: (0, 2 * i + group, 0)),
            pl.BlockSpec((heads, rows, 256), lambda i, o: (0, 2 * i + group, 0)),
            pl.BlockSpec((heads, rows, 128), lambda i, o: (0, 2 * i + group, 0)),
            pl.BlockSpec((rows, d), lambda i, o: (2 * i + group, 0)),
        ],
        aliases={9 + i: i for i in range(len(before))},
    )


def attend_kernel(order_ref, q_ref, k_ref, v_ref, *refs, tiles):
    att_ref, q2_ref, mix_ref = refs[-3:]
    head = pl.program_id(0)
    start = 0
    for tile in tiles:
        at = pl.ds(start, tile)
        start += tile
        lane = lane_iota((tile, 128))
        q = q_ref[0, at, :]
        s = mm(q, k_ref[0], NT)
        m = jnp.max(s, axis=1, keepdims=True)
        p = jnp.exp(s - m)
        o = mm(p.astype(bf16), v_ref[0])
        total = o[:, 64:65]
        att = o / total
        lse = m + jnp.log(total)
        att_ref[0, at, :] = att
        low_att = att[:, :64].astype(bf16)
        for h in range(3):
            @pl.when(head == h)
            def _(h=h):
                mix_ref[at, h * 64:(h + 1) * 64] = low_att
        a = q[:, :128].astype(f32)
        b = q[:, 128:].astype(f32)
        full = a + roll(b, 32) - lse
        high = full.astype(bf16)
        low = roll(full - high.astype(f32), 96)
        q2_ref[0, at, :128] = jnp.where((lane >= LH) & (lane < LW), high.astype(f32), a).astype(bf16)
        q2_ref[0, at, 128:] = jnp.where((lane >= 32) & (lane < 80), low, b).astype(bf16)


def attend(q, k, v, side):
    heads, tokens, _ = q.shape
    rows = tokens // 2
    tiles = (256,) * (rows // 256) + ((rows % 256,) if rows % 256 else ())
    return call(
        partial(attend_kernel, tiles=tiles), "attend", 19, (heads,), jnp.zeros((1,), jnp.int32), [q, k, v],
        [
            pl.BlockSpec((1, rows, 256), lambda h, o: (h, side, 0)),
            pl.BlockSpec((1, tokens, 256), lambda h, o: (h, 0, 0)),
            pl.BlockSpec((1, tokens, 128), lambda h, o: (h, 0, 0)),
        ],
        (struct((heads, rows, 128), f32), struct((heads, rows, 256)), struct((rows, heads * HD))),
        [pl.BlockSpec((1, rows, 128), lambda h, o: (h, 0, 0)), pl.BlockSpec((1, rows, 256), lambda h, o: (h, 0, 0)), whole((rows, heads * HD))],
    )


def back_kernel(order_ref, qa_ref, qb_ref, k_ref, v_ref, atta_ref, attb_ref, own_ref, beside_ref, core_ref, tab_ref, turn_ref,
                d_ref, table_ref, q_ref, go_ref, kt_ref, acc_ref, hi_ref, lo_ref, *, tile, sets, first, count):
    head, step = pl.program_id(0), pl.program_id(1)
    last = pl.num_programs(1) - 1
    tokens = k_ref.shape[1]
    rows = tokens // sets
    wide = count * 64

    @pl.when(step == 0)
    def _():
        lane = lane_iota((rows, 128))
        for n, (ref, from_row) in enumerate(((own_ref, 0), (core_ref, 0), (beside_ref, 0), (core_ref, rows))):
            at = pl.ds(n * rows, rows)
            for h in range(count):
                @pl.when(head == h)
                def _(ref=ref, at=at, h=h, from_row=from_row):
                    lo = (first + h) * 64
                    go_ref[at, :64] = ref[from_row:from_row + rows, lo:lo + 64]
        go = go_ref[...].astype(f32)
        lane = lane_iota(go.shape)
        go = jnp.where(lane < 64, go, 0.0)
        att = jnp.concatenate([atta_ref[0], attb_ref[0]], axis=0)
        q_ref[:tokens // 2] = qa_ref[0]
        q_ref[tokens // 2:] = qb_ref[0]
        dot = jnp.sum(jnp.where(lane < 64, go * att, 0.0), axis=1, keepdims=True)
        high = dot.astype(bf16).astype(f32)
        mid = (dot - high).astype(bf16).astype(f32)
        low = dot - high - mid
        go_ref[...] = jnp.where(lane < 64, go, jnp.where(lane == 64, -high, jnp.where(lane == 65, -mid, jnp.where(lane == 66, -low, 0.0)))).astype(bf16)
        acc_ref[...] = jnp.zeros_like(acc_ref)
        kt_ref[:LW] = k_ref[0, :, :128].T[:LW]
        kt_ref[LW:] = turn_ref[...]

    keys = tokens // pl.num_programs(1)
    for i in range(keys // tile):
        at = pl.ds(pl.multiple_of(step * keys + i * tile, tile), tile)
        s = mm(k_ref[0, at, :], q_ref[...], NT)
        p = jnp.exp(s)
        pb = p.astype(bf16)
        d = (p * mm(v_ref[0, at, :], go_ref[...], NT)).astype(bf16)
        dv = mm(pb, go_ref[...]).astype(bf16)
        dk = mm(d, q_ref[:, :128]).astype(bf16)
        for h in range(count):
            @pl.when(head == h)
            def _(h=h):
                d_ref[at, 2 * wide + h * 64:2 * wide + (h + 1) * 64] = dv[:, :64]
                d_ref[at, wide + h * 64:wide + (h + 1) * 64] = dk[:, :64]
        acc_ref[...] += mm(kt_ref[:, at], d)

    @pl.when(step == last)
    def _():
        small = lane_iota((G, 128))
        a = acc_ref[:128].T
        b = jnp.concatenate([acc_ref[128:160], jnp.zeros((96, tokens), f32)], axis=0).T
        for g in range(tokens // G):
            block, inner = divmod(g, rows // 2 // G)
            r = order_ref[block] + inner
            ag = a[g * G:(g + 1) * G]
            bg = b[g * G:(g + 1) * G]
            along_h = jnp.where((small >= LH) & (small < LW), ag, 0.0)
            along_w = jnp.where(small >= LW, ag, jnp.where(small < 32, bg, 0.0))
            along_h = roll(along_h, (256 + G - 1 - LH - r) % 128)
            along_w = roll(along_w, (128 - LW) % 128, 1)
            h_hi = along_h.astype(bf16)
            w_hi = along_w.astype(bf16)
            hi_ref[g * G:(g + 1) * G, :128] = h_hi
            hi_ref[g * G:(g + 1) * G, 128:] = w_hi
            lo_ref[g * G:(g + 1) * G, :128] = (along_h - h_hi.astype(f32)).astype(bf16)
            lo_ref[g * G:(g + 1) * G, 128:] = (along_w - w_hi.astype(f32)).astype(bf16)
        turned = mm(hi_ref[...], tab_ref[...], NT) + mm(lo_ref[...], tab_ref[...], NT)
        dq = (a * (HD ** -0.5) + turned).astype(bf16)
        for h in range(count):
            @pl.when(head == h)
            def _(h=h):
                d_ref[:, h * 64:(h + 1) * 64] = dq[:, :64]
        tables = mm(hi_ref[...], q_ref[:, :128], TN)

        @pl.when(head == 0)
        def _():
            table_ref[...] = tables

        @pl.when(head > 0)
        def _():
            table_ref[...] += tables


def attend_back(order, q2, k, v, att, grads, tab, turn, first, count, steps, tile, sets):
    _, tokens, _ = k.shape
    at = lambda h, i, o: (first + h, 0, 0)
    wide = 3 * count * HD
    per_head = lambda a: pl.BlockSpec((1,) + a.shape[1:], at)
    return call(
        partial(back_kernel, tile=tile, sets=sets, first=first, count=count), "attend_back", 21 * count,
        (count, steps), order, list(q2) + [k, v] + list(att) + list(grads) + [tab, turn],
        [per_head(a) for a in list(q2) + [k, v] + list(att)] + [whole(g.shape) for g in grads] + [whole(tab.shape), whole(turn.shape)],
        (struct((tokens, wide)), struct((256, 128), f32)),
        [whole((tokens, wide)), whole((256, 128))],
        [
            pltpu.VMEM((tokens, 256), bf16),
            pltpu.VMEM((tokens, 128), bf16),
            pltpu.VMEM((160, tokens), bf16),
            pltpu.VMEM((160, tokens), f32),
            pltpu.VMEM((tokens, 256), bf16),
            pltpu.VMEM((tokens, 256), bf16),
        ],
    )


def norm(v, gain, bias):
    mean = jnp.mean(v, axis=1, keepdims=True)
    centered = v - mean
    inverse = lax.rsqrt(jnp.mean(centered * centered, axis=1, keepdims=True) + eps)
    unit = centered * inverse
    return unit * gain + bias, unit, inverse


def norm_back(upstream, unit, inverse, gain):
    scaled = upstream * gain
    return inverse * (scaled - jnp.mean(scaled, axis=1, keepdims=True) - unit * jnp.mean(scaled * unit, axis=1, keepdims=True))


def mlp_kernel(order_ref, near_ref, beside_ref, core_ref, src0, src1, top0, top1, up_ref, down_ref, proj_ref, ub_ref, vec_ref,
               out0, out1, act_ref, hg_ref, n2_ref, mg_ref, br_ref, mix_ref, back_ref, ubg_ref, vg_ref,
               mid_ref, unit_ref, inv_ref, acc_ref, ng_ref, quad_ref, top_ref):
    step = pl.program_id(0)
    last = pl.num_programs(0) - 1
    part, d = src0.shape
    half = proj_ref.shape[3]
    width = near_ref.shape[1]

    def proj(i):
        return proj_ref[:, i].reshape(d, half)

    @pl.when(step == 0)
    def _():
        rows = near_ref.shape[0] // 2
        for k, piece in enumerate((near_ref[:rows], core_ref[:rows], beside_ref[:rows], core_ref[rows:])):
            quad_ref[order_ref[k]] = piece
        for i in range(4):
            mix_ref[:, i * width:(i + 1) * width] = quad_ref[i]
        top_ref[:part] = top0[...]
        top_ref[part:] = top1[...]
        mid = jnp.concatenate([src0[...], src1[...]], axis=0).astype(f32) + vec_ref[0:1] + mm(mix_ref[:, :half], proj(0), NT) + mm(mix_ref[:, half:], proj(1), NT)
        normed, unit, inverse = norm(mid, vec_ref[1:2], vec_ref[2:3])
        mid_ref[...] = mid
        unit_ref[...] = unit
        inv_ref[...] = inverse
        n2_ref[...] = normed.astype(bf16)

    tile = up_ref.shape[3]
    up = up_ref[:, 0].reshape(d, tile)
    down = down_ref[:, 0].reshape(d, tile)
    hidden = mm(n2_ref[...], up) + ub_ref[...]
    phi_all = 0.5 + 0.5 * lax.erf(hidden * (0.5 ** 0.5))
    slope = phi_all + hidden * (jnp.exp(-0.5 * hidden * hidden) * 0.3989422804014327)
    active = (hidden * phi_all).astype(bf16)
    hg = (mm(top_ref[...], down) * slope).astype(bf16)
    act_ref[...] = active
    hg_ref[...] = hg
    ubg_ref[...] = jnp.sum(hg.astype(f32), axis=0, keepdims=True)
    out = mm(active, down, NT)
    ng = mm(hg, up, NT)

    @pl.when(step == 0)
    def _():
        acc_ref[...] = out
        ng_ref[...] = ng

    @pl.when(step > 0)
    def _():
        acc_ref[...] += out
        ng_ref[...] += ng

    @pl.when(step == last)
    def _():
        top = top_ref[...].astype(f32)
        grad = ng_ref[...]
        unit = unit_ref[...]
        out = (mid_ref[...] + acc_ref[...] + vec_ref[3:4]).astype(bf16)
        out0[...] = out[:part]
        out1[...] = out[part:]
        middle = top + norm_back(grad, unit, inv_ref[...], vec_ref[1:2])
        branch = middle.astype(bf16)
        mg_ref[...] = middle
        br_ref[...] = branch
        for i in range(2):
            piece = mm(branch, proj(i)).astype(bf16)
            quad_ref[2 * i] = piece[:, :width]
            quad_ref[2 * i + 1] = piece[:, width:]
        for k in range(4):
            back_ref[k] = quad_ref[order_ref[k]]
        vg_ref[0:1] = jnp.sum(branch.astype(f32), axis=0, keepdims=True)
        vg_ref[1:2] = jnp.sum(grad * unit, axis=0, keepdims=True)
        vg_ref[2:3] = jnp.sum(grad, axis=0, keepdims=True)
        vg_ref[3:4] = jnp.sum(top, axis=0, keepdims=True)


def mlp(order, mixed, src, top, packed, up_bias, vecs, half_ff, tile):
    part, d = src[0].shape
    rows = 2 * part
    blocks, halves, depth, _ = packed.shape
    per = half_ff // tile
    half = d // halves
    quad = (4, rows, mixed[0].shape[1])
    ff = halves * half_ff
    by_tile = pl.BlockSpec((rows, tile), lambda i, o: (0, i))
    row_tile = pl.BlockSpec((1, tile), lambda i, o: (0, i))
    full = whole((rows, d))
    piece = whole((part, d))
    return call(
        mlp_kernel, "mlp", 24, (halves * per,), order,
        list(mixed) + list(src) + list(top) + [packed, packed, packed, up_bias, vecs],
        [whole(m.shape) for m in mixed] + [
            piece, piece, piece, piece,
            pl.BlockSpec((blocks, 1, depth, tile), lambda i, o: (0, i // per, 0, i % per)),
            pl.BlockSpec((blocks, 1, depth, tile), lambda i, o: (0, i // per, 0, per + i % per)),
            pl.BlockSpec((blocks, halves, depth, half), lambda i, o: (0, 0, 0, 2 * half_ff // half)),
            row_tile, whole(vecs.shape),
        ],
        (struct((part, d)), struct((part, d)), struct((rows, ff)), struct((rows, ff)), struct((rows, d)), struct((rows, d), f32), struct((rows, d)), struct((rows, d)))
        + (struct(quad),) + (struct((1, ff), f32), struct((4, d), f32)),
        [piece, piece, by_tile, by_tile, full, full, full, full] + [whole(quad)] + [row_tile, whole((4, d))],
        [
            pltpu.VMEM((rows, d), f32),
            pltpu.VMEM((rows, d), f32),
            pltpu.VMEM((rows, 1), f32),
            pltpu.VMEM((rows, d), f32),
            pltpu.VMEM((rows, d), f32),
            pltpu.VMEM(quad, bf16),
            pltpu.VMEM((rows, d), bf16),
        ],
    )


def wgrad_kernel(_, n2_ref, top0, top1, br_ref, hg_ref, act_ref, mix_ref, out_ref, left_ref):
    half, third = pl.program_id(0), pl.program_id(1)
    blocks, depth, tile = out_ref.shape

    @pl.when((half == 0) & (third == 0))
    def _():
        left_ref[0] = n2_ref[...].T
        left_ref[1] = jnp.concatenate([top0[...], top1[...]], axis=0).T
        left_ref[2] = br_ref[...].T

    at = 0
    for i, ref in enumerate((hg_ref, act_ref, mix_ref)):
        width = ref.shape[1]
        for k in range(3):
            lo, hi = max(at, k * tile), min(at + width, (k + 1) * tile)
            if lo < hi:
                @pl.when(third == k)
                def _(i=i, k=k, ref=ref, lo=lo, hi=hi, at=at):
                    part = mm(left_ref[i], ref[:, lo - at:hi - at]).astype(bf16)
                    out_ref[:, :, lo - k * tile:hi - k * tile] = part.reshape(blocks, depth, hi - lo)
        at += width


def wgrad(n2, top, branch, hg, active, mixed, blocks, halves):
    rows, d = n2.shape
    half_ff, half = hg.shape[1] // halves, d // halves
    depth = d // blocks
    total = 2 * half_ff + half
    by_half = lambda n: pl.BlockSpec((rows, n), lambda s, j, o: (0, s))
    return call(
        wgrad_kernel, "wgrad", 18, (halves, 3), jnp.zeros((1,), jnp.int32),
        [n2, top[0], top[1], branch, hg, active, mixed],
        [whole((rows, d)), whole(top[0].shape), whole(top[1].shape), whole((rows, d)), by_half(half_ff), by_half(half_ff), by_half(half)],
        struct((blocks, depth, halves * total)),
        pl.BlockSpec((blocks, depth, total // 3), lambda s, j, o: (0, 0, 3 * s + j)),
        [pltpu.VMEM((3, d, rows), bf16)],
    )


def down_kernel(_, a_ref, b_ref, w_ref, ng_ref):
    both = jnp.concatenate([a_ref[...], b_ref[...]], axis=1)
    ng_ref[0] = mm(both, w_ref[:, :both.shape[1]], NT).astype(bf16)


def grad_down(sets, grads, w, rows):
    d = w.shape[0]
    return call(
        down_kernel, "grad_down", 4, (2,), jnp.zeros((1,), jnp.int32), list(grads) + [w],
        [pl.BlockSpec((rows, g.shape[1]), lambda i, o: (2 * i + sets, 0)) for g in grads] + [whole(w.shape)],
        struct((2, rows, d)), pl.BlockSpec((1, rows, d), lambda i, o: (i, 0, 0)),
    )


def qkv_grad_kernel(_, x_ref, a_ref, b_ref, w_ref, wg_ref, bg_ref, ng_ref, acc_ref):
    step = pl.program_id(0)
    width = wg_ref.shape[-1]
    both = jnp.concatenate([a_ref[...], b_ref[...]], axis=1)
    add = mm(x_ref[...].T, both)
    sums = jnp.sum(both.astype(f32), axis=0, keepdims=True)

    @pl.when(step == 0)
    def _():
        acc_ref[...] = add
        bg_ref[...] = sums

    @pl.when(step > 0)
    def _():
        acc_ref[...] += add
        bg_ref[...] += sums

    @pl.when(step == pl.num_programs(0) - 1)
    def _():
        full = acc_ref[...]
        wg_ref[...] = full.astype(bf16).reshape(wg_ref.shape)
        w = w_ref[:, :width].astype(f32)
        lane = lane_iota(ng_ref.shape)
        a = jnp.sum(full * w, axis=1, keepdims=True)
        b = jnp.sum(bg_ref[...] * w, axis=1, keepdims=True)
        ng_ref[...] = jnp.where(lane == 0, a, jnp.where(lane == 1, b, 0.0))


def qkv_grad(x, grads, w, steps, blocks):
    tokens, d = x.shape
    rows = tokens // steps
    width = sum(g.shape[1] for g in grads)
    by_rows = lambda n: pl.BlockSpec((rows, n), lambda i, o: (i, 0))
    return call(
        qkv_grad_kernel, "qkv_grad", 5, (steps,), jnp.zeros((1,), jnp.int32), [x] + list(grads) + [w],
        [by_rows(d)] + [by_rows(g.shape[1]) for g in grads] + [whole(w.shape)],
        (struct((blocks, d // blocks, width)), struct((1, width), f32), struct((d, 128), f32)),
        [whole((blocks, d // blocks, width)), whole((1, width)), whole((d, 128))],
        [pltpu.VMEM((d, width), f32)],
    )


def finish_kernel(_, kept_ref, got_ref, passed_ref, middle_ref, src_ref, gain_ref, *refs):
    out_ref = refs[-1]
    grad = kept_ref[0].astype(f32) + got_ref[0].astype(f32) + passed_ref[...].astype(f32)
    _, unit, inverse = norm(src_ref[...].astype(f32), 1.0, 0.0)
    out_ref[...] = (middle_ref[...] + norm_back(grad, unit, inverse, gain_ref[...])).astype(bf16)


def finish(at, kept, got, passed, middle, src, gain, group, after=()):
    part, d = src.shape
    first = pl.BlockSpec((1, part, d), lambda i, o: (0, group, 0))
    return call(
        finish_kernel, "finish", 0.1, (1,), at, [kept, got, passed, middle, src, gain, *after],
        [first, first, whole((part, d)), pl.BlockSpec((part, d), lambda i, o: (group, 0)), whole((part, d)), whole(gain.shape)] + [ANY] * len(after),
        struct((part, d)), whole((part, d)),
    )


def assemble_kernel(at_ref, own_ref, other_ref, home_ref, home_other_ref, got_ref, out_ref):
    part = own_ref.shape[0]
    mine = pl.ds(pl.multiple_of(at_ref[0] * part, 16), part)
    other = pl.ds(pl.multiple_of((1 - at_ref[0]) * part, 16), part)
    same = at_ref[0] == at_ref[2]
    out_ref[at_ref[1], mine] = jnp.where(same, own_ref[...], home_ref[...])
    out_ref[1 - at_ref[1], mine] = jnp.where(same, other_ref[...], home_other_ref[...])
    out_ref[at_ref[1], other] = got_ref[0]
    out_ref[1 - at_ref[1], other] = got_ref[1]


def assemble(place, own, own_other, home, home_other, got):
    part, d = own.shape
    ins = [own, own_other, home, home_other, got]
    return call(
        assemble_kernel, "assemble", 0.1, (1,), place, ins, [whole(v.shape) for v in ins],
        struct((2, 2 * part, d)), whole((2, 2 * part, d)),
    )


AXES = ("fsdp", "ctx", "tp")


def pairs_of(shape, move):
    nf, nc, nt = shape["fsdp"], shape["ctx"], shape["tp"]
    flat = lambda f, z, t: (f * nc + z) * nt + t
    return [(flat(f, z, t), flat(*move(f, z, t))) for f in range(nf) for z in range(nc) for t in range(nt)]


def grouped(
    shape,
    images,
    norm1_gain,
    norm1_bias,
    qkv_weight,
    qv_bias,
    rel_pos_h,
    rel_pos_w,
    proj_weight,
    proj_bias,
    norm2_gain,
    norm2_bias,
    up_weight,
    up_bias,
    down_weight,
    down_bias,
    out_cotangent,
):
    nf, nc, nt = shape["fsdp"], shape["ctx"], shape["tp"]
    batch, quarter, d = images.shape
    sets = 4
    part = quarter // 2
    rows = 2 * part
    tokens = sets * rows
    half = qkv_weight.shape[2]
    width = half // 2
    heads = width // HD
    depth = qkv_weight.shape[1]
    blocks = nf * nc
    half_ff = up_weight.shape[1]
    fi, z, t = lax.axis_index("fsdp"), lax.axis_index("ctx"), lax.axis_index("tp")
    x, c = fi // 2, fi % 2
    zi, zp = z // 2, z % 2
    me = 2 * zp + c

    def send(v, move):
        return lax.ppermute(v, AXES, pairs_of(shape, move))

    core = lambda v: send(v, lambda f, w, u: (f ^ 1, w, u))
    tpswap = lambda v: send(v, lambda f, w, u: (f, w, u ^ 1))
    xswap = lambda v: send(v, lambda f, w, u: (f ^ 2, w, u))
    zswap = lambda v, k: send(v, lambda f, w, u: (f, w ^ k, u))
    beside = lambda v: zswap(v, 1)
    diagonal = lambda v: send(v, lambda f, w, u: (f ^ 1, w ^ 1, u))

    def pick(v, i, axis=0):
        return lax.dynamic_index_in_dim(v, i, axis, keepdims=False)

    def ordered(bit, mine, other, axis=0):
        return jnp.where(bit == 0, jnp.concatenate([mine, other], axis), jnp.concatenate([other, mine], axis))

    f = lambda v: v.astype(f32)
    tied = lambda *v: lax.optimization_barrier(v)
    ints = lambda *v: jnp.stack([jnp.asarray(i, jnp.int32) for i in v])
    place = ints(c, t, zi, zp)
    gain1, bias1 = f(norm1_gain)[None], f(norm1_bias)[None]

    image = lax.dynamic_index_in_dim(images, t, 0, False).reshape(2, part, d)
    is_far = lambda f, w: f % 2 != w // 2
    some = lambda v, move: lax.ppermute(
        v, AXES, [p for p in pairs_of(shape, move) if is_far(p[0] // (nc * nt), p[0] // nt % nc)]
    )
    far_a = some(pick(image, c), lambda f, w, u: (f, w ^ 2, u))
    far_b = some(pick(image, 1 - c), lambda f, w, u: (f ^ 1, w ^ 2, u))
    got = core(pack(place, images, qkv_weight))
    near, normed_near, w_own = route(place, images, got, qkv_weight, up_bias[None], qv_bias.reshape(1, d), gain1, bias1)
    w_other = tpswap(w_own)
    mine, yours = w_own[: 2 * depth, :576], w_other[: 2 * depth, :576]
    keep = jnp.where(t == zp, mine, yours)
    give = jnp.where(t == zp, yours, mine)
    w_z = [keep, zswap(give, 1), zswap(keep, 2), zswap(give, 3)]
    w = arrange(ints(fi * nc + z), w_z + [xswap(jnp.concatenate(w_z, axis=0))], d)
    near_sets = [normed_near, core(normed_near), beside(normed_near)]
    near_sets.append(core(near_sets[2]))
    far, normed_far = take_far(place, far_a, far_b, gain1, bias1, w_z[1:])

    own_w = jnp.concatenate([up_weight, down_weight, proj_weight], axis=1)
    own_w, normed_far = tied(own_w, normed_far)
    packed = lax.all_gather(own_w, AXES, axis=0, tiled=False).reshape(blocks, nt, depth, 2 * half_ff + half)

    far_sets = [normed_far, core(normed_far), beside(normed_far)]
    far_sets.append(core(far_sets[2]))

    bias = jnp.where(t == zp, qv_bias, w_other[2 * depth + 2].reshape(2, half))
    bias = pick(bias.reshape(2, 2, width), c, 1)
    bias = jnp.stack([bias[0], jnp.zeros_like(bias[0]), bias[1]])
    bias = f(jnp.concatenate([bias[:, :128].reshape(-1), bias[:, 128:].reshape(-1), jnp.zeros((64,), bf16)]))[None]
    flip = lambda v: jnp.pad(v[::-1].T, ((0, HD), (0, 128 - (2 * G - 1))))
    plain = lambda v: jnp.pad(v.T, ((0, HD), (0, 128 - (2 * G - 1))))
    tab = jnp.concatenate([flip(rel_pos_h), flip(rel_pos_w)], axis=1)
    tab_back = jnp.concatenate([flip(rel_pos_h), plain(rel_pos_w)], axis=1)
    block_rows = part // G
    first_of = lambda m, s_: (2 * m + s_ // 2) * (quarter // G) + (s_ % 2) * block_rows
    spot = np.concatenate([first_of(m, s_) * G + np.arange(part) for m in range(2) for s_ in range(sets)])
    at = np.arange(tokens)
    hot = np.zeros((tokens, 256), np.float32)
    for base, index in ((LH, spot // G), (LW, spot % G), (160, spot // G), (208, spot % G)):
        hot[at, base + index] = 1
    turn = np.zeros((G, tokens), np.float32)
    turn[G - 1 - at % G, at] = 1
    hot = jnp.asarray(hot.astype(ml_dtypes.bfloat16).reshape(2 * sets, part, 256))
    turn = jnp.asarray(turn.astype(ml_dtypes.bfloat16))

    order = [me ^ k for k in range(sets)]
    qkv = ()
    for g, group in enumerate((near_sets, far_sets)):
        m = zi ^ g
        spots = ints(*[m * sets + s for s in order], *[first_of(m, s) for s in order])
        qkv = prep(spots, group, w, bias, tab, hot, heads, qkv, g)
    q, k, v, normed = qkv

    normed, out_cotangent = tied(normed, out_cotangent)
    top_own = lax.dynamic_index_in_dim(out_cotangent, t, 0, False).reshape(2, part, d)
    top_got = core(pick(top_own, 1 - c))
    top_own = pick(top_own, c)
    top_near, top_far = jnp.where(c == zi, top_own, top_got), jnp.where(c == zi, top_got, top_own)
    q, top_near, top_far = tied(q, top_near, top_far)
    top_far = zswap(top_far, 2)
    att_far, q_far, mix_far = attend(q, k, v, 1)
    from_beside = beside(mix_far)
    att_near, q_near, mix_near = attend(q, k, v, 0)
    mix_near, from_beside, top_far = tied(mix_near, from_beside, top_far)
    top = [top_near, top_far]
    from_core = core(jnp.concatenate([mix_near[rows:], from_beside[rows:]], axis=0))
    att, q2 = (att_near, att_far), (q_near, q_far)

    other_up = w_other[2 * depth : 2 * depth + 2].reshape(-1)[:half_ff]
    full_bias = f(ordered(t, up_bias, other_up))[None]
    vecs = jnp.stack([f(proj_bias), f(norm2_gain), f(norm2_bias), f(down_bias)])
    (out0, out1, active, hidden_grad, normed2, middle_grad, branch, mixed, back, up_bias_grad, vec_grads) = mlp(
        ints(*order), [mix_near, from_beside, from_core], [near, far], top, packed, full_bias, vecs, half_ff, 768
    )
    back_beside = beside(back[2:].reshape(2 * rows, width))
    big = wgrad(normed2, top, branch, hidden_grad, active, mixed, blocks, nt)
    big, back_beside = tied(big, back_beside)
    back_core = core(jnp.concatenate([back[1], back_beside[rows:]], axis=0))
    back = [back[0], back_beside, back_core]
    big = lax.psum_scatter(big.reshape(d, -1), ("fsdp", "ctx"), scatter_dimension=0, tiled=True)

    def give_back(own, own_other, home, home_other):
        a = jnp.stack([own, own_other])
        b = jnp.stack([home, home_other])
        return own, own_other, home, home_other, core(jnp.where(c == zi, b, a))

    out_home, out_own = zswap(out1, 2), tpswap(out0)

    spots = ints(*[first_of(zi ^ g, s) for s in order for g in range(2)])
    b_back, b_tables = attend_back(spots, q2, k, v, att, back, tab_back, turn, 2, 1, 3, 256, sets)
    q2, b_back, out_home, out_own = tied(q2, b_back, out_home, out_own)
    home_other = tpswap(out_home)
    a_back, a_tables = attend_back(spots, q2, k, v, att, back, tab_back, turn, 0, 2, 3, 256, sets)
    home_other, a_back = tied(home_other, a_back)
    result = (out0, out_own, out_home, home_other)
    grads = [a_back, b_back]

    to_core = grad_down(1, grads, w, rows)
    w, to_core = tied(w, to_core)
    got = core(to_core)
    kept = grad_down(0, grads, w, rows)
    passed = (f(kept[1]) + f(got[1])).astype(bf16)
    normed, passed = tied(normed, passed)
    passed1, passed0 = beside(passed[part:]), beside(passed[:part])
    wg, sums, ng = qkv_grad(normed, grads, w, 3, blocks)
    grad1 = finish(place, kept, got, passed1, middle_grad, far, gain1, 1)
    wg = wg.reshape(2, 2, 2, 2, depth, 3 * width)
    wg_x = xswap(pick(wg, 1 - x))
    tables = (a_tables + b_tables)[:, :HD] * HD ** 0.5
    home = zswap(grad1, 2)


    def cut(v, sizes):
        at, out = 0, []
        v = v.reshape(-1)
        for size in sizes:
            out.append(lax.slice(v, (at,), (at + size,)))
            at += size
        return out

    grad1_, wg_x, tables, sums, ng, result = tied(grad1, wg_x, tables, sums, ng, result)
    sums = sums[0]
    qv = jnp.stack([jnp.concatenate([sums[i:i + 128], sums[j:j + 64]]) for i, j in ((0, 384), (256, 512))])
    qv = jnp.where(jnp.arange(sets)[:, None, None] == me, qv[None], 0.0).transpose(1, 0, 2).reshape(-1)
    small = jnp.concatenate(
        [v.reshape(-1, 128) for v in (vec_grads, up_bias_grad, ng[:, 0], ng[:, 1], qv, tables)], axis=0
    )
    for move in (core, tpswap, xswap):
        small = small + move(small)

    wg = f(pick(wg, x)) + f(wg_x)
    wg_low = wg.astype(bf16)
    wg = pick(wg, t, 2) + f(tpswap(pick(wg_low, 1 - t, 2)))
    result = assemble(place, *give_back(*result))
    grad0 = finish(place, kept, got, passed0, middle_grad, near, gain1, 0, [grad1, small, result])
    near_other = tpswap(grad0)
    grad1_, home, wg, small, result, grad0_, big = tied(grad1_, home, wg, small, result, grad0, big)
    big = big.reshape(depth, nt, -1)
    big = f(pick(big, t, 1)) + f(tpswap(pick(big, 1 - t, 1)))
    input_grad = assemble(place, *give_back(grad0_, near_other, home, tpswap(home)))
    wg_low = wg.astype(bf16)
    wg = pick(wg, zi, 1) + f(zswap(pick(wg_low, 1 - zi, 1), 2))
    wg = wg.astype(bf16)
    wg = send(wg, lambda f_, w_, u: (f_, (w_ // 2) * 2 + u, w_ % 2))
    wg = f(ordered(c, pick(wg, c)[None], core(pick(wg, 1 - c))[None]))
    wg = jnp.concatenate([wg[..., :384].reshape(2, depth, 3, 128), wg[..., 384:].reshape(2, depth, 3, 64)], axis=-1)
    wg = wg.transpose(2, 1, 0, 3).reshape(3, depth, half)

    for distance in (1, 2):
        small = small + zswap(small, distance)
    pb, g2, b2, db, ub, g1, b1, qv, tg = cut(small, (d, d, d, d, nt * half_ff, d, d, 2 * d, 256 * HD))
    g1 = (g1 - b1 * f(norm1_bias)) / f(norm1_gain)
    tg = tg.reshape(256, HD)
    return (
        result,
        input_grad,
        g1,
        b1,
        wg,
        pick(qv.reshape(2, nt, half), t, 1),
        tg[: 2 * G - 1][::-1],
        tg[128 : 128 + 2 * G - 1],
        big[:, 2 * half_ff :],
        pb,
        g2,
        b2,
        big[:, :half_ff],
        pick(ub.reshape(nt, half_ff), t),
        big[:, half_ff : 2 * half_ff],
        db,
    )


def layer_norm(values, gain_vec, shift_vec):
    centered = values - jnp.mean(values, axis=-1, keepdims=True)
    inverse = lax.rsqrt(jnp.mean(centered * centered, axis=-1, keepdims=True) + eps)
    standard = centered * inverse
    return (standard * gain_vec + shift_vec, standard, inverse)


def norm_back_plain(upstream, standard, inverse, gain_vec):
    scaled = upstream * gain_vec
    mean_term = jnp.mean(scaled, axis=-1, keepdims=True)
    proj_term = jnp.mean(scaled * standard, axis=-1, keepdims=True)
    return inverse * (scaled - mean_term - standard * proj_term)


def exact_gelu(values):
    return jax.nn.gelu(values, approximate=False)


def table_rows(pos_table, first_row, num_rows):
    table_len = pos_table.shape[0]
    grid_side = (table_len + 1) // 2
    query_row = first_row + lax.broadcasted_iota(jnp.int32, (num_rows, grid_side, table_len), 0)
    key_row = lax.broadcasted_iota(jnp.int32, (num_rows, grid_side, table_len), 1)
    entry_idx = lax.broadcasted_iota(jnp.int32, (num_rows, grid_side, table_len), 2)
    chooser = (query_row - key_row + grid_side - 1 == entry_idx).astype(jnp.float32)
    chooser = chooser.reshape(num_rows * grid_side, table_len)
    picked = jnp.dot(chooser, pos_table, precision=highest)
    return (picked.reshape(num_rows, grid_side, -1), chooser)


def rel_terms(query_f, row_first, rel_h, rel_w):
    grid_rows = query_f.shape[0] // G
    head_count = query_f.shape[1]
    near_h, pick_h = table_rows(rel_h, row_first, grid_rows)
    near_w, pick_w = table_rows(rel_w, 0, G)
    shaped = query_f.reshape(grid_rows, G, head_count, query_f.shape[2])
    term_h = jnp.einsum("awhc,akc->awhk", shaped, near_h, precision=highest)
    term_w = jnp.einsum("awhc,wkc->awhk", shaped, near_w, precision=highest)
    return (
        term_h.reshape(-1, head_count, G),
        term_w.reshape(-1, head_count, G),
        near_h,
        near_w,
        pick_h,
        pick_w,
    )


def piece_scores(query, key_h, term_h, term_w, factor):
    num_keys = key_h.shape[0]
    products = jnp.einsum("rhc,nhc->rhn", query, key_h, preferred_element_type=jnp.float32)
    position = (term_h[..., :, None] + term_w[..., None, :]).reshape(
        term_h.shape[0], term_h.shape[1], num_keys
    )
    return products * factor + position


def attend_step(running, pieces, offset, query, term_h, term_w, factor):
    run_max, run_sum, accumulated = running
    key_piece, value_piece = pieces
    num_keys = key_piece.shape[0]
    head_count = query.shape[1]
    key_h = key_piece.reshape(num_keys, head_count, -1)
    value_h = value_piece.reshape(num_keys, head_count, -1)
    scores = piece_scores(query, key_h, term_h, term_w, factor)
    new_max = jnp.maximum(run_max, jnp.max(scores, axis=-1))
    weights_p = jnp.exp(scores - new_max[..., None])
    run_sum = jnp.sum(weights_p, axis=-1)
    accumulated = jnp.einsum(
        "rhn,nhc->rhc", weights_p.astype(jnp.bfloat16), value_h, preferred_element_type=jnp.float32
    )
    return (new_max, run_sum, accumulated)


def grad_step(running, pieces, offset, query, out_grad, log_total, row_dot, term_h, term_w, factor):
    key_piece, value_piece = pieces
    num_keys = key_piece.shape[0]
    num_rows, head_count, head_size = query.shape
    key_h = key_piece.reshape(num_keys, head_count, head_size)
    value_h = value_piece.reshape(num_keys, head_count, head_size)
    scores = piece_scores(query, key_h, term_h, term_w, factor)
    weights_p = jnp.exp(scores - log_total[..., None])
    prob_grad = jnp.einsum("rhc,nhc->rhn", out_grad, value_h, preferred_element_type=jnp.float32)
    score_grad = (weights_p * (prob_grad - row_dot[..., None])).astype(jnp.bfloat16)
    query_acc = jnp.einsum("rhn,nhc->rhc", score_grad, key_h, preferred_element_type=jnp.float32)
    key_grad = (
        jnp.einsum("rhn,rhc->nhc", score_grad, query, preferred_element_type=jnp.float32) * factor
    )
    value_grad = jnp.einsum(
        "rhn,rhc->nhc", weights_p.astype(jnp.bfloat16), out_grad, preferred_element_type=jnp.float32
    )
    joined = jnp.concatenate(
        [key_grad.reshape(num_keys, -1), value_grad.reshape(num_keys, -1)], axis=1
    )
    grid_grad = score_grad.reshape(num_rows, head_count, num_keys // G, G)
    part_h = jnp.sum(grid_grad, axis=-1, dtype=jnp.float32)
    grad_w = jnp.sum(grid_grad, axis=-2, dtype=jnp.float32)
    return (query_acc, joined, part_h, grad_w)


def tensor_total(partial_sum):
    return lax.psum(partial_sum.astype(jnp.bfloat16), "tp").astype(jnp.float32)


def contract_last(left_mat, right_mat):
    return lax.dot_general(
        left_mat, right_mat, (((1,), (1,)), ((), ())), preferred_element_type=jnp.float32
    )


def micro_step(weights_full, picture, cotangent, params):
    (
        gain_one,
        shift_one,
        qv_shift,
        rel_h,
        rel_w,
        proj_shift,
        gain_two,
        shift_two,
        up_shift,
        down_shift,
    ) = params
    qkv_full, proj_full, up_full, down_full = weights_full
    rows_dev = picture.shape[0]
    half_width = qkv_full.shape[2]
    head_count = half_width // HD
    grid_rows = rows_dev // G
    row_first = lax.axis_index("ctx") * grid_rows
    factor = HD ** (-0.5)
    source = picture.astype(jnp.float32)
    normed_f, standard_one, inverse_one = layer_norm(source, gain_one, shift_one)
    normed = normed_f.astype(jnp.bfloat16)
    projected = jnp.einsum("rd,jde->jre", normed, qkv_full, preferred_element_type=jnp.float32)
    query_flat = (projected[0] + qv_shift[0]).astype(jnp.bfloat16)
    key_flat = projected[1].astype(jnp.bfloat16)
    value_flat = (projected[2] + qv_shift[1]).astype(jnp.bfloat16)
    query = query_flat.reshape(rows_dev, head_count, HD)
    query_f = query.astype(jnp.float32)
    term_h, term_w, near_h, near_w, pick_h, pick_w = rel_terms(query_f, row_first, rel_h, rel_w)
    start_state = (
        jnp.full((rows_dev, head_count), -1e30, jnp.float32),
        jnp.zeros((rows_dev, head_count), jnp.float32),
        jnp.zeros((rows_dev, head_count, HD), jnp.float32),
    )
    forward_fn = partial(attend_step, query=query, term_h=term_h, term_w=term_w, factor=factor)
    run_max, run_sum, accumulated = forward_fn(
        start_state,
        (
            lax.all_gather(key_flat, "ctx", axis=0, tiled=True),
            lax.all_gather(value_flat, "ctx", axis=0, tiled=True),
        ),
        jnp.int32(0),
    )
    attended = accumulated / run_sum[..., None]
    log_total = run_max + jnp.log(run_sum)
    mixed = attended.reshape(rows_dev, half_width).astype(jnp.bfloat16)
    middle = source + tensor_total(contract_last(mixed, proj_full)) + proj_shift
    normed2_f, standard_two, inverse_two = layer_norm(middle, gain_two, shift_two)
    normed2 = normed2_f.astype(jnp.bfloat16)
    hidden = jnp.dot(normed2, up_full, preferred_element_type=jnp.float32) + up_shift
    active, gelu_back = jax.vjp(exact_gelu, hidden)
    active_low = active.astype(jnp.bfloat16)
    result = (middle + tensor_total(contract_last(active_low, down_full)) + down_shift).astype(
        jnp.bfloat16
    )
    top_f = cotangent.astype(jnp.float32)
    down_grad = jnp.einsum("rd,rf->df", cotangent, active_low, preferred_element_type=jnp.float32)
    down_shift_grad = jnp.sum(top_f, axis=0)
    active_grad = jnp.dot(cotangent, down_full, preferred_element_type=jnp.float32)
    hidden_grad = gelu_back(active_grad)[0].astype(jnp.bfloat16)
    up_grad = jnp.einsum("rd,rf->df", normed2, hidden_grad, preferred_element_type=jnp.float32)
    up_shift_grad = jnp.sum(hidden_grad, axis=0, dtype=jnp.float32)
    normed2_grad = lax.psum(contract_last(hidden_grad, up_full).astype(jnp.bfloat16), "tp").astype(
        jnp.float32
    )
    middle_grad = top_f + norm_back_plain(normed2_grad, standard_two, inverse_two, gain_two)
    gain_two_grad = jnp.sum(normed2_grad * standard_two, axis=0)
    shift_two_grad = jnp.sum(normed2_grad, axis=0)
    branch_grad = middle_grad.astype(jnp.bfloat16)
    proj_grad = jnp.einsum("rd,re->de", branch_grad, mixed, preferred_element_type=jnp.float32)
    proj_shift_grad = jnp.sum(branch_grad, axis=0, dtype=jnp.float32)
    mixed_grad = (
        jnp.dot(branch_grad, proj_full, preferred_element_type=jnp.float32)
        .astype(jnp.bfloat16)
        .reshape(rows_dev, head_count, HD)
    )
    row_dot = jnp.sum(mixed_grad.astype(jnp.float32) * attended, axis=-1)
    ctx_count = lax.axis_size("ctx")
    start_back = (
        jnp.zeros((rows_dev, head_count, HD), jnp.float32),
        jnp.zeros((rows_dev * ctx_count, 2 * half_width), jnp.float32),
        jnp.zeros((rows_dev, head_count, G), jnp.float32),
        jnp.zeros((rows_dev, head_count, G), jnp.float32),
    )
    back_fn = partial(
        grad_step,
        query=query,
        out_grad=mixed_grad,
        log_total=log_total,
        row_dot=row_dot,
        term_h=term_h,
        term_w=term_w,
        factor=factor,
    )
    query_acc, key_value_acc, grad_h, grad_w = back_fn(
        start_back,
        (
            lax.all_gather(key_flat, "ctx", axis=0, tiled=True),
            lax.all_gather(value_flat, "ctx", axis=0, tiled=True),
        ),
        jnp.int32(0),
    )
    key_value_mine = lax.psum_scatter(
        key_value_acc.astype(jnp.bfloat16), "ctx", scatter_dimension=0, tiled=True
    ).astype(jnp.float32)
    grid_h = grad_h.reshape(grid_rows, G, head_count, G)
    grid_w = grad_w.reshape(grid_rows, G, head_count, G)
    shaped_q = query_f.reshape(grid_rows, G, head_count, HD)
    rel_query = jnp.einsum("awhk,akc->awhc", grid_h, near_h, precision=highest) + jnp.einsum(
        "awhk,wkc->awhc", grid_w, near_w, precision=highest
    )
    query_grad = (
        (query_acc * factor + rel_query.reshape(rows_dev, head_count, HD))
        .reshape(rows_dev, half_width)
        .astype(jnp.bfloat16)
    )
    key_grad = key_value_mine[:, :half_width].astype(jnp.bfloat16)
    value_grad = key_value_mine[:, half_width:].astype(jnp.bfloat16)
    table_h_part = jnp.dot(
        pick_h.T,
        jnp.einsum("awhk,awhc->akc", grid_h, shaped_q, precision=highest).reshape(-1, HD),
        precision=highest,
    )
    table_w_part = jnp.dot(
        pick_w.T,
        jnp.einsum("awhk,awhc->wkc", grid_w, shaped_q, precision=highest).reshape(-1, HD),
        precision=highest,
    )
    stacked = jnp.stack([query_grad, key_grad, value_grad])
    qkv_grad = jnp.einsum("rd,jre->jde", normed, stacked, preferred_element_type=jnp.float32)
    qv_shift_grad = jnp.stack(
        [
            jnp.sum(query_grad, axis=0, dtype=jnp.float32),
            jnp.sum(value_grad, axis=0, dtype=jnp.float32),
        ]
    )
    normed_part = jnp.einsum("jre,jde->rd", stacked, qkv_full, preferred_element_type=jnp.float32)
    normed_grad, table_h_grad, table_w_grad = (
        lax.psum(normed_part.astype(jnp.bfloat16), "tp").astype(jnp.float32),
        lax.psum(table_h_part.astype(jnp.bfloat16), "tp").astype(jnp.float32),
        lax.psum(table_w_part.astype(jnp.bfloat16), "tp").astype(jnp.float32),
    )
    input_grad = (middle_grad + norm_back_plain(normed_grad, standard_one, inverse_one, gain_one)).astype(
        jnp.bfloat16
    )
    gain_one_grad = jnp.sum(normed_grad * standard_one, axis=0)
    shift_one_grad = jnp.sum(normed_grad, axis=0)
    big_grads = (qkv_grad, proj_grad, up_grad, down_grad)
    small_grads = (
        gain_one_grad,
        shift_one_grad,
        qv_shift_grad,
        table_h_grad,
        table_w_grad,
        proj_shift_grad,
        gain_two_grad,
        shift_two_grad,
        up_shift_grad,
        down_shift_grad,
    )
    return (result, input_grad, big_grads, small_grads)


def add_trees(first_tree, second_tree):
    return jax.tree.map(lambda first_v, second_v: first_v + second_v, first_tree, second_tree)


def zeros_like_tree(tree):
    return jax.tree.map(lambda member: jnp.zeros(member.shape, jnp.float32), tree)


def local(
    images,
    norm1_gain,
    norm1_bias,
    qkv_weight,
    qv_bias,
    rel_pos_h,
    rel_pos_w,
    proj_weight,
    proj_bias,
    norm2_gain,
    norm2_bias,
    up_weight,
    up_bias,
    down_weight,
    down_bias,
    out_cotangent,
):
    params = tuple(
        (
            member.astype(jnp.float32)
            for member in (
                norm1_gain,
                norm1_bias,
                qv_bias,
                rel_pos_h,
                rel_pos_w,
                proj_bias,
                norm2_gain,
                norm2_bias,
                up_bias,
                down_bias,
            )
        )
    )
    small_start = zeros_like_tree(params)

    def per_batch(totals, pair):
        weights_full = (
            lax.all_gather(qkv_weight, ("fsdp", "ctx"), axis=1, tiled=True),
            lax.all_gather(proj_weight, ("fsdp", "ctx"), axis=0, tiled=True),
            lax.all_gather(up_weight, ("fsdp", "ctx"), axis=0, tiled=True),
            lax.all_gather(down_weight, ("fsdp", "ctx"), axis=0, tiled=True),
        )
        result, input_grad, big_grads, small_grads = micro_step(
            weights_full, pair[0], pair[1], params
        )
        shards = (
            lax.psum_scatter(big_grads[0], ("fsdp", "ctx"), scatter_dimension=1, tiled=True),
            lax.psum_scatter(big_grads[1], ("fsdp", "ctx"), scatter_dimension=0, tiled=True),
            lax.psum_scatter(big_grads[2], ("fsdp", "ctx"), scatter_dimension=0, tiled=True),
            lax.psum_scatter(big_grads[3], ("fsdp", "ctx"), scatter_dimension=0, tiled=True),
        )
        return (add_trees(totals, (shards, small_grads)), (result, input_grad))

    shard_start = zeros_like_tree((qkv_weight, proj_weight, up_weight, down_weight))
    (shard_totals, small_totals), (outputs, input_grads) = lax.scan(
        per_batch, (shard_start, small_start), (images, out_cotangent)
    )
    small_final = lax.psum(small_totals, ("fsdp", "ctx"))
    return (
        outputs,
        input_grads,
        small_final[0],
        small_final[1],
        shard_totals[0],
        small_final[2],
        small_final[3],
        small_final[4],
        shard_totals[1],
        small_final[5],
        small_final[6],
        small_final[7],
        shard_totals[2],
        small_final[8],
        shard_totals[3],
        small_final[9],
    )


def solution(mesh):
    shape = dict(mesh.shape)
    body = partial(grouped, shape) if shape == {"fsdp": 4, "ctx": 4, "tp": 2} else local
    placed = (
        P("fsdp", "ctx", None),
        P(),
        P(),
        P(None, ("fsdp", "ctx"), "tp"),
        P(None, "tp"),
        P(),
        P(),
        P(("fsdp", "ctx"), "tp"),
        P(),
        P(),
        P(),
        P(("fsdp", "ctx"), "tp"),
        P("tp"),
        P(("fsdp", "ctx"), "tp"),
        P(),
        P("fsdp", "ctx", None),
    )
    return jax.shard_map(
        body,
        mesh=mesh,
        in_specs=placed,
        out_specs=(
            P("fsdp", "ctx", None),
            P("fsdp", "ctx", None),
            P(),
            P(),
            P(None, ("fsdp", "ctx"), "tp"),
            P(None, "tp"),
            P(),
            P(),
            P(("fsdp", "ctx"), "tp"),
            P(),
            P(),
            P(),
            P(("fsdp", "ctx"), "tp"),
            P("tp"),
            P(("fsdp", "ctx"), "tp"),
            P(),
        ),
        check_vma=False,
    )
```

```python
from functools import partial

import jax
import jax.numpy as jnp
import ml_dtypes
import numpy as np
from jax import lax
from jax.experimental import pallas as pl
from jax.experimental.pallas import tpu as pltpu
from jax.sharding import PartitionSpec as P

G = 48
HD = 64


eps = 1e-06
highest = lax.Precision.HIGHEST
bf16, f32 = jnp.bfloat16, jnp.float32
VMEM_BYTES = 56 * 1024 * 1024
NN = (((1,), (0,)), ((), ()))
NT = (((1,), (1,)), ((), ()))
TN = (((0,), (0,)), ((), ()))
LH, LW = 64, 112
ANY = pl.BlockSpec(memory_space=pl.ANY)
PEAK = 5.0e15


def mm(a, b, dims=NN):
    return lax.dot_general(a, b, dims, preferred_element_type=f32)


def roll(x, shift, stride=None):
    extra = {} if stride is None else dict(stride=stride, stride_axis=0)
    return pltpu.roll(x, shift, 1, **extra)


def lane_iota(shape):
    return lax.broadcasted_iota(jnp.int32, shape, 1)


def struct(shape, dtype=bf16):
    return jax.ShapeDtypeStruct(shape, dtype)


def whole(shape):
    return pl.BlockSpec(shape, lambda *_: (0,) * len(shape))


def call(kernel, name, us, grid, prefetch, ins, in_specs, outs, out_specs, scratch=(), aliases=None):
    return pl.pallas_call(
        kernel,
        out_shape=outs,
        grid_spec=pltpu.PrefetchScalarGridSpec(
            num_scalar_prefetch=1, grid=grid, in_specs=in_specs, out_specs=out_specs, scratch_shapes=list(scratch)
        ),
        input_output_aliases=aliases or {},
        compiler_params=pltpu.CompilerParams(vmem_limit_bytes=VMEM_BYTES),
        cost_estimate=pl.CostEstimate(flops=int(us * 1e-6 * PEAK), bytes_accessed=0, transcendentals=0),
        name=name,
    )(prefetch, *ins)


def columns(w_ref, side):
    width = w_ref.shape[2] // 2
    parts = [jnp.where(side == 0, w_ref[j, :, :width], w_ref[j, :, width:]) for j in range(3)]
    return jnp.concatenate([p[:, :128] for p in parts] + [p[:, 128:] for p in parts], axis=1)


def pack_kernel(at_ref, image_ref, w_ref, out_ref):
    rows = image_ref.shape[1]
    depth = w_ref.shape[1]
    out_ref[:rows] = image_ref[0]
    out_ref[rows:] = jnp.zeros((depth, out_ref.shape[1]), bf16)
    out_ref[rows:, :576] = columns(w_ref, 1 - at_ref[0])


def pack(at, images, w):
    batch, quarter, d = images.shape
    rows = quarter // 2
    out = (rows + w.shape[1], d)
    return call(
        pack_kernel, "pack", 2, (1,), at, [images, w],
        [pl.BlockSpec((1, rows, d), lambda i, o: (o[1], 1 - o[0], 0)), whole(w.shape)], struct(out), whole(out),
    )


def route_kernel(at_ref, image_ref, got_ref, w_ref, ub_ref, qvb_ref, gain_ref, bias_ref, near_ref, normed_ref, w_out_ref):
    rows = image_ref.shape[1]
    depth = w_ref.shape[1]
    same = at_ref[0] == at_ref[2]
    own, got = image_ref[0], got_ref[:rows]
    near = jnp.where(same, own, got)
    near_ref[...] = near
    normed_ref[...] = norm(near.astype(f32), gain_ref[...], bias_ref[...])[0].astype(bf16)
    w_out_ref[...] = jnp.zeros(w_out_ref.shape, bf16)
    w_out_ref[:depth, :576] = columns(w_ref, at_ref[0])
    w_out_ref[depth:2 * depth] = got_ref[rows:]
    d = image_ref.shape[2]
    w_out_ref[2 * depth:2 * depth + 1] = ub_ref[:, :d]
    w_out_ref[2 * depth + 1:2 * depth + 2] = ub_ref[:, d:]
    w_out_ref[2 * depth + 2:2 * depth + 3] = qvb_ref[...]


def route(at, images, got, w, up_bias, qv_bias, gain, bias):
    batch, quarter, d = images.shape
    rows = quarter // 2
    half = (rows, d)
    out = (2 * w.shape[1] + 16, d)
    return call(
        route_kernel, "route", 3, (1,), at, [images, got, w, up_bias, qv_bias, gain, bias],
        [pl.BlockSpec((1, rows, d), lambda i, o: (o[1], o[0], 0))] + [whole(v.shape) for v in (got, w, up_bias, qv_bias, gain, bias)],
        (struct(half), struct(half), struct(out)), [whole(half)] * 2 + [whole(out)],
    )


def far_kernel(at_ref, a_ref, b_ref, gain_ref, bias_ref, *refs):
    far_ref, out_ref = refs[-2:]
    far = jnp.where(at_ref[0] == at_ref[2], a_ref[...], b_ref[...])
    far_ref[...] = far
    out_ref[...] = norm(far.astype(f32), gain_ref[...], bias_ref[...])[0].astype(bf16)


def take_far(at, a, b, gain, bias, after):
    return call(
        far_kernel, "take_far", 2, (1,), at, [a, b, gain, bias] + after, [whole(v.shape) for v in (a, b, gain, bias)] + [ANY] * len(after),
        (struct(a.shape), struct(a.shape)), [whole(a.shape)] * 2,
    )


def arrange_kernel(me_ref, *refs):
    pieces, out_ref = refs[:-1], refs[-1]
    depth = pieces[0].shape[0] // 2
    out_ref[:, 576:] = jnp.zeros((out_ref.shape[0], 64), bf16)
    for dx in range(2):
        for dz in range(4):
            for dc in range(2):
                ref, lo = (pieces[dz], dc) if dx == 0 else (pieces[4], dz * 2 + dc)
                at = (dx * 8 + dc * 4 + dz) ^ me_ref[0]
                out_ref[pl.ds(pl.multiple_of(at * depth, 16), depth), :576] = ref[lo * depth:(lo + 1) * depth]


def arrange(me, pieces, rows):
    return call(
        arrange_kernel, "arrange", 2, (1,), me, pieces, [whole(p.shape) for p in pieces],
        struct((rows, 640)), whole((rows, 640)),
    )


def prep_kernel(order_ref, *refs):
    xs, refs = refs[:4], refs[4:]
    w_ref, b_ref, tab_ref, hot_ref = refs[:4]
    q_ref, k_ref, v_ref, n_ref = refs[-4:]
    step = pl.program_id(0)
    rows = q_ref.shape[1]

    def work(x):
        first_row = order_ref[4 + step]
        n_ref[...] = x
        qkv = (mm(x, w_ref[...]) + b_ref[...]).astype(bf16).astype(f32)
        lane = lane_iota((G, 128))
        lane_all = lane_iota((rows, 128))
        hot_a = hot_ref[0, :, :128].astype(f32)
        hot_b = hot_ref[0, :, 128:]
        cols = [qkv[:, i * 128:(i + 1) * 128] for i in range(5)]
        back = [roll(v, 64) for v in cols[:4]]
        for h, (q, k, v) in enumerate(
            ((cols[0], cols[1], cols[2]), (back[0], back[1], back[2]), (cols[3], back[3], cols[4]))
        ):
            k_ref[h, :, :128] = jnp.where(lane_all < 64, k, hot_a).astype(bf16)
            k_ref[h, :, 128:] = hot_b
            v_ref[h] = jnp.where(lane_all < 64, v, jnp.where(lane_all < 67, 1.0, 0.0)).astype(bf16)
            turned = mm(q.astype(bf16), tab_ref[...])
            qf = q * (HD ** -0.5)
            for g in range(rows // G):
                r = first_row + g
                along_h = turned[g * G:(g + 1) * G, :128]
                along_w = turned[g * G:(g + 1) * G, 128:]
                h_a = roll(along_h, (LH - (G - 1) + 128 + r) % 128)
                h_b = roll(along_h, (32 - (G - 1) + 128 + r) % 128)
                w_a = roll(along_w, (LW - (G - 1)) % 128, 1)
                w_b = roll(along_w, (80 - (G - 1)) % 128, 1)
                h_lo = h_b - h_b.astype(bf16).astype(f32)
                w_lo = w_b - w_b.astype(bf16).astype(f32)
                first = jnp.where(lane < LH, qf[g * G:(g + 1) * G], jnp.where(lane < LW, h_a, w_a))
                second = jnp.where(lane < 32, w_a, jnp.where(lane < 80, h_lo, w_lo))
                q_ref[h, g * G:(g + 1) * G, :128] = first.astype(bf16)
                q_ref[h, g * G:(g + 1) * G, 128:] = second.astype(bf16)

    for k in range(4):
        @pl.when(step == k)
        def _(k=k):
            work(xs[k][...])


def prep(order, xs, w, b, tab, hot, heads, before, group):
    rows, d = xs[0].shape
    tokens = len(xs) * 2 * rows
    outs = (struct((heads, tokens, 256)), struct((heads, tokens, 256)), struct((heads, tokens, 128)), struct((tokens, d)))
    return call(
        prep_kernel, "prep", 7, (len(xs),), order, list(xs) + [w, b, tab, hot] + list(before),
        [whole(x.shape) for x in xs] + [whole(w.shape), whole(b.shape), whole(tab.shape)]
        + [pl.BlockSpec((1, rows, 256), lambda i, o: (o[i], 0, 0))] + [ANY] * len(before),
        outs,
        [
            pl.BlockSpec((heads, rows, 256), lambda i, o: (0, 2 * i + group, 0)),
            pl.BlockSpec((heads, rows, 256), lambda i, o: (0, 2 * i + group, 0)),
            pl.BlockSpec((heads, rows, 128), lambda i, o: (0, 2 * i + group, 0)),
            pl.BlockSpec((rows, d), lambda i, o: (2 * i + group, 0)),
        ],
        aliases={9 + i: i for i in range(len(before))},
    )


def attend_kernel(order_ref, q_ref, k_ref, v_ref, *refs, tiles):
    att_ref, q2_ref, mix_ref = refs[-3:]
    head = pl.program_id(0)
    start = 0
    for tile in tiles:
        at = pl.ds(start, tile)
        start += tile
        lane = lane_iota((tile, 128))
        q = q_ref[0, at, :]
        s = mm(q, k_ref[0], NT)
        m = jnp.max(s, axis=1, keepdims=True)
        p = jnp.exp(s - m)
        o = mm(p.astype(bf16), v_ref[0])
        total = o[:, 64:65]
        att = o / total
        lse = m + jnp.log(total)
        att_ref[0, at, :] = att
        low_att = att[:, :64].astype(bf16)
        for h in range(3):
            @pl.when(head == h)
            def _(h=h):
                mix_ref[at, h * 64:(h + 1) * 64] = low_att
        a = q[:, :128].astype(f32)
        b = q[:, 128:].astype(f32)
        full = a + roll(b, 32) - lse
        high = full.astype(bf16)
        low = roll(full - high.astype(f32), 96)
        q2_ref[0, at, :128] = jnp.where((lane >= LH) & (lane < LW), high.astype(f32), a).astype(bf16)
        q2_ref[0, at, 128:] = jnp.where((lane >= 32) & (lane < 80), low, b).astype(bf16)


def attend(q, k, v, side):
    heads, tokens, _ = q.shape
    rows = tokens // 2
    tiles = (256,) * (rows // 256) + ((rows % 256,) if rows % 256 else ())
    return call(
        partial(attend_kernel, tiles=tiles), "attend", 19, (heads,), jnp.zeros((1,), jnp.int32), [q, k, v],
        [
            pl.BlockSpec((1, rows, 256), lambda h, o: (h, side, 0)),
            pl.BlockSpec((1, tokens, 256), lambda h, o: (h, 0, 0)),
            pl.BlockSpec((1, tokens, 128), lambda h, o: (h, 0, 0)),
        ],
        (struct((heads, rows, 128), f32), struct((heads, rows, 256)), struct((rows, heads * HD))),
        [pl.BlockSpec((1, rows, 128), lambda h, o: (h, 0, 0)), pl.BlockSpec((1, rows, 256), lambda h, o: (h, 0, 0)), whole((rows, heads * HD))],
    )


def back_kernel(order_ref, qa_ref, qb_ref, k_ref, v_ref, atta_ref, attb_ref, own_ref, beside_ref, core_ref, tab_ref, turn_ref,
                d_ref, table_ref, q_ref, go_ref, kt_ref, acc_ref, hi_ref, lo_ref, *, tile, sets, first, count):
    head, step = pl.program_id(0), pl.program_id(1)
    last = pl.num_programs(1) - 1
    tokens = k_ref.shape[1]
    rows = tokens // sets
    wide = count * 64

    @pl.when(step == 0)
    def _():
        lane = lane_iota((rows, 128))
        for n, (ref, from_row) in enumerate(((own_ref, 0), (core_ref, 0), (beside_ref, 0), (core_ref, rows))):
            at = pl.ds(n * rows, rows)
            for h in range(count):
                @pl.when(head == h)
                def _(ref=ref, at=at, h=h, from_row=from_row):
                    lo = (first + h) * 64
                    go_ref[at, :64] = ref[from_row:from_row + rows, lo:lo + 64]
        go = go_ref[...].astype(f32)
        lane = lane_iota(go.shape)
        go = jnp.where(lane < 64, go, 0.0)
        att = jnp.concatenate([atta_ref[0], attb_ref[0]], axis=0)
        q_ref[:tokens // 2] = qa_ref[0]
        q_ref[tokens // 2:] = qb_ref[0]
        dot = jnp.sum(jnp.where(lane < 64, go * att, 0.0), axis=1, keepdims=True)
        high = dot.astype(bf16).astype(f32)
        mid = (dot - high).astype(bf16).astype(f32)
        low = dot - high - mid
        go_ref[...] = jnp.where(lane < 64, go, jnp.where(lane == 64, -high, jnp.where(lane == 65, -mid, jnp.where(lane == 66, -low, 0.0)))).astype(bf16)
        acc_ref[...] = jnp.zeros_like(acc_ref)
        kt_ref[:LW] = k_ref[0, :, :128].T[:LW]
        kt_ref[LW:] = turn_ref[...]

    keys = tokens // pl.num_programs(1)
    for i in range(keys // tile):
        at = pl.ds(pl.multiple_of(step * keys + i * tile, tile), tile)
        s = mm(k_ref[0, at, :], q_ref[...], NT)
        p = jnp.exp(s)
        pb = p.astype(bf16)
        d = (p * mm(v_ref[0, at, :], go_ref[...], NT)).astype(bf16)
        dv = mm(pb, go_ref[...]).astype(bf16)
        dk = mm(d, q_ref[:, :128]).astype(bf16)
        for h in range(count):
            @pl.when(head == h)
            def _(h=h):
                d_ref[at, 2 * wide + h * 64:2 * wide + (h + 1) * 64] = dv[:, :64]
                d_ref[at, wide + h * 64:wide + (h + 1) * 64] = dk[:, :64]
        acc_ref[...] += mm(kt_ref[:, at], d)

    @pl.when(step == last)
    def _():
        small = lane_iota((G, 128))
        a = acc_ref[:128].T
        b = jnp.concatenate([acc_ref[128:160], jnp.zeros((96, tokens), f32)], axis=0).T
        for g in range(tokens // G):
            block, inner = divmod(g, rows // 2 // G)
            r = order_ref[block] + inner
            ag = a[g * G:(g + 1) * G]
            bg = b[g * G:(g + 1) * G]
            along_h = jnp.where((small >= LH) & (small < LW), ag, 0.0)
            along_w = jnp.where(small >= LW, ag, jnp.where(small < 32, bg, 0.0))
            along_h = roll(along_h, (256 + G - 1 - LH - r) % 128)
            along_w = roll(along_w, (128 - LW) % 128, 1)
            h_hi = along_h.astype(bf16)
            w_hi = along_w.astype(bf16)
            hi_ref[g * G:(g + 1) * G, :128] = h_hi
            hi_ref[g * G:(g + 1) * G, 128:] = w_hi
            lo_ref[g * G:(g + 1) * G, :128] = (along_h - h_hi.astype(f32)).astype(bf16)
            lo_ref[g * G:(g + 1) * G, 128:] = (along_w - w_hi.astype(f32)).astype(bf16)
        turned = mm(hi_ref[...], tab_ref[...], NT) + mm(lo_ref[...], tab_ref[...], NT)
        dq = (a * (HD ** -0.5) + turned).astype(bf16)
        for h in range(count):
            @pl.when(head == h)
            def _(h=h):
                d_ref[:, h * 64:(h + 1) * 64] = dq[:, :64]
        tables = mm(hi_ref[...], q_ref[:, :128], TN)

        @pl.when(head == 0)
        def _():
            table_ref[...] = tables

        @pl.when(head > 0)
        def _():
            table_ref[...] += tables


def attend_back(order, q2, k, v, att, grads, tab, turn, first, count, steps, tile, sets):
    _, tokens, _ = k.shape
    at = lambda h, i, o: (first + h, 0, 0)
    wide = 3 * count * HD
    per_head = lambda a: pl.BlockSpec((1,) + a.shape[1:], at)
    return call(
        partial(back_kernel, tile=tile, sets=sets, first=first, count=count), "attend_back", 21 * count,
        (count, steps), order, list(q2) + [k, v] + list(att) + list(grads) + [tab, turn],
        [per_head(a) for a in list(q2) + [k, v] + list(att)] + [whole(g.shape) for g in grads] + [whole(tab.shape), whole(turn.shape)],
        (struct((tokens, wide)), struct((256, 128), f32)),
        [whole((tokens, wide)), whole((256, 128))],
        [
            pltpu.VMEM((tokens, 256), bf16),
            pltpu.VMEM((tokens, 128), bf16),
            pltpu.VMEM((160, tokens), bf16),
            pltpu.VMEM((160, tokens), f32),
            pltpu.VMEM((tokens, 256), bf16),
            pltpu.VMEM((tokens, 256), bf16),
        ],
    )


def norm(v, gain, bias):
    mean = jnp.mean(v, axis=1, keepdims=True)
    centered = v - mean
    inverse = lax.rsqrt(jnp.mean(centered * centered, axis=1, keepdims=True) + eps)
    unit = centered * inverse
    return unit * gain + bias, unit, inverse


def norm_back(upstream, unit, inverse, gain):
    scaled = upstream * gain
    return inverse * (scaled - jnp.mean(scaled, axis=1, keepdims=True) - unit * jnp.mean(scaled * unit, axis=1, keepdims=True))


def mlp_kernel(order_ref, near_ref, beside_ref, core_ref, src0, src1, top0, top1, up_ref, down_ref, proj_ref, ub_ref, vec_ref,
               out0, out1, act_ref, hg_ref, n2_ref, mg_ref, br_ref, mix_ref, back_ref, ubg_ref, vg_ref,
               mid_ref, unit_ref, inv_ref, acc_ref, ng_ref, quad_ref, top_ref):
    step = pl.program_id(0)
    last = pl.num_programs(0) - 1
    part, d = src0.shape
    half = proj_ref.shape[3]
    width = near_ref.shape[1]

    def proj(i):
        return proj_ref[:, i].reshape(d, half)

    @pl.when(step == 0)
    def _():
        rows = near_ref.shape[0] // 2
        for k, piece in enumerate((near_ref[:rows], core_ref[:rows], beside_ref[:rows], core_ref[rows:])):
            quad_ref[order_ref[k]] = piece
        for i in range(4):
            mix_ref[:, i * width:(i + 1) * width] = quad_ref[i]
        top_ref[:part] = top0[...]
        top_ref[part:] = top1[...]
        mid = jnp.concatenate([src0[...], src1[...]], axis=0).astype(f32) + vec_ref[0:1] + mm(mix_ref[:, :half], proj(0), NT) + mm(mix_ref[:, half:], proj(1), NT)
        normed, unit, inverse = norm(mid, vec_ref[1:2], vec_ref[2:3])
        mid_ref[...] = mid
        unit_ref[...] = unit
        inv_ref[...] = inverse
        n2_ref[...] = normed.astype(bf16)

    tile = up_ref.shape[3]
    up = up_ref[:, 0].reshape(d, tile)
    down = down_ref[:, 0].reshape(d, tile)
    hidden = mm(n2_ref[...], up) + ub_ref[...]
    phi_all = 0.5 + 0.5 * lax.erf(hidden * (0.5 ** 0.5))
    slope = phi_all + hidden * (jnp.exp(-0.5 * hidden * hidden) * 0.3989422804014327)
    active = (hidden * phi_all).astype(bf16)
    hg = (mm(top_ref[...], down) * slope).astype(bf16)
    act_ref[...] = active
    hg_ref[...] = hg
    ubg_ref[...] = jnp.sum(hg.astype(f32), axis=0, keepdims=True)
    out = mm(active, down, NT)
    ng = mm(hg, up, NT)

    @pl.when(step == 0)
    def _():
        acc_ref[...] = out
        ng_ref[...] = ng

    @pl.when(step > 0)
    def _():
        acc_ref[...] += out
        ng_ref[...] += ng

    @pl.when(step == last)
    def _():
        top = top_ref[...].astype(f32)
        grad = ng_ref[...]
        unit = unit_ref[...]
        out = (mid_ref[...] + acc_ref[...] + vec_ref[3:4]).astype(bf16)
        out0[...] = out[:part]
        out1[...] = out[part:]
        middle = top + norm_back(grad, unit, inv_ref[...], vec_ref[1:2])
        branch = middle.astype(bf16)
        mg_ref[...] = middle
        br_ref[...] = branch
        for i in range(2):
            piece = mm(branch, proj(i)).astype(bf16)
            quad_ref[2 * i] = piece[:, :width]
            quad_ref[2 * i + 1] = piece[:, width:]
        for k in range(4):
            back_ref[k] = quad_ref[order_ref[k]]
        vg_ref[0:1] = jnp.sum(branch.astype(f32), axis=0, keepdims=True)
        vg_ref[1:2] = jnp.sum(grad * unit, axis=0, keepdims=True)
        vg_ref[2:3] = jnp.sum(grad, axis=0, keepdims=True)
        vg_ref[3:4] = jnp.sum(top, axis=0, keepdims=True)


def mlp(order, mixed, src, top, packed, up_bias, vecs, half_ff, tile):
    part, d = src[0].shape
    rows = 2 * part
    blocks, halves, depth, _ = packed.shape
    per = half_ff // tile
    half = d // halves
    quad = (4, rows, mixed[0].shape[1])
    ff = halves * half_ff
    by_tile = pl.BlockSpec((rows, tile), lambda i, o: (0, i))
    row_tile = pl.BlockSpec((1, tile), lambda i, o: (0, i))
    full = whole((rows, d))
    piece = whole((part, d))
    return call(
        mlp_kernel, "mlp", 24, (halves * per,), order,
        list(mixed) + list(src) + list(top) + [packed, packed, packed, up_bias, vecs],
        [whole(m.shape) for m in mixed] + [
            piece, piece, piece, piece,
            pl.BlockSpec((blocks, 1, depth, tile), lambda i, o: (0, i // per, 0, i % per)),
            pl.BlockSpec((blocks, 1, depth, tile), lambda i, o: (0, i // per, 0, per + i % per)),
            pl.BlockSpec((blocks, halves, depth, half), lambda i, o: (0, 0, 0, 2 * half_ff // half)),
            row_tile, whole(vecs.shape),
        ],
        (struct((part, d)), struct((part, d)), struct((rows, ff)), struct((rows, ff)), struct((rows, d)), struct((rows, d), f32), struct((rows, d)), struct((rows, d)))
        + (struct(quad),) + (struct((1, ff), f32), struct((4, d), f32)),
        [piece, piece, by_tile, by_tile, full, full, full, full] + [whole(quad)] + [row_tile, whole((4, d))],
        [
            pltpu.VMEM((rows, d), f32),
            pltpu.VMEM((rows, d), f32),
            pltpu.VMEM((rows, 1), f32),
            pltpu.VMEM((rows, d), f32),
            pltpu.VMEM((rows, d), f32),
            pltpu.VMEM(quad, bf16),
            pltpu.VMEM((rows, d), bf16),
        ],
    )


def wgrad_kernel(_, n2_ref, top0, top1, br_ref, hg_ref, act_ref, mix_ref, out_ref, left_ref):
    half, third = pl.program_id(0), pl.program_id(1)
    blocks, depth, tile = out_ref.shape

    @pl.when((half == 0) & (third == 0))
    def _():
        left_ref[0] = n2_ref[...].T
        left_ref[1] = jnp.concatenate([top0[...], top1[...]], axis=0).T
        left_ref[2] = br_ref[...].T

    at = 0
    for i, ref in enumerate((hg_ref, act_ref, mix_ref)):
        width = ref.shape[1]
        for k in range(3):
            lo, hi = max(at, k * tile), min(at + width, (k + 1) * tile)
            if lo < hi:
                @pl.when(third == k)
                def _(i=i, k=k, ref=ref, lo=lo, hi=hi, at=at):
                    part = mm(left_ref[i], ref[:, lo - at:hi - at]).astype(bf16)
                    out_ref[:, :, lo - k * tile:hi - k * tile] = part.reshape(blocks, depth, hi - lo)
        at += width


def wgrad(n2, top, branch, hg, active, mixed, blocks, halves):
    rows, d = n2.shape
    half_ff, half = hg.shape[1] // halves, d // halves
    depth = d // blocks
    total = 2 * half_ff + half
    by_half = lambda n: pl.BlockSpec((rows, n), lambda s, j, o: (0, s))
    return call(
        wgrad_kernel, "wgrad", 18, (halves, 3), jnp.zeros((1,), jnp.int32),
        [n2, top[0], top[1], branch, hg, active, mixed],
        [whole((rows, d)), whole(top[0].shape), whole(top[1].shape), whole((rows, d)), by_half(half_ff), by_half(half_ff), by_half(half)],
        struct((blocks, depth, halves * total)),
        pl.BlockSpec((blocks, depth, total // 3), lambda s, j, o: (0, 0, 3 * s + j)),
        [pltpu.VMEM((3, d, rows), bf16)],
    )


def down_kernel(_, a_ref, b_ref, w_ref, ng_ref):
    both = jnp.concatenate([a_ref[...], b_ref[...]], axis=1)
    ng_ref[0] = mm(both, w_ref[:, :both.shape[1]], NT).astype(bf16)


def grad_down(sets, grads, w, rows):
    d = w.shape[0]
    return call(
        down_kernel, "grad_down", 4, (2,), jnp.zeros((1,), jnp.int32), list(grads) + [w],
        [pl.BlockSpec((rows, g.shape[1]), lambda i, o: (2 * i + sets, 0)) for g in grads] + [whole(w.shape)],
        struct((2, rows, d)), pl.BlockSpec((1, rows, d), lambda i, o: (i, 0, 0)),
    )


def qkv_grad_kernel(_, x_ref, a_ref, b_ref, w_ref, wg_ref, bg_ref, ng_ref, acc_ref):
    step = pl.program_id(0)
    width = wg_ref.shape[-1]
    both = jnp.concatenate([a_ref[...], b_ref[...]], axis=1)
    add = mm(x_ref[...].T, both)
    sums = jnp.sum(both.astype(f32), axis=0, keepdims=True)

    @pl.when(step == 0)
    def _():
        acc_ref[...] = add
        bg_ref[...] = sums

    @pl.when(step > 0)
    def _():
        acc_ref[...] += add
        bg_ref[...] += sums

    @pl.when(step == pl.num_programs(0) - 1)
    def _():
        full = acc_ref[...]
        wg_ref[...] = full.astype(bf16).reshape(wg_ref.shape)
        w = w_ref[:, :width].astype(f32)
        lane = lane_iota(ng_ref.shape)
        a = jnp.sum(full * w, axis=1, keepdims=True)
        b = jnp.sum(bg_ref[...] * w, axis=1, keepdims=True)
        ng_ref[...] = jnp.where(lane == 0, a, jnp.where(lane == 1, b, 0.0))


def qkv_grad(x, grads, w, steps, blocks):
    tokens, d = x.shape
    rows = tokens // steps
    width = sum(g.shape[1] for g in grads)
    by_rows = lambda n: pl.BlockSpec((rows, n), lambda i, o: (i, 0))
    return call(
        qkv_grad_kernel, "qkv_grad", 5, (steps,), jnp.zeros((1,), jnp.int32), [x] + list(grads) + [w],
        [by_rows(d)] + [by_rows(g.shape[1]) for g in grads] + [whole(w.shape)],
        (struct((blocks, d // blocks, width)), struct((1, width), f32), struct((d, 128), f32)),
        [whole((blocks, d // blocks, width)), whole((1, width)), whole((d, 128))],
        [pltpu.VMEM((d, width), f32)],
    )


def finish_kernel(_, kept_ref, got_ref, passed_ref, middle_ref, src_ref, gain_ref, *refs):
    out_ref = refs[-1]
    grad = kept_ref[0].astype(f32) + got_ref[0].astype(f32) + passed_ref[...].astype(f32)
    _, unit, inverse = norm(src_ref[...].astype(f32), 1.0, 0.0)
    out_ref[...] = (middle_ref[...] + norm_back(grad, unit, inverse, gain_ref[...])).astype(bf16)


def finish(at, kept, got, passed, middle, src, gain, group, after=()):
    part, d = src.shape
    first = pl.BlockSpec((1, part, d), lambda i, o: (0, group, 0))
    return call(
        finish_kernel, "finish", 0.1, (1,), at, [kept, got, passed, middle, src, gain, *after],
        [first, first, whole((part, d)), pl.BlockSpec((part, d), lambda i, o: (group, 0)), whole((part, d)), whole(gain.shape)] + [ANY] * len(after),
        struct((part, d)), whole((part, d)),
    )


def assemble_kernel(at_ref, own_ref, other_ref, home_ref, home_other_ref, got_ref, out_ref):
    part = own_ref.shape[0]
    mine = pl.ds(pl.multiple_of(at_ref[0] * part, 16), part)
    other = pl.ds(pl.multiple_of((1 - at_ref[0]) * part, 16), part)
    same = at_ref[0] == at_ref[2]
    out_ref[at_ref[1], mine] = jnp.where(same, own_ref[...], home_ref[...])
    out_ref[1 - at_ref[1], mine] = jnp.where(same, other_ref[...], home_other_ref[...])
    out_ref[at_ref[1], other] = got_ref[0]
    out_ref[1 - at_ref[1], other] = got_ref[1]


def assemble(place, own, own_other, home, home_other, got):
    part, d = own.shape
    ins = [own, own_other, home, home_other, got]
    return call(
        assemble_kernel, "assemble", 0.1, (1,), place, ins, [whole(v.shape) for v in ins],
        struct((2, 2 * part, d)), whole((2, 2 * part, d)),
    )


AXES = ("fsdp", "ctx", "tp")


def pairs_of(shape, move):
    nf, nc, nt = shape["fsdp"], shape["ctx"], shape["tp"]
    flat = lambda f, z, t: (f * nc + z) * nt + t
    return [(flat(f, z, t), flat(*move(f, z, t))) for f in range(nf) for z in range(nc) for t in range(nt)]


def grouped(
    shape,
    images,
    norm1_gain,
    norm1_bias,
    qkv_weight,
    qv_bias,
    rel_pos_h,
    rel_pos_w,
    proj_weight,
    proj_bias,
    norm2_gain,
    norm2_bias,
    up_weight,
    up_bias,
    down_weight,
    down_bias,
    out_cotangent,
):
    nf, nc, nt = shape["fsdp"], shape["ctx"], shape["tp"]
    batch, quarter, d = images.shape
    sets = 4
    part = quarter // 2
    rows = 2 * part
    tokens = sets * rows
    half = qkv_weight.shape[2]
    width = half // 2
    heads = width // HD
    depth = qkv_weight.shape[1]
    blocks = nf * nc
    half_ff = up_weight.shape[1]
    fi, z, t = lax.axis_index("fsdp"), lax.axis_index("ctx"), lax.axis_index("tp")
    x, c = fi // 2, fi % 2
    zi, zp = z // 2, z % 2
    me = 2 * zp + c

    def send(v, move):
        return lax.ppermute(v, AXES, pairs_of(shape, move))

    core = lambda v: send(v, lambda f, w, u: (f ^ 1, w, u))
    tpswap = lambda v: send(v, lambda f, w, u: (f, w, u ^ 1))
    xswap = lambda v: send(v, lambda f, w, u: (f ^ 2, w, u))
    zswap = lambda v, k: send(v, lambda f, w, u: (f, w ^ k, u))
    beside = lambda v: zswap(v, 1)
    diagonal = lambda v: send(v, lambda f, w, u: (f ^ 1, w ^ 1, u))

    def pick(v, i, axis=0):
        return lax.dynamic_index_in_dim(v, i, axis, keepdims=False)

    def ordered(bit, mine, other, axis=0):
        return jnp.where(bit == 0, jnp.concatenate([mine, other], axis), jnp.concatenate([other, mine], axis))

    f = lambda v: v.astype(f32)
    tied = lambda *v: lax.optimization_barrier(v)
    ints = lambda *v: jnp.stack([jnp.asarray(i, jnp.int32) for i in v])
    place = ints(c, t, zi, zp)
    gain1, bias1 = f(norm1_gain)[None], f(norm1_bias)[None]

    image = lax.dynamic_index_in_dim(images, t, 0, False).reshape(2, part, d)
    is_far = lambda f, w: f % 2 != w // 2
    some = lambda v, move: lax.ppermute(
        v, AXES, [p for p in pairs_of(shape, move) if is_far(p[0] // (nc * nt), p[0] // nt % nc)]
    )
    far_a = some(pick(image, c), lambda f, w, u: (f, w ^ 2, u))
    far_b = some(pick(image, 1 - c), lambda f, w, u: (f ^ 1, w ^ 2, u))
    got = core(pack(place, images, qkv_weight))
    near, normed_near, w_own = route(place, images, got, qkv_weight, up_bias[None], qv_bias.reshape(1, d), gain1, bias1)
    w_other = tpswap(w_own)
    mine, yours = w_own[: 2 * depth, :576], w_other[: 2 * depth, :576]
    keep = jnp.where(t == zp, mine, yours)
    give = jnp.where(t == zp, yours, mine)
    w_z = [keep, zswap(give, 1), zswap(keep, 2), zswap(give, 3)]
    w = arrange(ints(fi * nc + z), w_z + [xswap(jnp.concatenate(w_z, axis=0))], d)
    near_sets = [normed_near, core(normed_near), beside(normed_near)]
    near_sets.append(core(near_sets[2]))
    far, normed_far = take_far(place, far_a, far_b, gain1, bias1, w_z[1:])

    own_w = jnp.concatenate([up_weight, down_weight, proj_weight], axis=1)
    own_w, normed_far = tied(own_w, normed_far)
    packed = lax.all_gather(own_w, AXES, axis=0, tiled=False).reshape(blocks, nt, depth, 2 * half_ff + half)

    far_sets = [normed_far, core(normed_far), beside(normed_far)]
    far_sets.append(core(far_sets[2]))

    bias = jnp.where(t == zp, qv_bias, w_other[2 * depth + 2].reshape(2, half))
    bias = pick(bias.reshape(2, 2, width), c, 1)
    bias = jnp.stack([bias[0], jnp.zeros_like(bias[0]), bias[1]])
    bias = f(jnp.concatenate([bias[:, :128].reshape(-1), bias[:, 128:].reshape(-1), jnp.zeros((64,), bf16)]))[None]
    flip = lambda v: jnp.pad(v[::-1].T, ((0, HD), (0, 128 - (2 * G - 1))))
    plain = lambda v: jnp.pad(v.T, ((0, HD), (0, 128 - (2 * G - 1))))
    tab = jnp.concatenate([flip(rel_pos_h), flip(rel_pos_w)], axis=1)
    tab_back = jnp.concatenate([flip(rel_pos_h), plain(rel_pos_w)], axis=1)
    block_rows = part // G
    first_of = lambda m, s_: (2 * m + s_ // 2) * (quarter // G) + (s_ % 2) * block_rows
    spot = np.concatenate([first_of(m, s_) * G + np.arange(part) for m in range(2) for s_ in range(sets)])
    at = np.arange(tokens)
    hot = np.zeros((tokens, 256), np.float32)
    for base, index in ((LH, spot // G), (LW, spot % G), (160, spot // G), (208, spot % G)):
        hot[at, base + index] = 1
    turn = np.zeros((G, tokens), np.float32)
    turn[G - 1 - at % G, at] = 1
    hot = jnp.asarray(hot.astype(ml_dtypes.bfloat16).reshape(2 * sets, part, 256))
    turn = jnp.asarray(turn.astype(ml_dtypes.bfloat16))

    order = [me ^ k for k in range(sets)]
    qkv = ()
    for g, group in enumerate((near_sets, far_sets)):
        m = zi ^ g
        spots = ints(*[m * sets + s for s in order], *[first_of(m, s) for s in order])
        qkv = prep(spots, group, w, bias, tab, hot, heads, qkv, g)
    q, k, v, normed = qkv

    normed, out_cotangent = tied(normed, out_cotangent)
    top_own = lax.dynamic_index_in_dim(out_cotangent, t, 0, False).reshape(2, part, d)
    top_got = core(pick(top_own, 1 - c))
    top_own = pick(top_own, c)
    top_near, top_far = jnp.where(c == zi, top_own, top_got), jnp.where(c == zi, top_got, top_own)
    q, top_near, top_far = tied(q, top_near, top_far)
    top_far = zswap(top_far, 2)
    att_far, q_far, mix_far = attend(q, k, v, 1)
    from_beside = beside(mix_far)
    att_near, q_near, mix_near = attend(q, k, v, 0)
    mix_near, from_beside, top_far = tied(mix_near, from_beside, top_far)
    top = [top_near, top_far]
    from_core = core(jnp.concatenate([mix_near[rows:], from_beside[rows:]], axis=0))
    att, q2 = (att_near, att_far), (q_near, q_far)

    other_up = w_other[2 * depth : 2 * depth + 2].reshape(-1)[:half_ff]
    full_bias = f(ordered(t, up_bias, other_up))[None]
    vecs = jnp.stack([f(proj_bias), f(norm2_gain), f(norm2_bias), f(down_bias)])
    (out0, out1, active, hidden_grad, normed2, middle_grad, branch, mixed, back, up_bias_grad, vec_grads) = mlp(
        ints(*order), [mix_near, from_beside, from_core], [near, far], top, packed, full_bias, vecs, half_ff, 768
    )
    back_beside = beside(back[2:].reshape(2 * rows, width))
    big = wgrad(normed2, top, branch, hidden_grad, active, mixed, blocks, nt)
    big, back_beside = tied(big, back_beside)
    back_core = core(jnp.concatenate([back[1], back_beside[rows:]], axis=0))
    back = [back[0], back_beside, back_core]
    big = lax.psum_scatter(big.reshape(d, -1), ("fsdp", "ctx"), scatter_dimension=0, tiled=True)

    def give_back(own, own_other, home, home_other):
        a = jnp.stack([own, own_other])
        b = jnp.stack([home, home_other])
        return own, own_other, home, home_other, core(jnp.where(c == zi, b, a))

    out_home, out_own = zswap(out1, 2), tpswap(out0)

    spots = ints(*[first_of(zi ^ g, s) for s in order for g in range(2)])
    b_back, b_tables = attend_back(spots, q2, k, v, att, back, tab_back, turn, 2, 1, 3, 256, sets)
    q2, b_back, out_home, out_own = tied(q2, b_back, out_home, out_own)
    home_other = tpswap(out_home)
    a_back, a_tables = attend_back(spots, q2, k, v, att, back, tab_back, turn, 0, 2, 3, 256, sets)
    home_other, a_back = tied(home_other, a_back)
    result = (out0, out_own, out_home, home_other)
    grads = [a_back, b_back]

    to_core = grad_down(1, grads, w, rows)
    w, to_core = tied(w, to_core)
    got = core(to_core)
    kept = grad_down(0, grads, w, rows)
    passed = (f(kept[1]) + f(got[1])).astype(bf16)
    normed, passed = tied(normed, passed)
    passed1, passed0 = beside(passed[part:]), beside(passed[:part])
    wg, sums, ng = qkv_grad(normed, grads, w, 3, blocks)
    grad1 = finish(place, kept, got, passed1, middle_grad, far, gain1, 1)
    wg = wg.reshape(2, 2, 2, 2, depth, 3 * width)
    wg_x = xswap(pick(wg, 1 - x))
    tables = (a_tables + b_tables)[:, :HD] * HD ** 0.5
    home = zswap(grad1, 2)


    def cut(v, sizes):
        at, out = 0, []
        v = v.reshape(-1)
        for size in sizes:
            out.append(lax.slice(v, (at,), (at + size,)))
            at += size
        return out

    grad1_, tables, sums, ng, result = tied(grad1, tables, sums, ng, result)
    sums = sums[0]
    qv = jnp.stack([jnp.concatenate([sums[i:i + 128], sums[j:j + 64]]) for i, j in ((0, 384), (256, 512))])
    qv = jnp.where(jnp.arange(sets)[:, None, None] == me, qv[None], 0.0).transpose(1, 0, 2).reshape(-1)
    small = jnp.concatenate(
        [v.reshape(-1, 128) for v in (vec_grads, up_bias_grad, ng[:, 0], ng[:, 1], qv, tables)], axis=0
    )
    for move in (core, tpswap, xswap):
        small = small + move(small)

    result = assemble(place, *give_back(*result))
    wg_x, small, result = tied(wg_x, small, result)

    wg = f(pick(wg, x)) + f(wg_x)
    wg_low = wg.astype(bf16)
    wg = pick(wg, t, 2) + f(tpswap(pick(wg_low, 1 - t, 2)))
    grad0 = finish(place, kept, got, passed0, middle_grad, near, gain1, 0, [grad1, small, result])
    near_other = tpswap(grad0)
    grad1_, home, wg, small, result, grad0_, big = tied(grad1_, home, wg, small, result, grad0, big)
    big = big.reshape(depth, nt, -1)
    big = f(pick(big, t, 1)) + f(tpswap(pick(big, 1 - t, 1)))
    input_grad = assemble(place, *give_back(grad0_, near_other, home, tpswap(home)))
    wg_low = wg.astype(bf16)
    wg = pick(wg, zi, 1) + f(zswap(pick(wg_low, 1 - zi, 1), 2))
    wg = wg.astype(bf16)
    wg = send(wg, lambda f_, w_, u: (f_, (w_ // 2) * 2 + u, w_ % 2))
    wg = f(ordered(c, pick(wg, c)[None], core(pick(wg, 1 - c))[None]))
    wg = jnp.concatenate([wg[..., :384].reshape(2, depth, 3, 128), wg[..., 384:].reshape(2, depth, 3, 64)], axis=-1)
    wg = wg.transpose(2, 1, 0, 3).reshape(3, depth, half)

    for distance in (1, 2):
        small = small + zswap(small, distance)
    pb, g2, b2, db, ub, g1, b1, qv, tg = cut(small, (d, d, d, d, nt * half_ff, d, d, 2 * d, 256 * HD))
    g1 = (g1 - b1 * f(norm1_bias)) / f(norm1_gain)
    tg = tg.reshape(256, HD)
    return (
        result,
        input_grad,
        g1,
        b1,
        wg,
        pick(qv.reshape(2, nt, half), t, 1),
        tg[: 2 * G - 1][::-1],
        tg[128 : 128 + 2 * G - 1],
        big[:, 2 * half_ff :],
        pb,
        g2,
        b2,
        big[:, :half_ff],
        pick(ub.reshape(nt, half_ff), t),
        big[:, half_ff : 2 * half_ff],
        db,
    )


def layer_norm(values, gain_vec, shift_vec):
    centered = values - jnp.mean(values, axis=-1, keepdims=True)
    inverse = lax.rsqrt(jnp.mean(centered * centered, axis=-1, keepdims=True) + eps)
    standard = centered * inverse
    return (standard * gain_vec + shift_vec, standard, inverse)


def norm_back_plain(upstream, standard, inverse, gain_vec):
    scaled = upstream * gain_vec
    mean_term = jnp.mean(scaled, axis=-1, keepdims=True)
    proj_term = jnp.mean(scaled * standard, axis=-1, keepdims=True)
    return inverse * (scaled - mean_term - standard * proj_term)


def exact_gelu(values):
    return jax.nn.gelu(values, approximate=False)


def table_rows(pos_table, first_row, num_rows):
    table_len = pos_table.shape[0]
    grid_side = (table_len + 1) // 2
    query_row = first_row + lax.broadcasted_iota(jnp.int32, (num_rows, grid_side, table_len), 0)
    key_row = lax.broadcasted_iota(jnp.int32, (num_rows, grid_side, table_len), 1)
    entry_idx = lax.broadcasted_iota(jnp.int32, (num_rows, grid_side, table_len), 2)
    chooser = (query_row - key_row + grid_side - 1 == entry_idx).astype(jnp.float32)
    chooser = chooser.reshape(num_rows * grid_side, table_len)
    picked = jnp.dot(chooser, pos_table, precision=highest)
    return (picked.reshape(num_rows, grid_side, -1), chooser)


def rel_terms(query_f, row_first, rel_h, rel_w):
    grid_rows = query_f.shape[0] // G
    head_count = query_f.shape[1]
    near_h, pick_h = table_rows(rel_h, row_first, grid_rows)
    near_w, pick_w = table_rows(rel_w, 0, G)
    shaped = query_f.reshape(grid_rows, G, head_count, query_f.shape[2])
    term_h = jnp.einsum("awhc,akc->awhk", shaped, near_h, precision=highest)
    term_w = jnp.einsum("awhc,wkc->awhk", shaped, near_w, precision=highest)
    return (
        term_h.reshape(-1, head_count, G),
        term_w.reshape(-1, head_count, G),
        near_h,
        near_w,
        pick_h,
        pick_w,
    )


def piece_scores(query, key_h, term_h, term_w, factor):
    num_keys = key_h.shape[0]
    products = jnp.einsum("rhc,nhc->rhn", query, key_h, preferred_element_type=jnp.float32)
    position = (term_h[..., :, None] + term_w[..., None, :]).reshape(
        term_h.shape[0], term_h.shape[1], num_keys
    )
    return products * factor + position


def attend_step(running, pieces, offset, query, term_h, term_w, factor):
    run_max, run_sum, accumulated = running
    key_piece, value_piece = pieces
    num_keys = key_piece.shape[0]
    head_count = query.shape[1]
    key_h = key_piece.reshape(num_keys, head_count, -1)
    value_h = value_piece.reshape(num_keys, head_count, -1)
    scores = piece_scores(query, key_h, term_h, term_w, factor)
    new_max = jnp.maximum(run_max, jnp.max(scores, axis=-1))
    weights_p = jnp.exp(scores - new_max[..., None])
    run_sum = jnp.sum(weights_p, axis=-1)
    accumulated = jnp.einsum(
        "rhn,nhc->rhc", weights_p.astype(jnp.bfloat16), value_h, preferred_element_type=jnp.float32
    )
    return (new_max, run_sum, accumulated)


def grad_step(running, pieces, offset, query, out_grad, log_total, row_dot, term_h, term_w, factor):
    key_piece, value_piece = pieces
    num_keys = key_piece.shape[0]
    num_rows, head_count, head_size = query.shape
    key_h = key_piece.reshape(num_keys, head_count, head_size)
    value_h = value_piece.reshape(num_keys, head_count, head_size)
    scores = piece_scores(query, key_h, term_h, term_w, factor)
    weights_p = jnp.exp(scores - log_total[..., None])
    prob_grad = jnp.einsum("rhc,nhc->rhn", out_grad, value_h, preferred_element_type=jnp.float32)
    score_grad = (weights_p * (prob_grad - row_dot[..., None])).astype(jnp.bfloat16)
    query_acc = jnp.einsum("rhn,nhc->rhc", score_grad, key_h, preferred_element_type=jnp.float32)
    key_grad = (
        jnp.einsum("rhn,rhc->nhc", score_grad, query, preferred_element_type=jnp.float32) * factor
    )
    value_grad = jnp.einsum(
        "rhn,rhc->nhc", weights_p.astype(jnp.bfloat16), out_grad, preferred_element_type=jnp.float32
    )
    joined = jnp.concatenate(
        [key_grad.reshape(num_keys, -1), value_grad.reshape(num_keys, -1)], axis=1
    )
    grid_grad = score_grad.reshape(num_rows, head_count, num_keys // G, G)
    part_h = jnp.sum(grid_grad, axis=-1, dtype=jnp.float32)
    grad_w = jnp.sum(grid_grad, axis=-2, dtype=jnp.float32)
    return (query_acc, joined, part_h, grad_w)


def tensor_total(partial_sum):
    return lax.psum(partial_sum.astype(jnp.bfloat16), "tp").astype(jnp.float32)


def contract_last(left_mat, right_mat):
    return lax.dot_general(
        left_mat, right_mat, (((1,), (1,)), ((), ())), preferred_element_type=jnp.float32
    )


def micro_step(weights_full, picture, cotangent, params):
    (
        gain_one,
        shift_one,
        qv_shift,
        rel_h,
        rel_w,
        proj_shift,
        gain_two,
        shift_two,
        up_shift,
        down_shift,
    ) = params
    qkv_full, proj_full, up_full, down_full = weights_full
    rows_dev = picture.shape[0]
    half_width = qkv_full.shape[2]
    head_count = half_width // HD
    grid_rows = rows_dev // G
    row_first = lax.axis_index("ctx") * grid_rows
    factor = HD ** (-0.5)
    source = picture.astype(jnp.float32)
    normed_f, standard_one, inverse_one = layer_norm(source, gain_one, shift_one)
    normed = normed_f.astype(jnp.bfloat16)
    projected = jnp.einsum("rd,jde->jre", normed, qkv_full, preferred_element_type=jnp.float32)
    query_flat = (projected[0] + qv_shift[0]).astype(jnp.bfloat16)
    key_flat = projected[1].astype(jnp.bfloat16)
    value_flat = (projected[2] + qv_shift[1]).astype(jnp.bfloat16)
    query = query_flat.reshape(rows_dev, head_count, HD)
    query_f = query.astype(jnp.float32)
    term_h, term_w, near_h, near_w, pick_h, pick_w = rel_terms(query_f, row_first, rel_h, rel_w)
    start_state = (
        jnp.full((rows_dev, head_count), -1e30, jnp.float32),
        jnp.zeros((rows_dev, head_count), jnp.float32),
        jnp.zeros((rows_dev, head_count, HD), jnp.float32),
    )
    forward_fn = partial(attend_step, query=query, term_h=term_h, term_w=term_w, factor=factor)
    run_max, run_sum, accumulated = forward_fn(
        start_state,
        (
            lax.all_gather(key_flat, "ctx", axis=0, tiled=True),
            lax.all_gather(value_flat, "ctx", axis=0, tiled=True),
        ),
        jnp.int32(0),
    )
    attended = accumulated / run_sum[..., None]
    log_total = run_max + jnp.log(run_sum)
    mixed = attended.reshape(rows_dev, half_width).astype(jnp.bfloat16)
    middle = source + tensor_total(contract_last(mixed, proj_full)) + proj_shift
    normed2_f, standard_two, inverse_two = layer_norm(middle, gain_two, shift_two)
    normed2 = normed2_f.astype(jnp.bfloat16)
    hidden = jnp.dot(normed2, up_full, preferred_element_type=jnp.float32) + up_shift
    active, gelu_back = jax.vjp(exact_gelu, hidden)
    active_low = active.astype(jnp.bfloat16)
    result = (middle + tensor_total(contract_last(active_low, down_full)) + down_shift).astype(
        jnp.bfloat16
    )
    top_f = cotangent.astype(jnp.float32)
    down_grad = jnp.einsum("rd,rf->df", cotangent, active_low, preferred_element_type=jnp.float32)
    down_shift_grad = jnp.sum(top_f, axis=0)
    active_grad = jnp.dot(cotangent, down_full, preferred_element_type=jnp.float32)
    hidden_grad = gelu_back(active_grad)[0].astype(jnp.bfloat16)
    up_grad = jnp.einsum("rd,rf->df", normed2, hidden_grad, preferred_element_type=jnp.float32)
    up_shift_grad = jnp.sum(hidden_grad, axis=0, dtype=jnp.float32)
    normed2_grad = lax.psum(contract_last(hidden_grad, up_full).astype(jnp.bfloat16), "tp").astype(
        jnp.float32
    )
    middle_grad = top_f + norm_back_plain(normed2_grad, standard_two, inverse_two, gain_two)
    gain_two_grad = jnp.sum(normed2_grad * standard_two, axis=0)
    shift_two_grad = jnp.sum(normed2_grad, axis=0)
    branch_grad = middle_grad.astype(jnp.bfloat16)
    proj_grad = jnp.einsum("rd,re->de", branch_grad, mixed, preferred_element_type=jnp.float32)
    proj_shift_grad = jnp.sum(branch_grad, axis=0, dtype=jnp.float32)
    mixed_grad = (
        jnp.dot(branch_grad, proj_full, preferred_element_type=jnp.float32)
        .astype(jnp.bfloat16)
        .reshape(rows_dev, head_count, HD)
    )
    row_dot = jnp.sum(mixed_grad.astype(jnp.float32) * attended, axis=-1)
    ctx_count = lax.axis_size("ctx")
    start_back = (
        jnp.zeros((rows_dev, head_count, HD), jnp.float32),
        jnp.zeros((rows_dev * ctx_count, 2 * half_width), jnp.float32),
        jnp.zeros((rows_dev, head_count, G), jnp.float32),
        jnp.zeros((rows_dev, head_count, G), jnp.float32),
    )
    back_fn = partial(
        grad_step,
        query=query,
        out_grad=mixed_grad,
        log_total=log_total,
        row_dot=row_dot,
        term_h=term_h,
        term_w=term_w,
        factor=factor,
    )
    query_acc, key_value_acc, grad_h, grad_w = back_fn(
        start_back,
        (
            lax.all_gather(key_flat, "ctx", axis=0, tiled=True),
            lax.all_gather(value_flat, "ctx", axis=0, tiled=True),
        ),
        jnp.int32(0),
    )
    key_value_mine = lax.psum_scatter(
        key_value_acc.astype(jnp.bfloat16), "ctx", scatter_dimension=0, tiled=True
    ).astype(jnp.float32)
    grid_h = grad_h.reshape(grid_rows, G, head_count, G)
    grid_w = grad_w.reshape(grid_rows, G, head_count, G)
    shaped_q = query_f.reshape(grid_rows, G, head_count, HD)
    rel_query = jnp.einsum("awhk,akc->awhc", grid_h, near_h, precision=highest) + jnp.einsum(
        "awhk,wkc->awhc", grid_w, near_w, precision=highest
    )
    query_grad = (
        (query_acc * factor + rel_query.reshape(rows_dev, head_count, HD))
        .reshape(rows_dev, half_width)
        .astype(jnp.bfloat16)
    )
    key_grad = key_value_mine[:, :half_width].astype(jnp.bfloat16)
    value_grad = key_value_mine[:, half_width:].astype(jnp.bfloat16)
    table_h_part = jnp.dot(
        pick_h.T,
        jnp.einsum("awhk,awhc->akc", grid_h, shaped_q, precision=highest).reshape(-1, HD),
        precision=highest,
    )
    table_w_part = jnp.dot(
        pick_w.T,
        jnp.einsum("awhk,awhc->wkc", grid_w, shaped_q, precision=highest).reshape(-1, HD),
        precision=highest,
    )
    stacked = jnp.stack([query_grad, key_grad, value_grad])
    qkv_grad = jnp.einsum("rd,jre->jde", normed, stacked, preferred_element_type=jnp.float32)
    qv_shift_grad = jnp.stack(
        [
            jnp.sum(query_grad, axis=0, dtype=jnp.float32),
            jnp.sum(value_grad, axis=0, dtype=jnp.float32),
        ]
    )
    normed_part = jnp.einsum("jre,jde->rd", stacked, qkv_full, preferred_element_type=jnp.float32)
    normed_grad, table_h_grad, table_w_grad = (
        lax.psum(normed_part.astype(jnp.bfloat16), "tp").astype(jnp.float32),
        lax.psum(table_h_part.astype(jnp.bfloat16), "tp").astype(jnp.float32),
        lax.psum(table_w_part.astype(jnp.bfloat16), "tp").astype(jnp.float32),
    )
    input_grad = (middle_grad + norm_back_plain(normed_grad, standard_one, inverse_one, gain_one)).astype(
        jnp.bfloat16
    )
    gain_one_grad = jnp.sum(normed_grad * standard_one, axis=0)
    shift_one_grad = jnp.sum(normed_grad, axis=0)
    big_grads = (qkv_grad, proj_grad, up_grad, down_grad)
    small_grads = (
        gain_one_grad,
        shift_one_grad,
        qv_shift_grad,
        table_h_grad,
        table_w_grad,
        proj_shift_grad,
        gain_two_grad,
        shift_two_grad,
        up_shift_grad,
        down_shift_grad,
    )
    return (result, input_grad, big_grads, small_grads)


def add_trees(first_tree, second_tree):
    return jax.tree.map(lambda first_v, second_v: first_v + second_v, first_tree, second_tree)


def zeros_like_tree(tree):
    return jax.tree.map(lambda member: jnp.zeros(member.shape, jnp.float32), tree)


def local(
    images,
    norm1_gain,
    norm1_bias,
    qkv_weight,
    qv_bias,
    rel_pos_h,
    rel_pos_w,
    proj_weight,
    proj_bias,
    norm2_gain,
    norm2_bias,
    up_weight,
    up_bias,
    down_weight,
    down_bias,
    out_cotangent,
):
    params = tuple(
        (
            member.astype(jnp.float32)
            for member in (
                norm1_gain,
                norm1_bias,
                qv_bias,
                rel_pos_h,
                rel_pos_w,
                proj_bias,
                norm2_gain,
                norm2_bias,
                up_bias,
                down_bias,
            )
        )
    )
    small_start = zeros_like_tree(params)

    def per_batch(totals, pair):
        weights_full = (
            lax.all_gather(qkv_weight, ("fsdp", "ctx"), axis=1, tiled=True),
            lax.all_gather(proj_weight, ("fsdp", "ctx"), axis=0, tiled=True),
            lax.all_gather(up_weight, ("fsdp", "ctx"), axis=0, tiled=True),
            lax.all_gather(down_weight, ("fsdp", "ctx"), axis=0, tiled=True),
        )
        result, input_grad, big_grads, small_grads = micro_step(
            weights_full, pair[0], pair[1], params
        )
        shards = (
            lax.psum_scatter(big_grads[0], ("fsdp", "ctx"), scatter_dimension=1, tiled=True),
            lax.psum_scatter(big_grads[1], ("fsdp", "ctx"), scatter_dimension=0, tiled=True),
            lax.psum_scatter(big_grads[2], ("fsdp", "ctx"), scatter_dimension=0, tiled=True),
            lax.psum_scatter(big_grads[3], ("fsdp", "ctx"), scatter_dimension=0, tiled=True),
        )
        return (add_trees(totals, (shards, small_grads)), (result, input_grad))

    shard_start = zeros_like_tree((qkv_weight, proj_weight, up_weight, down_weight))
    (shard_totals, small_totals), (outputs, input_grads) = lax.scan(
        per_batch, (shard_start, small_start), (images, out_cotangent)
    )
    small_final = lax.psum(small_totals, ("fsdp", "ctx"))
    return (
        outputs,
        input_grads,
        small_final[0],
        small_final[1],
        shard_totals[0],
        small_final[2],
        small_final[3],
        small_final[4],
        shard_totals[1],
        small_final[5],
        small_final[6],
        small_final[7],
        shard_totals[2],
        small_final[8],
        shard_totals[3],
        small_final[9],
    )


def solution(mesh):
    shape = dict(mesh.shape)
    body = partial(grouped, shape) if shape == {"fsdp": 4, "ctx": 4, "tp": 2} else local
    placed = (
        P("fsdp", "ctx", None),
        P(),
        P(),
        P(None, ("fsdp", "ctx"), "tp"),
        P(None, "tp"),
        P(),
        P(),
        P(("fsdp", "ctx"), "tp"),
        P(),
        P(),
        P(),
        P(("fsdp", "ctx"), "tp"),
        P("tp"),
        P(("fsdp", "ctx"), "tp"),
        P(),
        P("fsdp", "ctx", None),
    )
    return jax.shard_map(
        body,
        mesh=mesh,
        in_specs=placed,
        out_specs=(
            P("fsdp", "ctx", None),
            P("fsdp", "ctx", None),
            P(),
            P(),
            P(None, ("fsdp", "ctx"), "tp"),
            P(None, "tp"),
            P(),
            P(),
            P(("fsdp", "ctx"), "tp"),
            P(),
            P(),
            P(),
            P(("fsdp", "ctx"), "tp"),
            P("tp"),
            P(("fsdp", "ctx"), "tp"),
            P(),
        ),
        check_vma=False,
    )
```
